128 devices in a mesh: depth: 8 (over z, y_lo), height: 16 (over x, y_hi, core).
Axes of the slice: x: 4, y: 4 (y_hi: 2, y_lo: 2; y = y_hi * 2 + y_lo), z: 4, core: 2. Of those that a mesh axis runs over, the one named last changes fastest.
Arguments:
- volume: bfloat16 [32, 32, 128, 128], P(None, 'depth', 'height'), may hold values from -6 to 6
- filters_three: bfloat16 [27, 64, 32], replicated, may hold values from -0.21875 to 0.21875
- filters_four: bfloat16 [27, 128, 64], P(None, 'height'), may hold values from -0.15625 to 0.15625
- cotangent: bfloat16 [128, 16, 64, 64], P(None, 'depth', 'height'), may hold values from -6 to 6
Outputs:
- grad_volume: bfloat16 [32, 32, 128, 128], P(None, 'depth', 'height')
- grad_three: float32 [27, 64, 32], replicated
- grad_four: float32 [27, 128, 64], P(None, 'height')
The draws below stay inside these ranges and needn't reach their ends.
All inputs are finite; a program needn't handle non-finite values.
Results may differ from the reference program's by a relative error of at most 0.023.
Values may be sent and summed in bfloat16 or wider, within the bound.
A program may use at most 256 MiB of HBM per device.

```python
import math
import jax
import jax.numpy as jnp
from jax import lax

CIN = 32
CMID = 64
COUT = 128
WID = 128
DEPTH = 32
HEIGHT = 128


def block_scale(own_key, extent, cuts, low, top_value):
    def one(axis_at, parts):
        steps = jax.random.uniform(jax.random.fold_in(jax.random.fold_in(own_key, 6), axis_at), (parts,), jnp.float32, low / len(cuts), top_value / len(cuts))
        return jnp.repeat(jnp.exp(steps), extent[axis_at] // parts).reshape((-1,) + (1,) * (len(extent) - axis_at - 1))

    loudness = one(*cuts[0])
    for cut in cuts[1:]:
        loudness = loudness * one(*cut)
    return loudness


def noise(stream_key, shape, scale, bound, pieces=(), dtype=jnp.bfloat16):
    drawn = jax.random.normal(stream_key, shape, jnp.float32) * scale
    if len(pieces) > 0:
        drawn = block_scale(stream_key, shape, pieces, -0.22, 0.18) * drawn
    return jnp.clip(drawn, min=-bound, max=bound).astype(dtype)


def setup_inputs(seed: int = 0) -> dict:
    keys = jax.random.split(jax.random.key(seed), 5)
    return {
        "volume": noise(keys[0], (CIN, DEPTH, HEIGHT, WID), 1.0, 6.0, ((1, 8), (2, 16))),
        "filters_three": noise(keys[1], (27, CMID, CIN), (27 * CIN) ** -0.5, 0.21875),
        "filters_four": noise(keys[2], (27, COUT, CMID), (27 * CMID) ** -0.5, 0.15625, ((1, 16),)),
        "cotangent": noise(keys[3], (COUT, DEPTH // 2, HEIGHT // 2, WID // 2), 1.0, 6.0, ((1, 8), (2, 16))),
    }


TANH_SCALE = 0.7978845608028654
CUBIC_TERM = 0.044715

def gelu_value(values_in):
    inner = jnp.tanh(TANH_SCALE * (values_in + CUBIC_TERM * values_in * values_in * values_in))
    return 0.5 * values_in * (1.0 + inner)

def gelu_slope(values_in):
    inner = jnp.tanh(TANH_SCALE * (values_in + CUBIC_TERM * values_in * values_in * values_in))
    return 0.5 * (1.0 + inner) + 0.5 * values_in * (1.0 - inner * inner) * TANH_SCALE * (1.0 + 3.0 * CUBIC_TERM * values_in * values_in)

def pad_cells(values_in):
    return jnp.pad(values_in, ((0, 0), (1, 1), (1, 1), (1, 1)))

def forward_taps(padded, weights, depth_cells, height_cells, width_cells):
    running = jnp.zeros((weights.shape[1], depth_cells, height_cells, width_cells), jnp.float32)
    for first in range(3):
        for second in range(3):
            for third in range(3):
                window_piece = padded[:, first:first + depth_cells, second:second + height_cells, third:third + width_cells]
                running = running + jnp.einsum('oi,idhw->odhw', weights[9 * first + 3 * second + third].astype(jnp.float32), window_piece.astype(jnp.float32))
    return running

def transpose_taps(padded, weights, depth_cells, height_cells, width_cells):
    running = jnp.zeros((weights.shape[2], depth_cells, height_cells, width_cells), jnp.float32)
    for first in range(3):
        for second in range(3):
            for third in range(3):
                window_piece = padded[:, 2 - first:2 - first + depth_cells, 2 - second:2 - second + height_cells, 2 - third:2 - third + width_cells]
                running = running + jnp.einsum('oi,odhw->idhw', weights[9 * first + 3 * second + third].astype(jnp.float32), window_piece.astype(jnp.float32))
    return running

def weight_taps(delta, padded, depth_cells, height_cells, width_cells):
    collected = []
    for first in range(3):
        for second in range(3):
            for third in range(3):
                window_piece = padded[:, first:first + depth_cells, second:second + height_cells, third:third + width_cells]
                collected.append(jnp.einsum('odhw,idhw->oi', delta.astype(jnp.float32), window_piece.astype(jnp.float32)))
    return jnp.stack(collected, axis=0)

def reference(volume, filters_three, filters_four, cotangent):
    scale_three = 1.0 / math.sqrt(DEPTH * HEIGHT * WID)
    scale_four = 1.0 / math.sqrt(DEPTH // 2 * (HEIGHT // 2) * (WID // 2))
    padded = pad_cells(volume)
    act_three = forward_taps(padded, filters_three, DEPTH, HEIGHT, WID)
    hidden = gelu_value(act_three).reshape(CMID, DEPTH // 2, 2, HEIGHT // 2, 2, WID // 2, 2)
    pooled = (lax.optimization_barrier(jnp.sum(hidden, axis=(2, 4, 6))) * 0.125).astype(jnp.bfloat16)
    pooled_pad = pad_cells(pooled)
    act_four = forward_taps(pooled_pad, filters_four, DEPTH // 2, HEIGHT // 2, WID // 2)
    delta_four = (cotangent.astype(jnp.float32) * gelu_slope(act_four)).astype(jnp.bfloat16)
    grad_four = weight_taps(delta_four, pooled_pad, DEPTH // 2, HEIGHT // 2, WID // 2) * scale_four
    back_pooled = transpose_taps(pad_cells(delta_four), filters_four, DEPTH // 2, HEIGHT // 2, WID // 2)
    spread = jnp.repeat(jnp.repeat(jnp.repeat(back_pooled, 2, axis=1), 2, axis=2), 2, axis=3) * 0.125
    delta_three = (spread * gelu_slope(act_three)).astype(jnp.bfloat16)
    grad_three = weight_taps(delta_three, padded, DEPTH, HEIGHT, WID) * scale_three
    grad_volume = transpose_taps(pad_cells(delta_three), filters_three, DEPTH, HEIGHT, WID).astype(jnp.bfloat16)
    return (grad_volume, grad_three, grad_four)
```

```python
import functools
import math

import jax
import jax.numpy as jnp
from jax import lax
from jax.experimental import pallas as pl
from jax.experimental.pallas import tpu as pltpu
from jax.sharding import PartitionSpec as P

TANH_SCALE = 0.7978845608028654
CUBIC_TERM = 0.044715
MESH = pl.DeviceIdType.MESH
F32 = jnp.float32
BF16 = jnp.bfloat16

ND = 8
NH = 16
DIRECTIONS = [(dd, hh) for dd in (-1, 0, 1) for hh in (-1, 0, 1) if (dd, hh) != (0, 0)]


def gelu_parts(v):
    u = v * v
    inner = jnp.tanh(TANH_SCALE * (v + CUBIC_TERM * v * u))
    half = 0.5 * (1.0 + inner)
    value = v * half
    slope = half + 0.5 * v * (1.0 - inner * inner) * TANH_SCALE * (1.0 + 3.0 * CUBIC_TERM * u)
    return value, slope


def lanes_iota(shape):
    return lax.broadcasted_iota(jnp.int32, shape, len(shape) - 1)


def shifted(v, step):
    lane = lanes_iota(v.shape)
    before = jnp.where(lane < step, 0.0, pltpu.roll(v, step, 1))
    after = jnp.where(lane >= 128 - step, 0.0, pltpu.roll(v, 128 - step, 1))
    return before, after


def stack_width(row, step):
    before, after = shifted(row.astype(F32), step)
    return jnp.concatenate([before.astype(BF16), row, after.astype(BF16)], axis=0)


def part(at, cells, far):
    if at == 0:
        return pl.ds(1, cells)
    if at < 0:
        return pl.ds(cells + 1, 1) if far else pl.ds(1, 1)
    return pl.ds(0, 1) if far else pl.ds(cells, 1)


def kernel(
    x_in, a3, a6, f4, cot,
    gv_out, g3_out, g4_out,
    xb, xx, slope3, pb, pp, d4, d3, bank, a4, a5,
    f4acc, r4, q4, t4, q4b,
    f3acc, r3, q3, t3, q3b, v3,
    halo_s, halo_r, ag_s, ag_r, s4_s, s4_r, b4_s, b4_r, s3_s, s3_r, b3_s, b3_r, c3_s, c3_r,
):
    d = lax.axis_index("depth")
    h = lax.axis_index("height")

    def dev_d(k):
        return (lax.rem(d + k + ND, ND), h)

    def dev_h(k):
        return (d, lax.rem(h + k + NH, NH))

    barrier = pltpu.get_barrier_semaphore()
    for k in range(1, NH):
        pl.semaphore_signal(barrier, inc=1, device_id=dev_h(k), device_id_type=MESH)
    for k in range(1, ND):
        pl.semaphore_signal(barrier, inc=1, device_id=dev_d(k), device_id_type=MESH)
    for dd in (-1, 1):
        for hh in (-1, 1):
            pl.semaphore_signal(
                barrier,
                inc=1,
                device_id=(lax.rem(d + dd + ND, ND), lax.rem(h + hh + NH, NH)),
                device_id_type=MESH,
            )
    pl.semaphore_wait(barrier, NH - 1 + ND - 1 + 4)

    def halo_copy(which, n, buf, cells_d, cells_h):
        dd, hh = DIRECTIONS[n]
        return pltpu.make_async_remote_copy(
            src_ref=buf.at[part(dd, cells_d, False), part(hh, cells_h, False)],
            dst_ref=buf.at[part(dd, cells_d, True), part(hh, cells_h, True)],
            send_sem=halo_s.at[which, n],
            recv_sem=halo_r.at[which, n],
            device_id=(lax.rem(d + dd + ND, ND), lax.rem(h + hh + NH, NH)),
            device_id_type=MESH,
        )

    def halo_start(which, buf, cells_d, cells_h):
        for n in range(8):
            halo_copy(which, n, buf, cells_d, cells_h).start()

    def halo_wait(which, buf, cells_d, cells_h):
        for n in range(8):
            halo_copy(which, n, buf, cells_d, cells_h).wait_send()
        for n in range(8):
            halo_copy(which, n, buf, cells_d, cells_h).wait_recv()
        channels = buf.shape[2]

        @pl.when(d == 0)
        def _():
            buf[0] = jnp.zeros((cells_h + 2, channels, 128), BF16)

        @pl.when(d == ND - 1)
        def _():
            buf[cells_d + 1] = jnp.zeros((cells_h + 2, channels, 128), BF16)

        @pl.when(h == 0)
        def _():
            buf[:, 0] = jnp.zeros((cells_d + 2, channels, 128), BF16)

        @pl.when(h == NH - 1)
        def _():
            buf[:, cells_h + 1] = jnp.zeros((cells_d + 2, channels, 128), BF16)

    def scatter_h(src, dst, send, recv, k):
        other = lax.rem(h + k, NH)
        return pltpu.make_async_remote_copy(
            src_ref=src.at[other],
            dst_ref=dst.at[k],
            send_sem=send.at[k],
            recv_sem=recv.at[k],
            device_id=(d, other),
            device_id_type=MESH,
        )

    def share_d(src, dst, send, recv, k):
        return pltpu.make_async_remote_copy(
            src_ref=src,
            dst_ref=dst.at[k],
            send_sem=send.at[k],
            recv_sem=recv.at[k],
            device_id=(lax.rem(d + k, ND), h),
            device_id_type=MESH,
        )

    def gather_send(src, dst, send, recv, k):
        return pltpu.make_async_remote_copy(
            src_ref=src,
            dst_ref=dst.at[h],
            send_sem=send.at[k],
            recv_sem=recv.at[k],
            device_id=(d, lax.rem(h + k, NH)),
            device_id_type=MESH,
        )

    def gather_recv(src, dst, send, recv, k):
        return pltpu.make_async_remote_copy(
            src_ref=src,
            dst_ref=dst.at[lax.rem(h - k + NH, NH)],
            send_sem=send.at[k],
            recv_sem=recv.at[k],
            device_id=(d, lax.rem(h + k, NH)),
            device_id_type=MESH,
        )

    def each(low, high, body):
        def step(k, carry):
            body(k)
            return carry

        lax.fori_loop(low, high, step, 0)

    xb[1:5, 1:9] = x_in[...]
    halo_start(0, xb, 4, 8)
    each(1, NH, lambda k: gather_send(f4, bank, ag_s, ag_r, k).start())
    bank[h] = f4[...]

    def stack_x(i):
        for j in range(10):
            xx[i, j] = stack_width(xb[i, j], 1)

    halo_wait(0, xb, 4, 8)
    each(0, 6, stack_x)

    def forward3(i):
        for j in range(4):
            total = None
            for di in range(2):
                cols = [
                    jnp.concatenate(
                        [xx[2 * i + di + a, 2 * j + s + b] for a in range(3) for b in range(3)],
                        axis=0,
                    )
                    for s in range(2)
                ]
                act = jnp.dot(
                    a3[...], jnp.concatenate(cols, axis=1), preferred_element_type=F32
                )
                value, slope = gelu_parts(act)
                for s in range(2):
                    slope3[2 * i + di, 2 * j + s] = slope[:, 128 * s : 128 * s + 128]
                both = value[:, :128] + value[:, 128:]
                total = both if total is None else total + both
            total = (total + pltpu.roll(total, 127, 1)) * 0.125
            even = lanes_iota(total.shape) % 2 == 0
            pb[1 + i, 1 + j] = jnp.where(even, total, 0.0).astype(BF16)

    each(0, 2, forward3)
    halo_start(1, pb, 2, 4)

    def wait_gather(k):
        gather_send(f4, bank, ag_s, ag_r, k).wait_send()
        gather_recv(f4, bank, ag_s, ag_r, k).wait_recv()

    each(1, NH, wait_gather)
    wide = [bank[s].astype(F32) for s in range(NH)]
    low = jnp.concatenate([w[:8] for w in wide], axis=0)
    high = jnp.concatenate([w[8:] for w in wide], axis=0)
    a4[...] = jnp.concatenate([low, high], axis=1).astype(BF16)
    for ab in range(9):
        a5[:, 128 * ab : 128 * ab + 128] = jnp.transpose(
            a4[:, 192 * ab : 192 * ab + 192].astype(F32)
        ).astype(BF16)

    halo_wait(1, pb, 2, 4)

    def stack_p(i):
        for j in range(6):
            pp[i, j] = stack_width(pb[i, j], 2)

    each(0, 4, stack_p)

    def forward4(i):
        for j in range(2):
            cols = [
                jnp.concatenate(
                    [pp[i + a, 2 * j + s + b] for a in range(3) for b in range(3)], axis=0
                )
                for s in range(2)
            ]
            act = jnp.dot(
                a4[:, :1728], jnp.concatenate(cols, axis=1), preferred_element_type=F32
            )
            _, slope = gelu_parts(act)
            for s in range(2):
                d4[1 + i, 1 + 2 * j + s] = (
                    cot[i, 2 * j + s].astype(F32) * slope[:, 128 * s : 128 * s + 128]
                ).astype(BF16)

    each(0, 2, forward4)
    halo_start(2, d4, 2, 4)

    cells4 = [(i, j) for i in range(2) for j in range(4)]
    left4 = jnp.concatenate([d4[1 + i, 1 + j] for i, j in cells4], axis=1)
    for g in range(5):
        taps = [ab for ab in (2 * g, 2 * g + 1) if ab < 9]
        right = jnp.concatenate(
            [
                jnp.concatenate([pp[i + ab // 3, j + ab % 3] for i, j in cells4], axis=1)
                for ab in taps
            ],
            axis=0,
        )
        piece = lax.dot_general(
            left4, right, (((1,), (1,)), ((), ())), preferred_element_type=F32
        )
        if len(taps) == 1:
            piece = jnp.concatenate([piece, jnp.zeros((128, 64), F32)], axis=1)
        f4acc[:, 384 * g : 384 * g + piece.shape[1]] = piece

    def pack4(s):
        rows = pl.ds(pl.multiple_of(8 * s, 8), 8)
        r4[s] = jnp.concatenate([f4acc[rows, :896], f4acc[rows, 896:]], axis=0).astype(BF16)

    each(0, NH, pack4)
    each(1, NH, lambda k: scatter_h(r4, q4, s4_s, s4_r, k).start())

    halo_wait(2, d4, 2, 4)

    def back4(i):
        for j in range(2):
            cols = [
                jnp.concatenate(
                    [d4[i + 2 - a, 2 * j + s + 2 - b] for a in range(3) for b in range(3)], axis=0
                )
                for s in range(2)
            ]
            y = jnp.dot(a5[...], jnp.concatenate(cols, axis=1), preferred_element_type=F32)
            for s in range(2):
                ys = y[:, 128 * s : 128 * s + 128]
                _, from_after = shifted(ys[:64], 2)
                from_before, _ = shifted(ys[128:], 2)
                back = (ys[64:128] + from_after + from_before) * 0.125
                spread = back + pltpu.roll(back, 1, 1)
                for di in range(2):
                    for dj in range(2):
                        row, col = 2 * i + di, 2 * (2 * j + s) + dj
                        d3[1 + row, 1 + col] = (spread * slope3[row, col]).astype(BF16)

    each(0, 2, back4)
    halo_start(3, d3, 4, 8)

    f3acc[...] = jnp.zeros(f3acc.shape, F32)

    def weight3(i):
        left = jnp.concatenate([d3[1 + i, 1 + j] for j in range(8)], axis=1)
        right = jnp.concatenate(
            [
                jnp.concatenate([xx[i + a, j + b] for j in range(8)], axis=1)
                for a in range(3)
                for b in range(3)
            ],
            axis=0,
        )
        f3acc[:, :864] += lax.dot_general(
            left, right, (((1,), (1,)), ((), ())), preferred_element_type=F32
        )

    each(0, 4, weight3)
    for c in range(16):
        r3[c] = f3acc[
            16 * (c % 4) : 16 * (c % 4) + 16, 256 * (c // 4) : 256 * (c // 4) + 256
        ].astype(BF16)
    each(1, NH, lambda k: scatter_h(r3, q3, s3_s, s3_r, k).start())

    def wait_4(k):
        copy = scatter_h(r4, q4, s4_s, s4_r, k)
        copy.wait_send()
        copy.wait_recv()

    each(1, NH, wait_4)
    total4 = r4[h].astype(F32)
    for k in range(1, NH):
        total4 = total4 + q4[k].astype(F32)
    t4[...] = total4.astype(BF16)
    each(1, ND, lambda k: share_d(t4, q4b, b4_s, b4_r, k).start())

    halo_wait(3, d3, 4, 8)

    def back3(i):
        for j in range(4):
            cols = [
                jnp.concatenate(
                    [d3[i + 2 - a, 2 * j + s + 2 - b] for a in range(3) for b in range(3)], axis=0
                )
                for s in range(2)
            ]
            y = jnp.dot(a6[...], jnp.concatenate(cols, axis=1), preferred_element_type=F32)
            for s in range(2):
                ys = y[:, 128 * s : 128 * s + 128]
                _, from_after = shifted(ys[:32], 1)
                from_before, _ = shifted(ys[64:], 1)
                gv_out[i, 2 * j + s] = (ys[32:64] + from_after + from_before).astype(BF16)

    def wait_3(k):
        copy = scatter_h(r3, q3, s3_s, s3_r, k)
        copy.wait_send()
        copy.wait_recv()

    each(1, NH, wait_3)
    total3 = r3[h].astype(F32)
    for k in range(1, NH):
        total3 = total3 + q3[k].astype(F32)
    t3[...] = total3
    each(1, ND, lambda k: share_d(t3, q3b, b3_s, b3_r, k).start())

    each(0, 4, back3)

    def wait_b3(k):
        copy = share_d(t3, q3b, b3_s, b3_r, k)
        copy.wait_send()
        copy.wait_recv()

    each(1, ND, wait_b3)
    whole3 = t3[...]
    for k in range(1, ND):
        whole3 = whole3 + q3b[k]
    v3[h] = (whole3 * (1.0 / math.sqrt(32 * 128 * 128))).astype(BF16)
    each(1, NH, lambda k: gather_send(v3.at[h], v3, c3_s, c3_r, k).start())

    def wait_b4(k):
        copy = share_d(t4, q4b, b4_s, b4_r, k)
        copy.wait_send()
        copy.wait_recv()

    each(1, ND, wait_b4)
    whole4 = t4[...].astype(F32)
    for k in range(1, ND):
        whole4 = whole4 + q4b[k].astype(F32)
    g4_out[...] = whole4 * (1.0 / math.sqrt(16 * 64 * 64))

    def wait_c3(k):
        gather_send(v3.at[h], v3, c3_s, c3_r, k).wait_send()
        gather_recv(v3.at[h], v3, c3_s, c3_r, k).wait_recv()

    each(1, NH, wait_c3)
    for c in range(16):
        g3_out[16 * (c % 4) : 16 * (c % 4) + 16, 256 * (c // 4) : 256 * (c // 4) + 256] = v3[
            c
        ].astype(F32)


def shards(volume, filters_three, filters_four, cotangent):
    x_in = jnp.transpose(volume, (1, 2, 0, 3))
    a3 = jnp.transpose(filters_three, (1, 0, 2)).reshape(64, 864)
    a6 = jnp.transpose(filters_three.reshape(9, 3, 64, 32), (1, 3, 0, 2)).reshape(96, 576)
    f4 = jnp.pad(jnp.transpose(filters_four, (1, 0, 2)).reshape(8, 1728), ((0, 0), (0, 64)))
    f4 = jnp.transpose(f4.reshape(8, 2, 896), (1, 0, 2)).reshape(16, 896)
    cot = jnp.transpose(cotangent, (1, 2, 0, 3))
    cot = lax.pad(cot, jnp.zeros((), BF16), ((0, 0, 0), (0, 0, 0), (0, 0, 0), (0, 1, 1)))

    vmem = pl.BlockSpec(memory_space=pltpu.VMEM)
    dma = pltpu.SemaphoreType.DMA
    gv, g3, g4 = pl.pallas_call(
        kernel,
        out_shape=(
            jax.ShapeDtypeStruct((4, 8, 32, 128), BF16),
            jax.ShapeDtypeStruct((64, 1024), F32),
            jax.ShapeDtypeStruct((16, 896), F32),
        ),
        in_specs=[vmem] * 5,
        out_specs=(vmem,) * 3,
        scratch_shapes=[
            pltpu.VMEM((6, 10, 32, 128), BF16),
            pltpu.VMEM((6, 10, 96, 128), BF16),
            pltpu.VMEM((4, 8, 64, 128), F32),
            pltpu.VMEM((4, 6, 64, 128), BF16),
            pltpu.VMEM((4, 6, 192, 128), BF16),
            pltpu.VMEM((4, 6, 128, 128), BF16),
            pltpu.VMEM((6, 10, 64, 128), BF16),
            pltpu.VMEM((16, 16, 896), BF16),
            pltpu.VMEM((128, 1792), BF16),
            pltpu.VMEM((192, 1152), BF16),
            pltpu.VMEM((128, 1792), F32),
            pltpu.VMEM((16, 16, 896), BF16),
            pltpu.VMEM((16, 16, 896), BF16),
            pltpu.VMEM((16, 896), BF16),
            pltpu.VMEM((8, 16, 896), BF16),
            pltpu.VMEM((64, 1024), F32),
            pltpu.VMEM((16, 16, 256), BF16),
            pltpu.VMEM((16, 16, 256), BF16),
            pltpu.VMEM((16, 256), F32),
            pltpu.VMEM((8, 16, 256), F32),
            pltpu.VMEM((16, 16, 256), BF16),
            dma((4, 8)),
            dma((4, 8)),
            dma((16,)),
            dma((16,)),
            dma((16,)),
            dma((16,)),
            dma((8,)),
            dma((8,)),
            dma((16,)),
            dma((16,)),
            dma((8,)),
            dma((8,)),
            dma((16,)),
            dma((16,)),
        ],
        compiler_params=pltpu.CompilerParams(
            collective_id=0, has_side_effects=True, vmem_limit_bytes=40 * 1024 * 1024
        ),
    )(x_in, a3, a6, f4, cot)

    grad_volume = jnp.transpose(gv, (2, 0, 1, 3))
    grad_three = jnp.transpose(g3[:, :864].reshape(64, 27, 32), (1, 0, 2))
    g4 = jnp.transpose(g4.reshape(2, 8, 896), (1, 0, 2)).reshape(8, 1792)
    grad_four = jnp.transpose(g4[:, :1728].reshape(8, 27, 64), (1, 0, 2))
    return (grad_volume, grad_three, grad_four)


def solution(mesh):
    in_specs = (
        P(None, "depth", "height", None),
        P(),
        P(None, "height", None),
        P(None, "depth", "height", None),
    )
    out_specs = (P(None, "depth", "height", None), P(), P(None, "height", None))
    return jax.shard_map(shards, mesh=mesh, in_specs=in_specs, out_specs=out_specs, check_vma=False)
```

```python
import functools
import math

import jax
import jax.numpy as jnp
from jax import lax
from jax.experimental import pallas as pl
from jax.experimental.pallas import tpu as pltpu
from jax.sharding import PartitionSpec as P

TANH_SCALE = 0.7978845608028654
CUBIC_TERM = 0.044715
MESH = pl.DeviceIdType.MESH
F32 = jnp.float32
BF16 = jnp.bfloat16

ND = 8
NH = 16
DIRECTIONS = [(dd, hh) for dd in (-1, 0, 1) for hh in (-1, 0, 1) if (dd, hh) != (0, 0)]


def gelu_parts(v):
    u = v * v
    inner = jnp.tanh(TANH_SCALE * (v + CUBIC_TERM * v * u))
    half = 0.5 * (1.0 + inner)
    value = v * half
    slope = half + 0.5 * v * (1.0 - inner * inner) * TANH_SCALE * (1.0 + 3.0 * CUBIC_TERM * u)
    return value, slope


def stage(name, body):
    body()


def lanes_iota(shape):
    return lax.broadcasted_iota(jnp.int32, shape, len(shape) - 1)


def shifted(v, step):
    lane = lanes_iota(v.shape)
    before = jnp.where(lane < step, 0.0, pltpu.roll(v, step, 1))
    after = jnp.where(lane >= 128 - step, 0.0, pltpu.roll(v, 128 - step, 1))
    return before, after


def stack_width(row, step):
    before, after = shifted(row.astype(F32), step)
    return jnp.concatenate([before.astype(BF16), row, after.astype(BF16)], axis=0)


def part(at, cells, width, far):
    if at == 0:
        return pl.ds(width, cells)
    if at < 0:
        return pl.ds(cells + width, width) if far else pl.ds(width, width)
    return pl.ds(0, width) if far else pl.ds(cells, width)


def interleave(even_row, odd_row):
    even = lanes_iota(even_row.shape) % 2 == 0
    return jnp.where(even, even_row, pltpu.roll(odd_row, 1, 1))


def interleave_odd(even_row, odd_row):
    even = lanes_iota(even_row.shape) % 2 == 0
    return jnp.where(even, pltpu.roll(even_row, 127, 1), odd_row)


def two_rows(first, second):
    return jnp.concatenate([interleave(first, second), interleave_odd(first, second)], axis=0)


def kernel(
    x_in, a3, a6, f4, cot,
    gv_out, g3_out, g4_out,
    xb, xx, slope3, ck, pk, pq, dq, dv, d3, bank, a4, a5,
    f4acc, r4, q4, t4, q4b,
    f3acc, r3, q3, t3, q3b, v3,
    halo_s, halo_r, ag_s, ag_r, s4_s, s4_r, b4_s, b4_r, s3_s, s3_r, b3_s, b3_r, c3_s, c3_r,
):
    d = lax.axis_index("depth")
    h = lax.axis_index("height")

    def around(dd, hh):
        return (lax.rem(d + dd + ND, ND), lax.rem(h + hh + NH, NH))

    def partner(other):
        flip = lax.rem(lax.rem(h, 4) // 2 + lax.rem(other, 4) // 2, 2)
        return (d + flip * (1 - 2 * lax.rem(d, 2)), other)

    def each(low, high, body):
        def step(k, carry):
            body(k)
            return carry

        lax.fori_loop(low, high, step, 0)

    barrier = pltpu.get_barrier_semaphore()

    def greet(device):
        pl.semaphore_signal(barrier, inc=1, device_id=device, device_id_type=MESH)

    for dd, hh in DIRECTIONS:
        greet(around(dd, hh))
    for k in range(1, NH):
        greet(partner(lax.rem(h + k, NH)))
    for k in range(2, ND - 1):
        greet(around(k, 0))

    def dilate():
        at = 2 * lax.broadcasted_iota(jnp.int32, (64, 128), 0)
        lane = lanes_iota((64, 128))
        to_even = (lane == at).astype(F32).astype(BF16)
        to_odd = (lane == at + 1).astype(F32).astype(BF16)
        for i in range(2):
            for j in range(4):
                row = cot[i, j]
                ck[1 + i, 1 + j] = (
                    jnp.dot(row[:64], to_even, preferred_element_type=F32)
                    + jnp.dot(row[64:], to_odd, preferred_element_type=F32)
                ).astype(BF16)

    xb[1:5, 1:9] = x_in[...]
    stage("dilate", dilate)
    pl.semaphore_wait(barrier, 8 + NH - 1 + ND - 3)

    def halo_copy(which, n, buf, cells_d, cells_h, width):
        dd, hh = DIRECTIONS[n]
        return pltpu.make_async_remote_copy(
            src_ref=buf.at[part(dd, cells_d, width, False), part(hh, cells_h, width, False)],
            dst_ref=buf.at[part(dd, cells_d, width, True), part(hh, cells_h, width, True)],
            send_sem=halo_s.at[which, n],
            recv_sem=halo_r.at[which, n],
            device_id=around(dd, hh),
            device_id_type=MESH,
        )

    def halo_start(*which):
        for n in range(8):
            halo_copy(which[0], n, *which[1:]).start()

    def halo_wait(*which):
        for n in range(8):
            halo_copy(which[0], n, *which[1:]).wait_send()
        for n in range(8):
            halo_copy(which[0], n, *which[1:]).wait_recv()
        _, buf, cells_d, cells_h, width = which
        channels = buf.shape[2]
        across = (width, cells_h + 2 * width, channels, 128)
        along = (cells_d + 2 * width, width, channels, 128)

        @pl.when(d == 0)
        def _():
            buf[0:width] = jnp.zeros(across, BF16)

        @pl.when(d == ND - 1)
        def _():
            buf[cells_d + width : cells_d + 2 * width] = jnp.zeros(across, BF16)

        @pl.when(h == 0)
        def _():
            buf[:, 0:width] = jnp.zeros(along, BF16)

        @pl.when(h == NH - 1)
        def _():
            buf[:, cells_h + width : cells_h + 2 * width] = jnp.zeros(along, BF16)

    def scatter_h(src, dst, send, recv, k):
        other = lax.rem(h + k, NH)
        return pltpu.make_async_remote_copy(
            src_ref=src.at[other],
            dst_ref=dst.at[k],
            send_sem=send.at[k],
            recv_sem=recv.at[k],
            device_id=partner(other),
            device_id_type=MESH,
        )

    def share_d(src, dst, send, recv, k):
        return pltpu.make_async_remote_copy(
            src_ref=src,
            dst_ref=dst.at[k],
            send_sem=send.at[k],
            recv_sem=recv.at[k],
            device_id=around(k, 0),
            device_id_type=MESH,
        )

    def gather_send(src, dst, send, recv, k):
        return pltpu.make_async_remote_copy(
            src_ref=src,
            dst_ref=dst.at[h],
            send_sem=send.at[k],
            recv_sem=recv.at[k],
            device_id=partner(lax.rem(h + k, NH)),
            device_id_type=MESH,
        )

    def gather_recv(src, dst, send, recv, k):
        return pltpu.make_async_remote_copy(
            src_ref=src,
            dst_ref=dst.at[lax.rem(h - k + NH, NH)],
            send_sem=send.at[k],
            recv_sem=recv.at[k],
            device_id=partner(lax.rem(h + k, NH)),
            device_id_type=MESH,
        )

    halo_x = (0, xb, 4, 8, 1)
    halo_p = (1, pk, 2, 4, 2)
    halo_c = (2, ck, 2, 4, 1)
    halo_d3 = (3, d3, 4, 8, 1)
    halo_start(*halo_x)
    each(1, NH, lambda k: gather_send(f4, bank, ag_s, ag_r, k).start())
    bank[h] = f4[...]

    def stack_x(i):
        for j in range(10):
            xx[i, j] = stack_width(xb[i, j], 1)

    halo_wait(*halo_x)
    halo_start(*halo_c)
    stage("stack_x", lambda: each(0, 6, stack_x))

    def forward3(i):
        for j in range(4):
            total = None
            for di in range(2):
                cols = [
                    jnp.concatenate(
                        [xx[2 * i + di + a, 2 * j + s + b] for a in range(3) for b in range(3)],
                        axis=0,
                    )
                    for s in range(2)
                ]
                act = jnp.dot(
                    a3[...], jnp.concatenate(cols, axis=1), preferred_element_type=F32
                )
                value, slope = gelu_parts(act)
                for s in range(2):
                    slope3[2 * i + di, 2 * j + s] = slope[:, 128 * s : 128 * s + 128]
                both = value[:, :128] + value[:, 128:]
                total = both if total is None else total + both
            total = (total + pltpu.roll(total, 127, 1)) * 0.125
            pk[2 + i, 2 + j] = interleave(total[:32], total[32:]).astype(BF16)

    stage("forward3", lambda: each(0, 2, forward3))
    halo_start(*halo_p)

    def wait_gather(k):
        gather_send(f4, bank, ag_s, ag_r, k).wait_send()
        gather_recv(f4, bank, ag_s, ag_r, k).wait_recv()

    each(1, NH, wait_gather)

    def arrange():
        wide = [bank[s].astype(F32) for s in range(NH)]
        low = jnp.concatenate([w[:8] for w in wide], axis=0)
        high = jnp.concatenate([w[8:] for w in wide], axis=0)
        a4[...] = jnp.concatenate([low, high], axis=1).astype(BF16)
        for ab in range(9):
            a5[:, 128 * ab : 128 * ab + 128] = jnp.transpose(
                a4[:, 192 * ab : 192 * ab + 192].astype(F32)
            ).astype(BF16)

    stage("arrange", arrange)
    halo_wait(*halo_c)
    halo_wait(*halo_p)

    def stack_p(i):
        for j in range(8):
            both = two_rows(pk[i, j].astype(F32), pk[i + 2, j].astype(F32))
            before, after = shifted(both, 2)
            pq[i, j] = jnp.concatenate([before, both, after], axis=0).astype(BF16)

    stage("stack_p", lambda: each(0, 4, stack_p))

    def forward4(i):
        for j in range(3):
            cols = [
                jnp.concatenate(
                    [pq[i + a, 2 * j + s + b] for a in range(3) for b in range(3)], axis=0
                )
                for s in range(2)
            ]
            act = jnp.dot(
                a4[:, :1728], jnp.concatenate(cols, axis=1), preferred_element_type=F32
            )
            _, slope = gelu_parts(act)
            for s in range(2):
                col = 2 * j + s
                both = two_rows(ck[i, col].astype(F32), ck[i + 2, col].astype(F32))
                dq[i, col] = (both * slope[:, 128 * s : 128 * s + 128]).astype(BF16)

    stage("forward4", lambda: each(0, 2, forward4))

    def pair_rows():
        for j in range(6):
            one, two = dq[0, j].astype(F32), dq[1, j].astype(F32)
            even = lanes_iota(one.shape) % 2 == 0
            dv[0, j] = interleave_odd(one, two).astype(BF16)
            dv[1, j] = jnp.where(even, two, one).astype(BF16)
            dv[2, j] = interleave(one, two).astype(BF16)

    stage("pair_rows", pair_rows)

    def back4(j):
        cols = [
            jnp.concatenate([dv[a, 2 * j + s + 2 - b] for a in range(3) for b in range(3)], axis=0)
            for s in range(2)
        ]
        y = jnp.dot(a5[...], jnp.concatenate(cols, axis=1), preferred_element_type=F32)
        for s in range(2):
            ys = y[:, 128 * s : 128 * s + 128]
            _, from_after = shifted(ys[:64], 2)
            from_before, _ = shifted(ys[128:], 2)
            back = (ys[64:128] + from_after + from_before) * 0.125
            even = lanes_iota(back.shape) % 2 == 0
            spread = [
                jnp.where(even, back, pltpu.roll(back, 1, 1)),
                jnp.where(even, pltpu.roll(back, 127, 1), back),
            ]
            for i in range(2):
                for di in range(2):
                    for dj in range(2):
                        row, col = 2 * i + di, 2 * (2 * j + s) + dj
                        d3[1 + row, 1 + col] = (spread[i] * slope3[row, col]).astype(BF16)

    stage("back4", lambda: each(0, 2, back4))
    halo_start(*halo_d3)

    f3acc[...] = jnp.zeros(f3acc.shape, F32)

    def weight3(i):
        left = jnp.concatenate([d3[1 + i, 1 + j] for j in range(8)], axis=1)
        right = jnp.concatenate(
            [
                jnp.concatenate([xx[i + a, j + b] for j in range(8)], axis=1)
                for a in range(3)
                for b in range(3)
            ],
            axis=0,
        )
        f3acc[:, :864] += lax.dot_general(
            left, right, (((1,), (1,)), ((), ())), preferred_element_type=F32
        )

    stage("weight3", lambda: each(0, 4, weight3))

    def pack3():
        for c in range(16):
            r3[c] = f3acc[
                16 * (c % 4) : 16 * (c % 4) + 16, 256 * (c // 4) : 256 * (c // 4) + 256
            ].astype(BF16)

    stage("pack3", pack3)
    each(1, NH, lambda k: scatter_h(r3, q3, s3_s, s3_r, k).start())

    cells4 = [(i, j) for i in range(2) for j in range(4)]

    def weight4():
        even = lanes_iota((128, 128)) % 2 == 0
        left = jnp.concatenate(
            [
                jnp.where(even if i == 0 else ~even, dq[1 - i, 1 + j].astype(F32), 0.0)
                for i, j in cells4
            ],
            axis=1,
        ).astype(BF16)
        for g in range(5):
            taps = [ab for ab in (2 * g, 2 * g + 1) if ab < 9]
            right = jnp.concatenate(
                [
                    jnp.concatenate(
                        [pq[ab // 3 + 1 - i, j + ab % 3 + 1] for i, j in cells4], axis=1
                    )
                    for ab in taps
                ],
                axis=0,
            )
            piece = lax.dot_general(
                left, right, (((1,), (1,)), ((), ())), preferred_element_type=F32
            )
            if len(taps) == 1:
                piece = jnp.concatenate([piece, jnp.zeros((128, 64), F32)], axis=1)
            f4acc[:, 384 * g : 384 * g + piece.shape[1]] = piece

    stage("weight4", weight4)

    def pack4(s):
        rows = pl.ds(pl.multiple_of(8 * s, 8), 8)
        r4[s] = jnp.concatenate([f4acc[rows, :896], f4acc[rows, 896:]], axis=0).astype(BF16)

    stage("pack4", lambda: each(0, NH, pack4))
    each(1, NH, lambda k: scatter_h(r4, q4, s4_s, s4_r, k).start())

    def wait_both(copy):
        copy.wait_send()
        copy.wait_recv()

    each(1, NH, lambda k: wait_both(scatter_h(r3, q3, s3_s, s3_r, k)))

    def sum3():
        total3 = r3[h].astype(F32)
        for k in range(1, NH):
            total3 = total3 + q3[k].astype(F32)
        t3[...] = total3

    stage("sum3", sum3)
    each(1, ND, lambda k: share_d(t3, q3b, b3_s, b3_r, k).start())

    halo_wait(*halo_d3)

    def back3(i):
        for j in range(4):
            cols = [
                jnp.concatenate(
                    [d3[i + 2 - a, 2 * j + s + 2 - b] for a in range(3) for b in range(3)], axis=0
                )
                for s in range(2)
            ]
            y = jnp.dot(a6[...], jnp.concatenate(cols, axis=1), preferred_element_type=F32)
            for s in range(2):
                ys = y[:, 128 * s : 128 * s + 128]
                _, from_after = shifted(ys[:32], 1)
                from_before, _ = shifted(ys[64:], 1)
                gv_out[i, 2 * j + s] = (ys[32:64] + from_after + from_before).astype(BF16)

    stage("back3", lambda: each(0, 4, back3))

    each(1, NH, lambda k: wait_both(scatter_h(r4, q4, s4_s, s4_r, k)))

    def sum4():
        total4 = r4[h].astype(F32)
        for k in range(1, NH):
            total4 = total4 + q4[k].astype(F32)
        t4[...] = total4.astype(BF16)

    stage("sum4", sum4)
    each(1, ND, lambda k: share_d(t4, q4b, b4_s, b4_r, k).start())

    each(1, ND, lambda k: wait_both(share_d(t3, q3b, b3_s, b3_r, k)))
    whole3 = t3[...]
    for k in range(1, ND):
        whole3 = whole3 + q3b[k]
    v3[h] = (whole3 * (1.0 / math.sqrt(32 * 128 * 128))).astype(BF16)
    each(1, NH, lambda k: gather_send(v3.at[h], v3, c3_s, c3_r, k).start())

    each(1, ND, lambda k: wait_both(share_d(t4, q4b, b4_s, b4_r, k)))
    whole4 = t4[...].astype(F32)
    for k in range(1, ND):
        whole4 = whole4 + q4b[k].astype(F32)
    g4_out[...] = whole4 * (1.0 / math.sqrt(16 * 64 * 64))

    def wait_c3(k):
        gather_send(v3.at[h], v3, c3_s, c3_r, k).wait_send()
        gather_recv(v3.at[h], v3, c3_s, c3_r, k).wait_recv()

    each(1, NH, wait_c3)
    for c in range(16):
        g3_out[16 * (c % 4) : 16 * (c % 4) + 16, 256 * (c // 4) : 256 * (c // 4) + 256] = v3[
            c
        ].astype(F32)


def shards(volume, filters_three, filters_four, cotangent):
    x_in = jnp.transpose(volume, (1, 2, 0, 3))
    a3 = jnp.transpose(filters_three, (1, 0, 2)).reshape(64, 864)
    a6 = jnp.transpose(filters_three.reshape(9, 3, 64, 32), (1, 3, 0, 2)).reshape(96, 576)
    f4 = jnp.pad(jnp.transpose(filters_four, (1, 0, 2)).reshape(8, 1728), ((0, 0), (0, 64)))
    f4 = jnp.transpose(f4.reshape(8, 2, 896), (1, 0, 2)).reshape(16, 896)
    cot = jnp.transpose(cotangent, (1, 2, 0, 3))

    vmem = pl.BlockSpec(memory_space=pltpu.VMEM)
    dma = pltpu.SemaphoreType.DMA
    gv, g3, g4 = pl.pallas_call(
        kernel,
        out_shape=(
            jax.ShapeDtypeStruct((4, 8, 32, 128), BF16),
            jax.ShapeDtypeStruct((64, 1024), F32),
            jax.ShapeDtypeStruct((16, 896), F32),
        ),
        in_specs=[vmem] * 5,
        out_specs=(vmem,) * 3,
        scratch_shapes=[
            pltpu.VMEM((6, 10, 32, 128), BF16),
            pltpu.VMEM((6, 10, 96, 128), BF16),
            pltpu.VMEM((4, 8, 64, 128), F32),
            pltpu.VMEM((4, 6, 64, 128), BF16),
            pltpu.VMEM((6, 8, 32, 128), BF16),
            pltpu.VMEM((4, 8, 192, 128), BF16),
            pltpu.VMEM((2, 6, 128, 128), BF16),
            pltpu.VMEM((3, 6, 128, 128), BF16),
            pltpu.VMEM((6, 10, 64, 128), BF16),
            pltpu.VMEM((16, 16, 896), BF16),
            pltpu.VMEM((128, 1792), BF16),
            pltpu.VMEM((192, 1152), BF16),
            pltpu.VMEM((128, 1792), F32),
            pltpu.VMEM((16, 16, 896), BF16),
            pltpu.VMEM((16, 16, 896), BF16),
            pltpu.VMEM((16, 896), BF16),
            pltpu.VMEM((8, 16, 896), BF16),
            pltpu.VMEM((64, 1024), F32),
            pltpu.VMEM((16, 16, 256), BF16),
            pltpu.VMEM((16, 16, 256), BF16),
            pltpu.VMEM((16, 256), F32),
            pltpu.VMEM((8, 16, 256), F32),
            pltpu.VMEM((16, 16, 256), BF16),
            dma((4, 8)),
            dma((4, 8)),
            dma((16,)),
            dma((16,)),
            dma((16,)),
            dma((16,)),
            dma((8,)),
            dma((8,)),
            dma((16,)),
            dma((16,)),
            dma((8,)),
            dma((8,)),
            dma((16,)),
            dma((16,)),
        ],
        compiler_params=pltpu.CompilerParams(
            collective_id=0, has_side_effects=True, vmem_limit_bytes=40 * 1024 * 1024
        ),
    )(x_in, a3, a6, f4, cot)

    grad_volume = jnp.transpose(gv, (2, 0, 1, 3))
    grad_three = jnp.transpose(g3[:, :864].reshape(64, 27, 32), (1, 0, 2))
    g4 = jnp.transpose(g4.reshape(2, 8, 896), (1, 0, 2)).reshape(8, 1792)
    grad_four = jnp.transpose(g4[:, :1728].reshape(8, 27, 64), (1, 0, 2))
    return (grad_volume, grad_three, grad_four)


def solution(mesh):
    in_specs = (
        P(None, "depth", "height", None),
        P(),
        P(None, "height", None),
        P(None, "depth", "height", None),
    )
    out_specs = (P(None, "depth", "height", None), P(), P(None, "height", None))
    return jax.shard_map(shards, mesh=mesh, in_specs=in_specs, out_specs=out_specs, check_vma=False)
```

```python
import functools
import math

import jax
import jax.numpy as jnp
from jax import lax
from jax.experimental import pallas as pl
from jax.experimental.pallas import tpu as pltpu
from jax.sharding import PartitionSpec as P

TANH_SCALE = 0.7978845608028654
CUBIC_TERM = 0.044715
MESH = pl.DeviceIdType.MESH
F32 = jnp.float32
BF16 = jnp.bfloat16

ND = 8
NH = 16
DIRECTIONS = [(dd, hh) for dd in (-1, 0, 1) for hh in (-1, 0, 1) if (dd, hh) != (0, 0)]


def gelu_parts(v):
    u = v * v
    inner = jnp.tanh(v * (TANH_SCALE + TANH_SCALE * CUBIC_TERM * u))
    half = 0.5 + 0.5 * inner
    value = v * half
    slope = half + value * (1.0 - inner) * (TANH_SCALE + 3.0 * TANH_SCALE * CUBIC_TERM * u)
    return value, slope


def stage(name, body):
    body()


def lanes_iota(shape):
    return lax.broadcasted_iota(jnp.int32, shape, len(shape) - 1)


def shifted(v, step):
    lane = lanes_iota(v.shape)
    before = jnp.where(lane < step, 0.0, pltpu.roll(v, step, 1))
    after = jnp.where(lane >= 128 - step, 0.0, pltpu.roll(v, 128 - step, 1))
    return before, after


def stack_width(row, step):
    before, after = shifted(row.astype(F32), step)
    return jnp.concatenate([before.astype(BF16), row, after.astype(BF16)], axis=0)


def part(at, cells, width, far):
    if at == 0:
        return pl.ds(width, cells)
    if at < 0:
        return pl.ds(cells + width, width) if far else pl.ds(width, width)
    return pl.ds(0, width) if far else pl.ds(cells, width)


def interleave(even_row, odd_row):
    even = lanes_iota(even_row.shape) % 2 == 0
    return jnp.where(even, even_row, pltpu.roll(odd_row, 1, 1))


def interleave_odd(even_row, odd_row):
    even = lanes_iota(even_row.shape) % 2 == 0
    return jnp.where(even, pltpu.roll(even_row, 127, 1), odd_row)


def two_rows(first, second):
    return jnp.concatenate([interleave(first, second), interleave_odd(first, second)], axis=0)


def kernel(
    x_hbm, f3_hbm, f4_hbm, cot_hbm,
    gv_out, g3_out, g4_out,
    x_in, f3, f4_in, cot, f4, a3, a6,
    xb, xx, slope3, ck, pk, pq, dq, dv, d3, dd3, bank, a4, a5,
    f4acc, r4, q4, t4, q4b,
    f3acc, r3, q3, t3, q3b, v3,
    in_sem, halo_s, halo_r, ag_s, ag_r, s4_s, s4_r, b4_s, b4_r, s3_s, s3_r, b3_s, b3_r, c3_s, c3_r,
):
    d = lax.axis_index("depth")
    h = lax.axis_index("height")

    def around(dd, hh):
        return (lax.rem(d + dd + ND, ND), lax.rem(h + hh + NH, NH))

    def partner(other):
        flip = lax.rem(lax.rem(h, 4) // 2 + lax.rem(other, 4) // 2, 2)
        return (d + flip * (1 - 2 * lax.rem(d, 2)), other)

    def each(low, high, body):
        def step(k, carry):
            body(k)
            return carry

        lax.fori_loop(low, high, step, 0)

    barrier = pltpu.get_barrier_semaphore()

    def greet(device):
        pl.semaphore_signal(barrier, inc=1, device_id=device, device_id_type=MESH)

    for dd, hh in DIRECTIONS:
        greet(around(dd, hh))
    for k in range(1, NH):
        greet(partner(lax.rem(h + k, NH)))
    for k in range(2, ND - 1):
        greet(around(k, 0))

    fetches = [
        pltpu.make_async_copy(src, dst, in_sem.at[n])
        for n, (src, dst) in enumerate(
            [(x_hbm, x_in), (f4_hbm, f4_in), (f3_hbm, f3), (cot_hbm, cot)]
        )
    ]
    for fetch in fetches:
        fetch.start()

    def rows_x():
        for i in range(4):
            block = jnp.transpose(x_in[:, i].astype(F32), (1, 0, 2)).astype(BF16)
            for j in range(8):
                xb[1 + i, 1 + j] = block[j]

    fetches[0].wait()
    stage("rows_x", rows_x)

    def rows_f4():
        taps = [f4_in[t].astype(F32) for t in range(27)] + [jnp.zeros((8, 64), F32)]
        tiles = [jnp.concatenate([taps[2 * m], taps[2 * m + 1]], axis=1) for m in range(14)]
        f4[...] = jnp.concatenate(
            [jnp.concatenate(tiles[:7], axis=1), jnp.concatenate(tiles[7:], axis=1)], axis=0
        ).astype(BF16)

    fetches[1].wait()
    stage("rows_f4", rows_f4)
    pl.semaphore_wait(barrier, 8 + NH - 1 + ND - 3)

    def halo_copy(which, n, buf, cells_d, cells_h, width):
        dd, hh = DIRECTIONS[n]
        return pltpu.make_async_remote_copy(
            src_ref=buf.at[part(dd, cells_d, width, False), part(hh, cells_h, width, False)],
            dst_ref=buf.at[part(dd, cells_d, width, True), part(hh, cells_h, width, True)],
            send_sem=halo_s.at[which, n],
            recv_sem=halo_r.at[which, n],
            device_id=around(dd, hh),
            device_id_type=MESH,
        )

    def halo_start(*which):
        for n in range(8):
            halo_copy(which[0], n, *which[1:]).start()

    def halo_wait(*which):
        for n in range(8):
            halo_copy(which[0], n, *which[1:]).wait_send()
        for n in range(8):
            halo_copy(which[0], n, *which[1:]).wait_recv()
        _, buf, cells_d, cells_h, width = which
        channels = buf.shape[2]
        across = (width, cells_h + 2 * width, channels, 128)
        along = (cells_d + 2 * width, width, channels, 128)

        @pl.when(d == 0)
        def _():
            buf[0:width] = jnp.zeros(across, BF16)

        @pl.when(d == ND - 1)
        def _():
            buf[cells_d + width : cells_d + 2 * width] = jnp.zeros(across, BF16)

        @pl.when(h == 0)
        def _():
            buf[:, 0:width] = jnp.zeros(along, BF16)

        @pl.when(h == NH - 1)
        def _():
            buf[:, cells_h + width : cells_h + 2 * width] = jnp.zeros(along, BF16)

    def scatter_h(src, dst, send, recv, k):
        other = lax.rem(h + k, NH)
        return pltpu.make_async_remote_copy(
            src_ref=src.at[other],
            dst_ref=dst.at[k],
            send_sem=send.at[k],
            recv_sem=recv.at[k],
            device_id=partner(other),
            device_id_type=MESH,
        )

    def share_d(src, dst, send, recv, k):
        return pltpu.make_async_remote_copy(
            src_ref=src,
            dst_ref=dst.at[k],
            send_sem=send.at[k],
            recv_sem=recv.at[k],
            device_id=around(k, 0),
            device_id_type=MESH,
        )

    def gather_send(src, dst, send, recv, k):
        return pltpu.make_async_remote_copy(
            src_ref=src,
            dst_ref=dst.at[h],
            send_sem=send.at[k],
            recv_sem=recv.at[k],
            device_id=partner(lax.rem(h + k, NH)),
            device_id_type=MESH,
        )

    def gather_recv(src, dst, send, recv, k):
        return pltpu.make_async_remote_copy(
            src_ref=src,
            dst_ref=dst.at[lax.rem(h - k + NH, NH)],
            send_sem=send.at[k],
            recv_sem=recv.at[k],
            device_id=partner(lax.rem(h + k, NH)),
            device_id_type=MESH,
        )

    halo_x = (0, xb, 4, 8, 1)
    halo_p = (1, pk, 2, 4, 2)
    halo_c = (2, ck, 2, 4, 1)
    halo_d3 = (3, d3, 4, 8, 1)
    halo_start(*halo_x)
    each(1, NH, lambda k: gather_send(f4, bank, ag_s, ag_r, k).start())
    bank[h] = f4[...]

    def dilate():
        at = 2 * lax.broadcasted_iota(jnp.int32, (64, 128), 0)
        to_even = (lanes_iota((64, 128)) == at).astype(F32).astype(BF16)
        for i in range(2):
            for j in range(4):
                wide = lax.dot_general(
                    cot[i, j], to_even, (((0,), (0,)), ((), ())), preferred_element_type=F32
                )
                ck[1 + i, 1 + j] = interleave(wide[:64], wide[64:]).astype(BF16)

    def rows_f3():
        flat = f3[...].astype(F32).reshape(864, 64)
        none = jnp.zeros((288, 64), F32)
        both = jnp.concatenate(
            [jnp.concatenate([flat, none], axis=0), jnp.concatenate([none, flat], axis=0)], axis=1
        )
        a3[...] = jnp.transpose(both).astype(BF16)
        a6[...] = jnp.concatenate(
            [flat[96 * ab : 96 * ab + 96] for ab in range(9)], axis=1
        ).astype(BF16)

    def stack_row(i, j):
        xx[i, j] = stack_width(xb[i, j], 1)

    def stack_x(i):
        for j in range(8):
            stack_row(1 + i, 1 + j)

    fetches[2].wait()
    stage("rows_f3", rows_f3)
    fetches[3].wait()
    stage("dilate", dilate)
    stage("stack_x", lambda: each(0, 4, stack_x))
    halo_wait(*halo_x)
    halo_start(*halo_c)

    def stack_rim():
        for j in range(10):
            stack_row(0, j)
            stack_row(5, j)
        for i in range(4):
            stack_row(1 + i, 0)
            stack_row(1 + i, 9)

    stage("stack_rim", stack_rim)

    def forward3(i):
        for j in range(4):
            cols = [
                jnp.concatenate(
                    [xx[2 * i + a, 2 * j + s + b] for a in range(4) for b in range(3)], axis=0
                )
                for s in range(2)
            ]
            act = jnp.dot(a3[...], jnp.concatenate(cols, axis=1), preferred_element_type=F32)
            value, slope = gelu_parts(act)
            for di in range(2):
                for s in range(2):
                    slope3[2 * i + di, 2 * j + s] = slope[
                        64 * di : 64 * di + 64, 128 * s : 128 * s + 128
                    ]
            total = value[:64] + value[64:]
            total = total[:, :128] + total[:, 128:]
            total = (total + pltpu.roll(total, 127, 1)) * 0.125
            pk[2 + i, 2 + j] = interleave(total[:32], total[32:]).astype(BF16)

    stage("forward3", lambda: each(0, 2, forward3))
    halo_start(*halo_p)

    def wait_gather(k):
        gather_send(f4, bank, ag_s, ag_r, k).wait_send()
        gather_recv(f4, bank, ag_s, ag_r, k).wait_recv()

    each(1, NH, wait_gather)

    def arrange():
        wide = [bank[s].astype(F32) for s in range(NH)]
        low = jnp.concatenate([w[:8] for w in wide], axis=0)
        high = jnp.concatenate([w[8:] for w in wide], axis=0)
        a4[...] = jnp.concatenate([low, high], axis=1).astype(BF16)
        for ab in range(9):
            a5[:, 128 * ab : 128 * ab + 128] = jnp.transpose(
                a4[:, 192 * ab : 192 * ab + 192].astype(F32)
            ).astype(BF16)

    stage("arrange", arrange)
    halo_wait(*halo_c)
    halo_wait(*halo_p)

    def stack_p(i):
        for j in range(8):
            both = two_rows(pk[i, j].astype(F32), pk[i + 2, j].astype(F32))
            before, after = shifted(both, 2)
            pq[i, j] = jnp.concatenate([before, both, after], axis=0).astype(BF16)

    stage("stack_p", lambda: each(0, 4, stack_p))

    def forward4(i):
        for j in range(3):
            cols = [
                jnp.concatenate(
                    [pq[i + a, 2 * j + s + b] for a in range(3) for b in range(3)], axis=0
                )
                for s in range(2)
            ]
            act = jnp.dot(
                a4[:, :1728], jnp.concatenate(cols, axis=1), preferred_element_type=F32
            )
            _, slope = gelu_parts(act)
            for s in range(2):
                col = 2 * j + s
                both = two_rows(ck[i, col].astype(F32), ck[i + 2, col].astype(F32))
                dq[i, col] = (both * slope[:, 128 * s : 128 * s + 128]).astype(BF16)

    stage("forward4", lambda: each(0, 2, forward4))

    def pair_rows():
        for j in range(6):
            one, two = dq[0, j].astype(F32), dq[1, j].astype(F32)
            even = lanes_iota(one.shape) % 2 == 0
            dv[0, j] = interleave_odd(one, two).astype(BF16)
            dv[1, j] = jnp.where(even, two, one).astype(BF16)
            dv[2, j] = interleave(one, two).astype(BF16)

    stage("pair_rows", pair_rows)

    def back4(j):
        cols = [
            jnp.concatenate([dv[a, 2 * j + s + 2 - b] for a in range(3) for b in range(3)], axis=0)
            for s in range(2)
        ]
        y = jnp.dot(a5[...], jnp.concatenate(cols, axis=1), preferred_element_type=F32)
        for s in range(2):
            ys = y[:, 128 * s : 128 * s + 128]
            _, from_after = shifted(ys[:64], 2)
            from_before, _ = shifted(ys[128:], 2)
            back = (ys[64:128] + from_after + from_before) * 0.125
            even = lanes_iota(back.shape) % 2 == 0
            spread = [
                jnp.where(even, back, pltpu.roll(back, 1, 1)),
                jnp.where(even, pltpu.roll(back, 127, 1), back),
            ]
            for i in range(2):
                for di in range(2):
                    for dj in range(2):
                        row, col = 2 * i + di, 2 * (2 * j + s) + dj
                        delta = spread[i] * slope3[row, col]
                        before, after = shifted(delta, 1)
                        stack = jnp.concatenate([after, delta, before], axis=0).astype(BF16)
                        dd3[row, col] = stack
                        d3[1 + row, 1 + col] = stack[64:128]

    stage("back4", lambda: each(0, 2, back4))
    halo_start(*halo_d3)

    f3acc[...] = jnp.zeros(f3acc.shape, F32)

    def weight3(i):
        left = jnp.concatenate(
            [
                jnp.concatenate([xb[i + a, j + b] for j in range(8)], axis=1)
                for a in range(3)
                for b in range(3)
            ],
            axis=0,
        )
        right = jnp.concatenate([dd3[i, j] for j in range(8)], axis=1)
        f3acc[...] += lax.dot_general(
            left, right, (((1,), (1,)), ((), ())), preferred_element_type=F32
        )

    stage("weight3", lambda: each(0, 4, weight3))

    def pack3():
        last = f3acc[:, 128:]
        flat = jnp.concatenate(
            [
                f3acc[:, :128],
                jnp.concatenate([last[:144], last[144:]], axis=1),
                jnp.zeros((80, 128), F32),
            ],
            axis=0,
        ).astype(BF16)
        for c in range(16):
            r3[c] = flat[32 * c : 32 * c + 32]

    stage("pack3", pack3)
    each(1, NH, lambda k: scatter_h(r3, q3, s3_s, s3_r, k).start())

    cells4 = [(i, j) for i in range(2) for j in range(4)]

    def weight4():
        even = lanes_iota((128, 128)) % 2 == 0
        left = jnp.concatenate(
            [
                jnp.where(even if i == 0 else ~even, dq[1 - i, 1 + j].astype(F32), 0.0)
                for i, j in cells4
            ],
            axis=1,
        ).astype(BF16)
        for g in range(5):
            taps = [ab for ab in (2 * g, 2 * g + 1) if ab < 9]
            right = jnp.concatenate(
                [
                    jnp.concatenate(
                        [pq[ab // 3 + 1 - i, j + ab % 3 + 1] for i, j in cells4], axis=1
                    )
                    for ab in taps
                ],
                axis=0,
            )
            piece = lax.dot_general(
                left, right, (((1,), (1,)), ((), ())), preferred_element_type=F32
            )
            if len(taps) == 1:
                piece = jnp.concatenate([piece, jnp.zeros((128, 64), F32)], axis=1)
            f4acc[:, 384 * g : 384 * g + piece.shape[1]] = piece

    stage("weight4", weight4)

    def pack4(s):
        rows = pl.ds(pl.multiple_of(8 * s, 8), 8)
        r4[s] = jnp.concatenate([f4acc[rows, :896], f4acc[rows, 896:]], axis=0).astype(BF16)

    stage("pack4", lambda: each(0, NH, pack4))
    each(1, NH, lambda k: scatter_h(r4, q4, s4_s, s4_r, k).start())

    def wait_both(copy):
        copy.wait_send()
        copy.wait_recv()

    each(1, NH, lambda k: wait_both(scatter_h(r3, q3, s3_s, s3_r, k)))

    def sum3():
        total3 = r3[h].astype(F32)
        for k in range(1, NH):
            total3 = total3 + q3[k].astype(F32)
        t3[...] = total3

    stage("sum3", sum3)
    each(1, ND, lambda k: share_d(t3, q3b, b3_s, b3_r, k).start())

    halo_wait(*halo_d3)

    def back3(i):
        done = []
        for j in range(4):
            cols = [
                jnp.concatenate(
                    [d3[i + 2 - a, 2 * j + s + 2 - b] for a in range(3) for b in range(3)], axis=0
                )
                for s in range(2)
            ]
            y = jnp.dot(a6[...], jnp.concatenate(cols, axis=1), preferred_element_type=F32)
            for s in range(2):
                ys = y[:, 128 * s : 128 * s + 128]
                _, from_after = shifted(ys[:32], 1)
                from_before, _ = shifted(ys[64:], 1)
                done.append(ys[32:64] + from_after + from_before)
        gv_out[:, i] = jnp.transpose(jnp.stack(done, axis=0), (1, 0, 2)).astype(BF16)

    stage("back3", lambda: each(0, 4, back3))

    each(1, NH, lambda k: wait_both(scatter_h(r4, q4, s4_s, s4_r, k)))

    def sum4():
        total4 = r4[h].astype(F32)
        for k in range(1, NH):
            total4 = total4 + q4[k].astype(F32)
        t4[...] = total4.astype(BF16)

    stage("sum4", sum4)
    each(1, ND, lambda k: share_d(t4, q4b, b4_s, b4_r, k).start())

    each(1, ND, lambda k: wait_both(share_d(t3, q3b, b3_s, b3_r, k)))
    whole3 = t3[...]
    for k in range(1, ND):
        whole3 = whole3 + q3b[k]
    v3[h] = (whole3 * (1.0 / math.sqrt(32 * 128 * 128))).astype(BF16)
    each(1, NH, lambda k: gather_send(v3.at[h], v3, c3_s, c3_r, k).start())

    each(1, ND, lambda k: wait_both(share_d(t4, q4b, b4_s, b4_r, k)))
    whole4 = t4[...].astype(F32)
    for k in range(1, ND):
        whole4 = whole4 + q4b[k].astype(F32)
    whole4 = whole4 * (1.0 / math.sqrt(16 * 64 * 64))
    for t in range(27):
        rows, lane = 8 * (t // 14), 64 * (t % 14)
        g4_out[t] = whole4[rows : rows + 8, lane : lane + 64]

    def wait_c3(k):
        gather_send(v3.at[h], v3, c3_s, c3_r, k).wait_send()
        gather_recv(v3.at[h], v3, c3_s, c3_r, k).wait_recv()

    each(1, NH, wait_c3)
    flat3 = jnp.concatenate([v3[c].astype(F32) for c in range(14)], axis=0)
    last3 = jnp.concatenate([flat3[288:432, :64], flat3[288:432, 64:]], axis=0)
    for ab in range(9):
        rows = slice(32 * ab, 32 * ab + 32)
        g3_out[3 * ab] = flat3[rows, :64]
        g3_out[3 * ab + 1] = flat3[rows, 64:]
        g3_out[3 * ab + 2] = last3[rows]


def shards(volume, filters_three, filters_four, cotangent):
    vmem = pl.BlockSpec(memory_space=pltpu.VMEM)
    hbm = pl.BlockSpec(memory_space=pl.ANY)
    dma = pltpu.SemaphoreType.DMA
    gv, g3, g4 = pl.pallas_call(
        kernel,
        out_shape=(
            jax.ShapeDtypeStruct((32, 4, 8, 128), BF16),
            jax.ShapeDtypeStruct((27, 32, 64), F32),
            jax.ShapeDtypeStruct((27, 8, 64), F32),
        ),
        in_specs=[hbm] * 4,
        out_specs=(vmem,) * 3,
        scratch_shapes=[
            pltpu.VMEM((32, 4, 8, 128), BF16),
            pltpu.VMEM((27, 32, 64), BF16),
            pltpu.VMEM((27, 8, 64), BF16),
            pltpu.VMEM((2, 4, 64, 128), BF16),
            pltpu.VMEM((16, 896), BF16),
            pltpu.VMEM((128, 1152), BF16),
            pltpu.VMEM((96, 576), BF16),
            pltpu.VMEM((6, 10, 32, 128), BF16),
            pltpu.VMEM((6, 10, 96, 128), BF16),
            pltpu.VMEM((4, 8, 64, 128), F32),
            pltpu.VMEM((4, 6, 64, 128), BF16),
            pltpu.VMEM((6, 8, 32, 128), BF16),
            pltpu.VMEM((4, 8, 192, 128), BF16),
            pltpu.VMEM((2, 6, 128, 128), BF16),
            pltpu.VMEM((3, 6, 128, 128), BF16),
            pltpu.VMEM((6, 10, 64, 128), BF16),
            pltpu.VMEM((4, 8, 192, 128), BF16),
            pltpu.VMEM((16, 16, 896), BF16),
            pltpu.VMEM((128, 1792), BF16),
            pltpu.VMEM((192, 1152), BF16),
            pltpu.VMEM((128, 1792), F32),
            pltpu.VMEM((16, 16, 896), BF16),
            pltpu.VMEM((16, 16, 896), BF16),
            pltpu.VMEM((16, 896), BF16),
            pltpu.VMEM((8, 16, 896), BF16),
            pltpu.VMEM((288, 192), F32),
            pltpu.VMEM((16, 32, 128), BF16),
            pltpu.VMEM((16, 32, 128), BF16),
            pltpu.VMEM((32, 128), F32),
            pltpu.VMEM((8, 32, 128), F32),
            pltpu.VMEM((16, 32, 128), BF16),
            dma((4,)),
            dma((4, 8)),
            dma((4, 8)),
            dma((16,)),
            dma((16,)),
            dma((16,)),
            dma((16,)),
            dma((8,)),
            dma((8,)),
            dma((16,)),
            dma((16,)),
            dma((8,)),
            dma((8,)),
            dma((16,)),
            dma((16,)),
        ],
        compiler_params=pltpu.CompilerParams(
            collective_id=0, has_side_effects=True, vmem_limit_bytes=40 * 1024 * 1024
        ),
    )(
        volume,
        jnp.transpose(filters_three, (0, 2, 1)),
        filters_four,
        jnp.transpose(cotangent, (1, 2, 3, 0)),
    )
    return (gv, jnp.transpose(g3, (0, 2, 1)), g4)


def solution(mesh):
    in_specs = (
        P(None, "depth", "height", None),
        P(),
        P(None, "height", None),
        P(None, "depth", "height", None),
    )
    out_specs = (P(None, "depth", "height", None), P(), P(None, "height", None))
    return jax.shard_map(shards, mesh=mesh, in_specs=in_specs, out_specs=out_specs, check_vma=False)
```

```python
import functools
import math

import jax
import jax.numpy as jnp
from jax import lax
from jax.experimental import pallas as pl
from jax.experimental.pallas import tpu as pltpu
from jax.sharding import PartitionSpec as P

TANH_SCALE = 0.7978845608028654
CUBIC_TERM = 0.044715
MESH = pl.DeviceIdType.MESH
F32 = jnp.float32
BF16 = jnp.bfloat16

ND = 8
NH = 16
DIRECTIONS = [(dd, hh) for dd in (-1, 0, 1) for hh in (-1, 0, 1) if (dd, hh) != (0, 0)]


def gelu_parts(v):
    u = v * v
    inner = jnp.tanh(v * (TANH_SCALE + TANH_SCALE * CUBIC_TERM * u))
    half = 0.5 + 0.5 * inner
    value = v * half
    slope = half + value * (1.0 - inner) * (TANH_SCALE + 3.0 * TANH_SCALE * CUBIC_TERM * u)
    return value, slope


def stage(name, body):
    body()


def lanes_iota(shape):
    return lax.broadcasted_iota(jnp.int32, shape, len(shape) - 1)


def shifted(v, step):
    lane = lanes_iota(v.shape)
    before = jnp.where(lane < step, 0.0, pltpu.roll(v, step, 1))
    after = jnp.where(lane >= 128 - step, 0.0, pltpu.roll(v, 128 - step, 1))
    return before, after


def stack_width(row, step):
    before, after = shifted(row.astype(F32), step)
    return jnp.concatenate([before.astype(BF16), row, after.astype(BF16)], axis=0)


def part(at, cells, width, far):
    if at == 0:
        return pl.ds(width, cells)
    if at < 0:
        return pl.ds(cells + width, width) if far else pl.ds(width, width)
    return pl.ds(0, width) if far else pl.ds(cells, width)


def interleave(even_row, odd_row):
    even = lanes_iota(even_row.shape) % 2 == 0
    return jnp.where(even, even_row, pltpu.roll(odd_row, 1, 1))


def interleave_odd(even_row, odd_row):
    even = lanes_iota(even_row.shape) % 2 == 0
    return jnp.where(even, pltpu.roll(even_row, 127, 1), odd_row)


def two_rows(first, second):
    return jnp.concatenate([interleave(first, second), interleave_odd(first, second)], axis=0)


def kernel(
    x_hbm, f3_hbm, f4_hbm, cot_hbm,
    gv_out, g3_out, g4_out,
    x_in, f3, f4_in, cot, f4, a3, a6,
    xb, xx, slope3, ck, pk, pq, dq, dv, d3, dd3, bank, a4, a5,
    f4acc, r4, q4, t4, q4b,
    f3acc, r3, q3, t3, q3b, v3,
    in_sem, halo_s, halo_r, ag_s, ag_r, s4_s, s4_r, b4_s, b4_r, s3_s, s3_r, b3_s, b3_r, c3_s, c3_r,
):
    d = lax.axis_index("depth")
    h = lax.axis_index("height")

    def around(dd, hh):
        return (lax.rem(d + dd + ND, ND), lax.rem(h + hh + NH, NH))

    def partner(other):
        flip = lax.rem(lax.rem(h, 4) // 2 + lax.rem(other, 4) // 2, 2)
        return (d + flip * (1 - 2 * lax.rem(d, 2)), other)

    def each(low, high, body):
        def step(k, carry):
            body(k)
            return carry

        lax.fori_loop(low, high, step, 0)

    barrier = pltpu.get_barrier_semaphore()

    def greet(device):
        pl.semaphore_signal(barrier, inc=1, device_id=device, device_id_type=MESH)

    for dd, hh in DIRECTIONS:
        greet(around(dd, hh))
    for k in range(1, NH):
        greet(partner(lax.rem(h + k, NH)))
    for k in range(2, ND - 1):
        greet(around(k, 0))

    fetches = [
        pltpu.make_async_copy(src, dst, in_sem.at[n])
        for n, (src, dst) in enumerate(
            [(x_hbm, x_in), (f4_hbm, f4_in), (f3_hbm, f3), (cot_hbm, cot)]
        )
    ]
    for fetch in fetches:
        fetch.start()

    def rows_x():
        for i in range(4):
            block = jnp.transpose(x_in[:, i].astype(F32), (1, 0, 2)).astype(BF16)
            for j in range(8):
                xb[1 + i, 1 + j] = block[j]

    fetches[0].wait()
    stage("rows_x", rows_x)

    def rows_f4():
        taps = [f4_in[t].astype(F32) for t in range(27)] + [jnp.zeros((8, 64), F32)]
        tiles = [jnp.concatenate([taps[2 * m], taps[2 * m + 1]], axis=1) for m in range(14)]
        f4[...] = jnp.concatenate(
            [jnp.concatenate(tiles[:7], axis=1), jnp.concatenate(tiles[7:], axis=1)], axis=0
        ).astype(BF16)

    fetches[1].wait()
    stage("rows_f4", rows_f4)
    pl.semaphore_wait(barrier, 8 + NH - 1 + ND - 3)

    def halo_copy(which, n, buf, cells_d, cells_h, width):
        dd, hh = DIRECTIONS[n]
        return pltpu.make_async_remote_copy(
            src_ref=buf.at[part(dd, cells_d, width, False), part(hh, cells_h, width, False)],
            dst_ref=buf.at[part(dd, cells_d, width, True), part(hh, cells_h, width, True)],
            send_sem=halo_s.at[which, n],
            recv_sem=halo_r.at[which, n],
            device_id=around(dd, hh),
            device_id_type=MESH,
        )

    def halo_start(*which):
        for n in range(8):
            halo_copy(which[0], n, *which[1:]).start()

    def halo_wait(*which):
        for n in range(8):
            halo_copy(which[0], n, *which[1:]).wait_send()
        for n in range(8):
            halo_copy(which[0], n, *which[1:]).wait_recv()
        _, buf, cells_d, cells_h, width = which
        channels = buf.shape[2]
        across = (width, cells_h + 2 * width, channels, 128)
        along = (cells_d + 2 * width, width, channels, 128)

        @pl.when(d == 0)
        def _():
            buf[0:width] = jnp.zeros(across, BF16)

        @pl.when(d == ND - 1)
        def _():
            buf[cells_d + width : cells_d + 2 * width] = jnp.zeros(across, BF16)

        @pl.when(h == 0)
        def _():
            buf[:, 0:width] = jnp.zeros(along, BF16)

        @pl.when(h == NH - 1)
        def _():
            buf[:, cells_h + width : cells_h + 2 * width] = jnp.zeros(along, BF16)

    def scatter_h(src, dst, send, recv, k):
        other = lax.rem(h + k, NH)
        return pltpu.make_async_remote_copy(
            src_ref=src.at[other],
            dst_ref=dst.at[k],
            send_sem=send.at[k],
            recv_sem=recv.at[k],
            device_id=partner(other),
            device_id_type=MESH,
        )

    def share_d(src, dst, send, recv, k):
        return pltpu.make_async_remote_copy(
            src_ref=src,
            dst_ref=dst.at[k],
            send_sem=send.at[k],
            recv_sem=recv.at[k],
            device_id=around(k, 0),
            device_id_type=MESH,
        )

    def gather_send(src, dst, send, recv, k):
        return pltpu.make_async_remote_copy(
            src_ref=src,
            dst_ref=dst.at[h],
            send_sem=send.at[k],
            recv_sem=recv.at[k],
            device_id=partner(lax.rem(h + k, NH)),
            device_id_type=MESH,
        )

    def gather_recv(src, dst, send, recv, k):
        return pltpu.make_async_remote_copy(
            src_ref=src,
            dst_ref=dst.at[lax.rem(h - k + NH, NH)],
            send_sem=send.at[k],
            recv_sem=recv.at[k],
            device_id=partner(lax.rem(h + k, NH)),
            device_id_type=MESH,
        )

    halo_x = (0, xb, 4, 8, 1)
    halo_p = (1, pk, 2, 4, 2)
    halo_c = (2, ck, 2, 4, 1)
    halo_d3 = (3, d3, 4, 8, 1)
    halo_start(*halo_x)
    each(1, NH, lambda k: gather_send(f4, bank, ag_s, ag_r, k).start())
    bank[h] = f4[...]

    def dilate():
        at = 2 * lax.broadcasted_iota(jnp.int32, (64, 128), 0)
        to_even = (lanes_iota((64, 128)) == at).astype(F32).astype(BF16)
        for i in range(2):
            for j in range(4):
                wide = lax.dot_general(
                    cot[i, j], to_even, (((0,), (0,)), ((), ())), preferred_element_type=F32
                )
                ck[1 + i, 1 + j] = interleave(wide[:64], wide[64:]).astype(BF16)

    def rows_f3():
        flat = f3[...].astype(F32).reshape(864, 64)
        none = jnp.zeros((288, 64), F32)
        both = jnp.concatenate(
            [jnp.concatenate([flat, none], axis=0), jnp.concatenate([none, flat], axis=0)], axis=1
        )
        a3[...] = jnp.transpose(both).astype(BF16)
        a6[...] = jnp.concatenate(
            [flat[96 * ab : 96 * ab + 96] for ab in range(9)], axis=1
        ).astype(BF16)

    def stack_row(i, j):
        xx[i, j] = stack_width(xb[i, j], 1)

    def stack_x(i):
        for j in range(8):
            stack_row(1 + i, 1 + j)

    fetches[3].wait()
    stage("dilate", dilate)
    halo_start(*halo_c)
    fetches[2].wait()
    stage("rows_f3", rows_f3)
    stage("stack_x", lambda: each(0, 4, stack_x))
    halo_wait(*halo_x)

    def stack_rim():
        for j in range(10):
            stack_row(0, j)
            stack_row(5, j)
        for i in range(4):
            stack_row(1 + i, 0)
            stack_row(1 + i, 9)

    stage("stack_rim", stack_rim)

    def forward3(i):
        for j in range(4):
            cols = [
                jnp.concatenate(
                    [xx[2 * i + a, 2 * j + s + b] for a in range(4) for b in range(3)], axis=0
                )
                for s in range(2)
            ]
            act = jnp.dot(a3[...], jnp.concatenate(cols, axis=1), preferred_element_type=F32)
            value, slope = gelu_parts(act)
            for di in range(2):
                for s in range(2):
                    slope3[2 * i + di, 2 * j + s] = slope[
                        64 * di : 64 * di + 64, 128 * s : 128 * s + 128
                    ]
            total = value[:64] + value[64:]
            total = total[:, :128] + total[:, 128:]
            total = (total + pltpu.roll(total, 127, 1)) * 0.125
            pk[2 + i, 2 + j] = interleave(total[:32], total[32:]).astype(BF16)

    stage("forward3", lambda: each(0, 2, forward3))
    halo_start(*halo_p)

    def wait_gather(k):
        gather_send(f4, bank, ag_s, ag_r, k).wait_send()
        gather_recv(f4, bank, ag_s, ag_r, k).wait_recv()

    each(1, NH, wait_gather)

    def arrange():
        wide = [bank[s].astype(F32) for s in range(NH)]
        low = jnp.concatenate([w[:8] for w in wide], axis=0)
        high = jnp.concatenate([w[8:] for w in wide], axis=0)
        a4[...] = jnp.concatenate([low, high], axis=1).astype(BF16)
        for ab in range(9):
            a5[:, 128 * ab : 128 * ab + 128] = jnp.transpose(
                a4[:, 192 * ab : 192 * ab + 192].astype(F32)
            ).astype(BF16)

    stage("arrange", arrange)
    halo_wait(*halo_c)
    halo_wait(*halo_p)

    def stack_p(i):
        for j in range(8):
            both = two_rows(pk[i, j].astype(F32), pk[i + 2, j].astype(F32))
            before, after = shifted(both, 2)
            pq[i, j] = jnp.concatenate([before, both, after], axis=0).astype(BF16)

    stage("stack_p", lambda: each(0, 4, stack_p))

    def forward4(i):
        for j in range(3):
            cols = [
                jnp.concatenate(
                    [pq[i + a, 2 * j + s + b] for a in range(3) for b in range(3)], axis=0
                )
                for s in range(2)
            ]
            act = jnp.dot(
                a4[:, :1728], jnp.concatenate(cols, axis=1), preferred_element_type=F32
            )
            _, slope = gelu_parts(act)
            for s in range(2):
                col = 2 * j + s
                both = two_rows(ck[i, col].astype(F32), ck[i + 2, col].astype(F32))
                dq[i, col] = (both * slope[:, 128 * s : 128 * s + 128]).astype(BF16)

    stage("forward4", lambda: each(0, 2, forward4))

    def pair_rows():
        for j in range(6):
            one, two = dq[0, j].astype(F32), dq[1, j].astype(F32)
            even = lanes_iota(one.shape) % 2 == 0
            dv[0, j] = interleave_odd(one, two).astype(BF16)
            dv[1, j] = jnp.where(even, two, one).astype(BF16)
            dv[2, j] = interleave(one, two).astype(BF16)

    stage("pair_rows", pair_rows)

    def back4(j):
        cols = [
            jnp.concatenate([dv[a, 2 * j + s + 2 - b] for a in range(3) for b in range(3)], axis=0)
            for s in range(2)
        ]
        y = jnp.dot(a5[...], jnp.concatenate(cols, axis=1), preferred_element_type=F32)
        for s in range(2):
            ys = y[:, 128 * s : 128 * s + 128]
            _, from_after = shifted(ys[:64], 2)
            from_before, _ = shifted(ys[128:], 2)
            back = (ys[64:128] + from_after + from_before) * 0.125
            even = lanes_iota(back.shape) % 2 == 0
            spread = [
                jnp.where(even, back, pltpu.roll(back, 1, 1)),
                jnp.where(even, pltpu.roll(back, 127, 1), back),
            ]
            for i in range(2):
                for di in range(2):
                    for dj in range(2):
                        row, col = 2 * i + di, 2 * (2 * j + s) + dj
                        delta = spread[i] * slope3[row, col]
                        before, after = shifted(delta, 1)
                        stack = jnp.concatenate([after, delta, before], axis=0).astype(BF16)
                        dd3[row, col] = stack
                        d3[1 + row, 1 + col] = stack[64:128]

    stage("back4", lambda: each(0, 2, back4))
    halo_start(*halo_d3)

    f3acc[...] = jnp.zeros(f3acc.shape, F32)

    def weight3(i):
        left = jnp.concatenate(
            [
                jnp.concatenate([xb[i + a, j + b] for j in range(8)], axis=1)
                for a in range(3)
                for b in range(3)
            ],
            axis=0,
        )
        right = jnp.concatenate([dd3[i, j] for j in range(8)], axis=1)
        f3acc[...] += lax.dot_general(
            left, right, (((1,), (1,)), ((), ())), preferred_element_type=F32
        )

    stage("weight3", lambda: each(0, 4, weight3))

    def pack3():
        last = f3acc[:, 128:]
        flat = jnp.concatenate(
            [
                f3acc[:, :128],
                jnp.concatenate([last[:144], last[144:]], axis=1),
                jnp.zeros((80, 128), F32),
            ],
            axis=0,
        ).astype(BF16)
        for c in range(16):
            r3[c] = flat[32 * c : 32 * c + 32]

    stage("pack3", pack3)
    each(1, NH, lambda k: scatter_h(r3, q3, s3_s, s3_r, k).start())

    cells4 = [(i, j) for i in range(2) for j in range(4)]

    def weight4():
        even = lanes_iota((128, 128)) % 2 == 0
        left = jnp.concatenate(
            [
                jnp.where(even if i == 0 else ~even, dq[1 - i, 1 + j].astype(F32), 0.0)
                for i, j in cells4
            ],
            axis=1,
        ).astype(BF16)
        for g in range(5):
            taps = [ab for ab in (2 * g, 2 * g + 1) if ab < 9]
            right = jnp.concatenate(
                [
                    jnp.concatenate(
                        [pq[ab // 3 + 1 - i, j + ab % 3 + 1] for i, j in cells4], axis=1
                    )
                    for ab in taps
                ],
                axis=0,
            )
            piece = lax.dot_general(
                left, right, (((1,), (1,)), ((), ())), preferred_element_type=F32
            )
            if len(taps) == 1:
                piece = jnp.concatenate([piece, jnp.zeros((128, 64), F32)], axis=1)
            f4acc[:, 384 * g : 384 * g + piece.shape[1]] = piece

    stage("weight4", weight4)

    def pack4(s):
        rows = pl.ds(pl.multiple_of(8 * s, 8), 8)
        r4[s] = jnp.concatenate([f4acc[rows, :896], f4acc[rows, 896:]], axis=0).astype(BF16)

    stage("pack4", lambda: each(0, NH, pack4))
    each(1, NH, lambda k: scatter_h(r4, q4, s4_s, s4_r, k).start())

    def wait_both(copy):
        copy.wait_send()
        copy.wait_recv()

    each(1, NH, lambda k: wait_both(scatter_h(r3, q3, s3_s, s3_r, k)))

    def sum3():
        total3 = r3[h].astype(F32)
        for k in range(1, NH):
            total3 = total3 + q3[k].astype(F32)
        t3[...] = total3

    stage("sum3", sum3)
    each(1, ND, lambda k: share_d(t3, q3b, b3_s, b3_r, k).start())

    halo_wait(*halo_d3)

    def back3(i):
        done = []
        for j in range(4):
            cols = [
                jnp.concatenate(
                    [d3[i + 2 - a, 2 * j + s + 2 - b] for a in range(3) for b in range(3)], axis=0
                )
                for s in range(2)
            ]
            y = jnp.dot(a6[...], jnp.concatenate(cols, axis=1), preferred_element_type=F32)
            for s in range(2):
                ys = y[:, 128 * s : 128 * s + 128]
                _, from_after = shifted(ys[:32], 1)
                from_before, _ = shifted(ys[64:], 1)
                done.append(ys[32:64] + from_after + from_before)
        gv_out[:, i] = jnp.transpose(jnp.stack(done, axis=0), (1, 0, 2)).astype(BF16)

    stage("back3", lambda: each(0, 4, back3))

    each(1, NH, lambda k: wait_both(scatter_h(r4, q4, s4_s, s4_r, k)))

    def sum4():
        total4 = r4[h].astype(F32)
        for k in range(1, NH):
            total4 = total4 + q4[k].astype(F32)
        t4[...] = total4.astype(BF16)

    stage("sum4", sum4)
    each(1, ND, lambda k: share_d(t4, q4b, b4_s, b4_r, k).start())

    each(1, ND, lambda k: wait_both(share_d(t3, q3b, b3_s, b3_r, k)))
    whole3 = t3[...]
    for k in range(1, ND):
        whole3 = whole3 + q3b[k]
    v3[h] = (whole3 * (1.0 / math.sqrt(32 * 128 * 128))).astype(BF16)
    each(1, NH, lambda k: gather_send(v3.at[h], v3, c3_s, c3_r, k).start())

    each(1, ND, lambda k: wait_both(share_d(t4, q4b, b4_s, b4_r, k)))
    whole4 = t4[...].astype(F32)
    for k in range(1, ND):
        whole4 = whole4 + q4b[k].astype(F32)
    whole4 = whole4 * (1.0 / math.sqrt(16 * 64 * 64))
    for t in range(27):
        rows, lane = 8 * (t // 14), 64 * (t % 14)
        g4_out[t] = whole4[rows : rows + 8, lane : lane + 64]

    def wait_c3(k):
        gather_send(v3.at[h], v3, c3_s, c3_r, k).wait_send()
        gather_recv(v3.at[h], v3, c3_s, c3_r, k).wait_recv()

    each(1, NH, wait_c3)
    flat3 = jnp.concatenate([v3[c].astype(F32) for c in range(14)], axis=0)
    last3 = jnp.concatenate([flat3[288:432, :64], flat3[288:432, 64:]], axis=0)
    for ab in range(9):
        rows = slice(32 * ab, 32 * ab + 32)
        g3_out[3 * ab] = flat3[rows, :64]
        g3_out[3 * ab + 1] = flat3[rows, 64:]
        g3_out[3 * ab + 2] = last3[rows]


def shards(volume, filters_three, filters_four, cotangent):
    vmem = pl.BlockSpec(memory_space=pltpu.VMEM)
    hbm = pl.BlockSpec(memory_space=pl.ANY)
    dma = pltpu.SemaphoreType.DMA
    gv, g3, g4 = pl.pallas_call(
        kernel,
        out_shape=(
            pltpu.VMEM((32, 4, 8, 128), BF16),
            pltpu.VMEM((27, 32, 64), F32),
            pltpu.VMEM((27, 8, 64), F32),
        ),
        in_specs=[hbm] * 4,
        out_specs=(vmem,) * 3,
        scratch_shapes=[
            pltpu.VMEM((32, 4, 8, 128), BF16),
            pltpu.VMEM((27, 32, 64), BF16),
            pltpu.VMEM((27, 8, 64), BF16),
            pltpu.VMEM((2, 4, 64, 128), BF16),
            pltpu.VMEM((16, 896), BF16),
            pltpu.VMEM((128, 1152), BF16),
            pltpu.VMEM((96, 576), BF16),
            pltpu.VMEM((6, 10, 32, 128), BF16),
            pltpu.VMEM((6, 10, 96, 128), BF16),
            pltpu.VMEM((4, 8, 64, 128), F32),
            pltpu.VMEM((4, 6, 64, 128), BF16),
            pltpu.VMEM((6, 8, 32, 128), BF16),
            pltpu.VMEM((4, 8, 192, 128), BF16),
            pltpu.VMEM((2, 6, 128, 128), BF16),
            pltpu.VMEM((3, 6, 128, 128), BF16),
            pltpu.VMEM((6, 10, 64, 128), BF16),
            pltpu.VMEM((4, 8, 192, 128), BF16),
            pltpu.VMEM((16, 16, 896), BF16),
            pltpu.VMEM((128, 1792), BF16),
            pltpu.VMEM((192, 1152), BF16),
            pltpu.VMEM((128, 1792), F32),
            pltpu.VMEM((16, 16, 896), BF16),
            pltpu.VMEM((16, 16, 896), BF16),
            pltpu.VMEM((16, 896), BF16),
            pltpu.VMEM((8, 16, 896), BF16),
            pltpu.VMEM((288, 192), F32),
            pltpu.VMEM((16, 32, 128), BF16),
            pltpu.VMEM((16, 32, 128), BF16),
            pltpu.VMEM((32, 128), F32),
            pltpu.VMEM((8, 32, 128), F32),
            pltpu.VMEM((16, 32, 128), BF16),
            dma((4,)),
            dma((4, 8)),
            dma((4, 8)),
            dma((16,)),
            dma((16,)),
            dma((16,)),
            dma((16,)),
            dma((8,)),
            dma((8,)),
            dma((16,)),
            dma((16,)),
            dma((8,)),
            dma((8,)),
            dma((16,)),
            dma((16,)),
        ],
        compiler_params=pltpu.CompilerParams(
            collective_id=0, has_side_effects=True, vmem_limit_bytes=58000 * 1024
        ),
    )(
        volume,
        jnp.transpose(filters_three, (0, 2, 1)),
        filters_four,
        jnp.transpose(cotangent, (1, 2, 3, 0)),
    )
    return (gv, jnp.transpose(g3, (0, 2, 1)), g4)


def solution(mesh):
    in_specs = (
        P(None, "depth", "height", None),
        P(),
        P(None, "height", None),
        P(None, "depth", "height", None),
    )
    out_specs = (P(None, "depth", "height", None), P(), P(None, "height", None))
    return jax.shard_map(shards, mesh=mesh, in_specs=in_specs, out_specs=out_specs, check_vma=False)
```

```python
import functools
import math

import jax
import jax.numpy as jnp
from jax import lax
from jax.experimental import pallas as pl
from jax.experimental.pallas import tpu as pltpu
from jax.sharding import PartitionSpec as P

TANH_SCALE = 0.7978845608028654
CUBIC_TERM = 0.044715
MESH = pl.DeviceIdType.MESH
F32 = jnp.float32
BF16 = jnp.bfloat16

ND = 8
NH = 16
DIRECTIONS = [(dd, hh) for dd in (-1, 0, 1) for hh in (-1, 0, 1) if (dd, hh) != (0, 0)]


def gelu_parts(v):
    u = v * v
    inner = jnp.tanh(v * (TANH_SCALE + TANH_SCALE * CUBIC_TERM * u))
    half = 0.5 + 0.5 * inner
    value = v * half
    slope = half + value * (1.0 - inner) * (TANH_SCALE + 3.0 * TANH_SCALE * CUBIC_TERM * u)
    return value, slope


def stage(name, body):
    body()


def lanes_iota(shape):
    return lax.broadcasted_iota(jnp.int32, shape, len(shape) - 1)


def shifted(v, step):
    lane = lanes_iota(v.shape)
    zero = jnp.zeros((), v.dtype)
    before = jnp.where(lane < step, zero, pltpu.roll(v, step, 1))
    after = jnp.where(lane >= 128 - step, zero, pltpu.roll(v, 128 - step, 1))
    return before, after


def stack_width(row, step):
    before, after = shifted(row, step)
    return jnp.concatenate([before, row, after], axis=0)


def part(at, cells, width, far):
    if at == 0:
        return pl.ds(width, cells)
    if at < 0:
        return pl.ds(cells + width, width) if far else pl.ds(width, width)
    return pl.ds(0, width) if far else pl.ds(cells, width)


def interleave(even_row, odd_row):
    even = lanes_iota(even_row.shape) % 2 == 0
    return jnp.where(even, even_row, pltpu.roll(odd_row, 1, 1))


def interleave_odd(even_row, odd_row):
    even = lanes_iota(even_row.shape) % 2 == 0
    return jnp.where(even, pltpu.roll(even_row, 127, 1), odd_row)


def two_rows(first, second):
    return jnp.concatenate([interleave(first, second), interleave_odd(first, second)], axis=0)


def kernel(
    x_hbm, f3_hbm, f4_hbm, cot_hbm,
    gv_out, g3_out, g4_out,
    x_in, f3, f4_in, cot, f4, a3, a6,
    xb, xx, slope3, ck, pk, pq, dq, dv, d3, dd3, rim, near, gown, bank, a4, a5,
    f4acc, r4, q40, r4b, q4, t4, q4b,
    f3acc, r3, q3, t3, q3b, v3,
    in_sem, halo_s, halo_r, s40_s, s40_r, ag_s, ag_r, s4_s, s4_r, b4_s, b4_r, s3_s, s3_r, b3_s, b3_r, c3_s, c3_r,
):
    d = lax.axis_index("depth")
    h = lax.axis_index("height")

    def around(dd, hh):
        return (lax.rem(d + dd + ND, ND), lax.rem(h + hh + NH, NH))

    def partner(other):
        flip = lax.rem(lax.rem(h, 4) // 2 + lax.rem(other, 4) // 2, 2)
        return (d + flip * (1 - 2 * lax.rem(d, 2)), other)

    def each(low, high, body):
        def step(k, carry):
            body(k)
            return carry

        lax.fori_loop(low, high, step, 0)

    barrier = pltpu.get_barrier_semaphore()

    def greet(device):
        pl.semaphore_signal(barrier, inc=1, device_id=device, device_id_type=MESH)

    for dd, hh in DIRECTIONS:
        greet(around(dd, hh))
    for k in range(1, NH):
        greet(partner(lax.rem(h + k, NH)))
    for k in range(2, ND - 1):
        greet(around(k, 0))

    fetches = [
        pltpu.make_async_copy(src, dst, in_sem.at[n])
        for n, (src, dst) in enumerate(
            [(x_hbm, x_in), (f4_hbm, f4_in), (f3_hbm, f3), (cot_hbm, cot)]
        )
    ]
    for fetch in fetches:
        fetch.start()

    def rows_x():
        for i in range(4):
            block = jnp.transpose(x_in[:, i].astype(F32), (1, 0, 2)).astype(BF16)
            for j in range(8):
                xb[1 + i, 1 + j] = block[j]

    fetches[0].wait()
    stage("rows_x", rows_x)

    def rows_f4():
        taps = [f4_in[t].astype(F32) for t in range(27)] + [jnp.zeros((8, 64), F32)]
        tiles = [jnp.concatenate([taps[2 * m], taps[2 * m + 1]], axis=1) for m in range(14)]
        f4[...] = jnp.concatenate(
            [jnp.concatenate(tiles[:7], axis=1), jnp.concatenate(tiles[7:], axis=1)], axis=0
        ).astype(BF16)

    fetches[1].wait()
    stage("rows_f4", rows_f4)
    pl.semaphore_wait(barrier, 8 + NH - 1 + ND - 3)

    def halo_copy(which, n, buf, cells_d, cells_h, width, beyond=None):
        dd, hh = DIRECTIONS[n]
        if beyond is None:
            src = buf.at[part(dd, cells_d, width, False), part(hh, cells_h, width, False)]
        else:
            src = beyond.at[part(-dd, cells_d, width, True), part(-hh, cells_h, width, True)]
        return pltpu.make_async_remote_copy(
            src_ref=src,
            dst_ref=buf.at[part(dd, cells_d, width, True), part(hh, cells_h, width, True)],
            send_sem=halo_s.at[which, n],
            recv_sem=halo_r.at[which, n],
            device_id=around(dd, hh),
            device_id_type=MESH,
        )

    def halo_start(*which):
        for n in range(8):
            halo_copy(which[0], n, *which[1:]).start()

    def halo_wait(*which):
        for n in range(8):
            halo_copy(which[0], n, *which[1:]).wait_send()
        for n in range(8):
            halo_copy(which[0], n, *which[1:]).wait_recv()
        _, buf, cells_d, cells_h, width = which[:5]
        channels = buf.shape[2]
        across = (width, cells_h + 2 * width, channels, 128)
        along = (cells_d + 2 * width, width, channels, 128)

        @pl.when(d == 0)
        def _():
            buf[0:width] = jnp.zeros(across, BF16)

        @pl.when(d == ND - 1)
        def _():
            buf[cells_d + width : cells_d + 2 * width] = jnp.zeros(across, BF16)

        @pl.when(h == 0)
        def _():
            buf[:, 0:width] = jnp.zeros(along, BF16)

        @pl.when(h == NH - 1)
        def _():
            buf[:, cells_h + width : cells_h + 2 * width] = jnp.zeros(along, BF16)

    def scatter_h(src, dst, send, recv, k):
        other = lax.rem(h + k, NH)
        return pltpu.make_async_remote_copy(
            src_ref=src.at[other],
            dst_ref=dst.at[k],
            send_sem=send.at[k],
            recv_sem=recv.at[k],
            device_id=partner(other),
            device_id_type=MESH,
        )

    def share_d(src, dst, send, recv, k):
        return pltpu.make_async_remote_copy(
            src_ref=src,
            dst_ref=dst.at[k],
            send_sem=send.at[k],
            recv_sem=recv.at[k],
            device_id=around(k, 0),
            device_id_type=MESH,
        )

    def gather_send(src, dst, send, recv, k):
        return pltpu.make_async_remote_copy(
            src_ref=src,
            dst_ref=dst.at[h],
            send_sem=send.at[k],
            recv_sem=recv.at[k],
            device_id=partner(lax.rem(h + k, NH)),
            device_id_type=MESH,
        )

    def gather_recv(src, dst, send, recv, k):
        return pltpu.make_async_remote_copy(
            src_ref=src,
            dst_ref=dst.at[lax.rem(h - k + NH, NH)],
            send_sem=send.at[k],
            recv_sem=recv.at[k],
            device_id=partner(lax.rem(h + k, NH)),
            device_id_type=MESH,
        )

    halo_x = (0, xb, 4, 8, 1)
    halo_p = (1, pk, 2, 4, 2)
    halo_c = (2, ck, 2, 4, 1)
    halo_g = (3, near, 4, 8, 1, rim)
    halo_start(*halo_x)
    each(1, NH, lambda k: gather_send(f4, bank, ag_s, ag_r, k).start())
    bank[h] = f4[...]

    def dilate():
        at = 2 * lax.broadcasted_iota(jnp.int32, (64, 128), 0)
        to_even = (lanes_iota((64, 128)) == at).astype(F32).astype(BF16)
        for i in range(2):
            for j in range(4):
                wide = lax.dot_general(
                    cot[i, j], to_even, (((0,), (0,)), ((), ())), preferred_element_type=F32
                )
                ck[1 + i, 1 + j] = interleave(wide[:64], wide[64:]).astype(BF16)

    def rows_f3():
        flat = f3[...].astype(F32).reshape(864, 64)
        none = jnp.zeros((288, 64), F32)
        both = jnp.concatenate(
            [jnp.concatenate([flat, none], axis=0), jnp.concatenate([none, flat], axis=0)], axis=1
        )
        a3[...] = jnp.transpose(both).astype(BF16)
        a6[...] = jnp.concatenate(
            [flat[96 * ab : 96 * ab + 96] for ab in range(9)], axis=1
        ).astype(BF16)

    def stack_row(i, j):
        xx[i, j] = stack_width(xb[i, j], 1)

    def stack_x(i):
        for j in range(8):
            stack_row(1 + i, 1 + j)

    fetches[3].wait()
    stage("dilate", dilate)
    halo_start(*halo_c)
    fetches[2].wait()
    stage("rows_f3", rows_f3)
    stage("stack_x", lambda: each(0, 4, stack_x))
    halo_wait(*halo_x)

    def stack_rim():
        for j in range(10):
            stack_row(0, j)
            stack_row(5, j)
        for i in range(4):
            stack_row(1 + i, 0)
            stack_row(1 + i, 9)

    stage("stack_rim", stack_rim)

    def forward3(i):
        for j in range(4):
            cols = [
                jnp.concatenate(
                    [xx[2 * i + a, 2 * j + s + b] for a in range(4) for b in range(3)], axis=0
                )
                for s in range(2)
            ]
            act = jnp.dot(a3[...], jnp.concatenate(cols, axis=1), preferred_element_type=F32)
            value, slope = gelu_parts(act)
            for di in range(2):
                for s in range(2):
                    slope3[2 * i + di, 2 * j + s] = slope[
                        64 * di : 64 * di + 64, 128 * s : 128 * s + 128
                    ]
            total = value[:64] + value[64:]
            total = total[:, :128] + total[:, 128:]
            total = (total + pltpu.roll(total, 127, 1)) * 0.125
            pk[2 + i, 2 + j] = interleave(total[:32], total[32:]).astype(BF16)

    stage("forward3", lambda: each(0, 2, forward3))
    halo_start(*halo_p)

    def wait_gather(k):
        gather_send(f4, bank, ag_s, ag_r, k).wait_send()
        gather_recv(f4, bank, ag_s, ag_r, k).wait_recv()

    each(1, NH, wait_gather)

    def arrange():
        wide = [bank[s].astype(F32) for s in range(NH)]
        low = jnp.concatenate([w[:8] for w in wide], axis=0)
        high = jnp.concatenate([w[8:] for w in wide], axis=0)
        a4[...] = jnp.concatenate([low, high], axis=1).astype(BF16)
        for ab in range(9):
            a5[:, 128 * ab : 128 * ab + 128] = jnp.transpose(
                a4[:, 192 * ab : 192 * ab + 192].astype(F32)
            ).astype(BF16)

    stage("arrange", arrange)
    halo_wait(*halo_c)
    halo_wait(*halo_p)

    def stack_p(i):
        for j in range(8):
            pq[i, j] = stack_width(two_rows(pk[i, j], pk[i + 2, j]), 2)

    stage("stack_p", lambda: each(0, 4, stack_p))

    def forward4(i):
        for j in range(3):
            cols = [
                jnp.concatenate(
                    [pq[i + a, 2 * j + s + b] for a in range(3) for b in range(3)], axis=0
                )
                for s in range(2)
            ]
            act = jnp.dot(
                a4[:, :1728], jnp.concatenate(cols, axis=1), preferred_element_type=F32
            )
            _, slope = gelu_parts(act)
            for s in range(2):
                col = 2 * j + s
                both = two_rows(ck[i, col], ck[i + 2, col]).astype(F32)
                dq[i, col] = (both * slope[:, 128 * s : 128 * s + 128]).astype(BF16)

    stage("forward4", lambda: each(0, 2, forward4))

    def pair_rows():
        for j in range(6):
            one, two = dq[0, j], dq[1, j]
            even = lanes_iota(one.shape) % 2 == 0
            dv[0, j] = interleave_odd(one, two)
            dv[1, j] = jnp.where(even, two, one)
            dv[2, j] = interleave(one, two)

    stage("pair_rows", pair_rows)

    def back4(j):
        cols = [
            jnp.concatenate([dv[a, 2 * j + s + 2 - b] for a in range(3) for b in range(3)], axis=0)
            for s in range(2)
        ]
        y = jnp.dot(a5[...], jnp.concatenate(cols, axis=1), preferred_element_type=F32)
        for s in range(2):
            ys = y[:, 128 * s : 128 * s + 128]
            _, from_after = shifted(ys[:64], 2)
            from_before, _ = shifted(ys[128:], 2)
            back = (ys[64:128] + from_after + from_before) * 0.125
            even = lanes_iota(back.shape) % 2 == 0
            spread = [
                jnp.where(even, back, pltpu.roll(back, 1, 1)),
                jnp.where(even, pltpu.roll(back, 127, 1), back),
            ]
            for i in range(2):
                for di in range(2):
                    for dj in range(2):
                        row, col = 2 * i + di, 2 * (2 * j + s) + dj
                        delta = (spread[i] * slope3[row, col]).astype(BF16)
                        before, after = shifted(delta, 1)
                        dd3[row, col] = jnp.concatenate([after, delta, before], axis=0)
                        d3[1 + row, 1 + col] = delta

    stage("back4", lambda: each(0, 2, back4))
    d3[0] = jnp.zeros((10, 64, 128), BF16)
    d3[5] = jnp.zeros((10, 64, 128), BF16)
    d3[:, 0] = jnp.zeros((6, 64, 128), BF16)
    d3[:, 9] = jnp.zeros((6, 64, 128), BF16)

    f3acc[...] = jnp.zeros(f3acc.shape, F32)

    def weight3(i):
        left = jnp.concatenate(
            [
                jnp.concatenate([xb[i + a, j + b] for j in range(8)], axis=1)
                for a in range(3)
                for b in range(3)
            ],
            axis=0,
        )
        right = jnp.concatenate([dd3[i, j] for j in range(8)], axis=1)
        f3acc[...] += lax.dot_general(
            left, right, (((1,), (1,)), ((), ())), preferred_element_type=F32
        )

    stage("weight3", lambda: each(0, 4, weight3))

    def pack3():
        last = f3acc[:, 128:]
        flat = jnp.concatenate(
            [
                f3acc[:, :128],
                jnp.concatenate([last[:144], last[144:]], axis=1),
                jnp.zeros((80, 128), F32),
            ],
            axis=0,
        ).astype(BF16)
        for c in range(16):
            r3[c] = flat[32 * c : 32 * c + 32]

    stage("pack3", pack3)
    each(1, NH, lambda k: scatter_h(r3, q3, s3_s, s3_r, k).start())

    cells4 = [(i, j) for i in range(2) for j in range(4)]

    def weight4():
        even = lanes_iota((128, 128)) % 2 == 0
        left = jnp.concatenate(
            [
                jnp.where(even if i == 0 else ~even, dq[1 - i, 1 + j], jnp.zeros((), BF16))
                for i, j in cells4
            ],
            axis=1,
        )
        for g in range(5):
            taps = [ab for ab in (2 * g, 2 * g + 1) if ab < 9]
            right = jnp.concatenate(
                [
                    jnp.concatenate(
                        [pq[ab // 3 + 1 - i, j + ab % 3 + 1] for i, j in cells4], axis=1
                    )
                    for ab in taps
                ],
                axis=0,
            )
            piece = lax.dot_general(
                left, right, (((1,), (1,)), ((), ())), preferred_element_type=F32
            )
            if len(taps) == 1:
                piece = jnp.concatenate([piece, jnp.zeros((128, 64), F32)], axis=1)
            f4acc[:, 384 * g : 384 * g + piece.shape[1]] = piece

    stage("weight4", weight4)

    def pack4(s):
        rows = pl.ds(pl.multiple_of(8 * s, 8), 8)
        r4[lax.rem(s, 2), s // 2] = jnp.concatenate(
            [f4acc[rows, :896], f4acc[rows, 896:]], axis=0
        ).astype(BF16)

    stage("pack4", lambda: each(0, NH, pack4))
    core = lax.rem(h, 2)
    pair = h // 2

    def swap4():
        return pltpu.make_async_remote_copy(
            src_ref=r4.at[1 - core],
            dst_ref=q40,
            send_sem=s40_s,
            recv_sem=s40_r,
            device_id=(d, h + 1 - 2 * core),
            device_id_type=MESH,
        )

    def scatter4(k):
        other = lax.rem(pair + k, NH // 2)
        return pltpu.make_async_remote_copy(
            src_ref=r4b.at[other],
            dst_ref=q4.at[k],
            send_sem=s4_s.at[k],
            recv_sem=s4_r.at[k],
            device_id=partner(2 * other + core),
            device_id_type=MESH,
        )

    swap4().start()

    def gather_width(y, s):
        ys = y[:, 128 * s : 128 * s + 128]
        _, from_after = shifted(ys[:32], 1)
        from_before, _ = shifted(ys[64:], 1)
        return ys[32:64] + from_after + from_before

    def back_rim():
        for j in range(5):
            for a, row in ((0, 0), (2, 5)):
                source = 1 if row == 0 else 4
                cols = [
                    jnp.concatenate(
                        [
                            d3[source, 2 * j + s + 1 - b]
                            if 0 <= 2 * j + s + 1 - b <= 9
                            else jnp.zeros((64, 128), BF16)
                            for b in range(3)
                        ],
                        axis=0,
                    )
                    for s in range(2)
                ]
                y = jnp.dot(
                    a6[:, 192 * a : 192 * a + 192],
                    jnp.concatenate(cols, axis=1),
                    preferred_element_type=F32,
                )
                for s in range(2):
                    rim[row, 2 * j + s] = gather_width(y, s).astype(BF16)
        for b, col, source in ((0, 0, 1), (2, 9, 8)):
            weights = jnp.concatenate(
                [a6[:, 192 * a + 64 * b : 192 * a + 64 * b + 64] for a in range(3)], axis=1
            )
            for i in range(2):
                cols = [
                    jnp.concatenate([d3[2 * i + s + 2 - a, source] for a in range(3)], axis=0)
                    for s in range(2)
                ]
                y = jnp.dot(weights, jnp.concatenate(cols, axis=1), preferred_element_type=F32)
                for s in range(2):
                    rim[1 + 2 * i + s, col] = gather_width(y, s).astype(BF16)

    stage("back_rim", back_rim)
    halo_start(*halo_g)

    def wait_both(copy):
        copy.wait_send()
        copy.wait_recv()

    wait_both(swap4())

    def add4():
        for m in range(8):
            r4b[m] = (r4[core, m].astype(F32) + q40[m].astype(F32)).astype(BF16)

    stage("add4", add4)
    each(1, NH // 2, lambda k: scatter4(k).start())

    def back3(i):
        for j in range(4):
            cols = [
                jnp.concatenate(
                    [d3[i + 2 - a, 2 * j + s + 2 - b] for a in range(3) for b in range(3)], axis=0
                )
                for s in range(2)
            ]
            y = jnp.dot(a6[...], jnp.concatenate(cols, axis=1), preferred_element_type=F32)
            for s in range(2):
                gown[i, 2 * j + s] = gather_width(y, s)

    stage("back3a", lambda: each(0, 2, back3))

    each(1, NH, lambda k: wait_both(scatter_h(r3, q3, s3_s, s3_r, k)))

    def sum3():
        total3 = r3[h].astype(F32)
        for k in range(1, NH):
            total3 = total3 + q3[k].astype(F32)
        t3[...] = total3

    stage("sum3", sum3)
    each(1, ND, lambda k: share_d(t3, q3b, b3_s, b3_r, k).start())
    stage("back3b", lambda: each(2, 4, back3))

    halo_wait(*halo_g)

    def finish_gv():
        for i in range(4):
            done = []
            for j in range(8):
                total = gown[i, j]
                if i in (0, 3):
                    total = total + near[0 if i == 0 else 5, 1 + j].astype(F32)
                if j in (0, 7):
                    total = total + near[1 + i, 0 if j == 0 else 9].astype(F32)
                if i in (0, 3) and j in (0, 7):
                    total = total + near[0 if i == 0 else 5, 0 if j == 0 else 9].astype(F32)
                done.append(total)
            gv_out[:, i] = jnp.transpose(jnp.stack(done, axis=0), (1, 0, 2)).astype(BF16)

    stage("finish_gv", finish_gv)

    each(1, NH // 2, lambda k: wait_both(scatter4(k)))

    def sum4():
        total4 = r4b[pair].astype(F32)
        for k in range(1, NH // 2):
            total4 = total4 + q4[k].astype(F32)
        t4[...] = total4.astype(BF16)

    stage("sum4", sum4)
    each(1, ND, lambda k: share_d(t4, q4b, b4_s, b4_r, k).start())

    each(1, ND, lambda k: wait_both(share_d(t3, q3b, b3_s, b3_r, k)))
    whole3 = t3[...]
    for k in range(1, ND):
        whole3 = whole3 + q3b[k]
    v3[h] = (whole3 * (1.0 / math.sqrt(32 * 128 * 128))).astype(BF16)
    each(1, NH, lambda k: gather_send(v3.at[h], v3, c3_s, c3_r, k).start())

    each(1, ND, lambda k: wait_both(share_d(t4, q4b, b4_s, b4_r, k)))
    whole4 = t4[...].astype(F32)
    for k in range(1, ND):
        whole4 = whole4 + q4b[k].astype(F32)
    whole4 = whole4 * (1.0 / math.sqrt(16 * 64 * 64))
    for t in range(27):
        rows, lane = 8 * (t // 14), 64 * (t % 14)
        g4_out[t] = whole4[rows : rows + 8, lane : lane + 64]

    def wait_c3(k):
        gather_send(v3.at[h], v3, c3_s, c3_r, k).wait_send()
        gather_recv(v3.at[h], v3, c3_s, c3_r, k).wait_recv()

    each(1, NH, wait_c3)
    flat3 = jnp.concatenate([v3[c].astype(F32) for c in range(14)], axis=0)
    last3 = jnp.concatenate([flat3[288:432, :64], flat3[288:432, 64:]], axis=0)
    for ab in range(9):
        rows = slice(32 * ab, 32 * ab + 32)
        g3_out[3 * ab] = flat3[rows, :64]
        g3_out[3 * ab + 1] = flat3[rows, 64:]
        g3_out[3 * ab + 2] = last3[rows]


def shards(volume, filters_three, filters_four, cotangent):
    vmem = pl.BlockSpec(memory_space=pltpu.VMEM)
    hbm = pl.BlockSpec(memory_space=pl.ANY)
    dma = pltpu.SemaphoreType.DMA
    gv, g3, g4 = pl.pallas_call(
        kernel,
        out_shape=(
            pltpu.VMEM((32, 4, 8, 128), BF16),
            pltpu.VMEM((27, 32, 64), F32),
            pltpu.VMEM((27, 8, 64), F32),
        ),
        in_specs=[hbm] * 4,
        out_specs=(vmem,) * 3,
        scratch_shapes=[
            pltpu.VMEM((32, 4, 8, 128), BF16),
            pltpu.VMEM((27, 32, 64), BF16),
            pltpu.VMEM((27, 8, 64), BF16),
            pltpu.VMEM((2, 4, 64, 128), BF16),
            pltpu.VMEM((16, 896), BF16),
            pltpu.VMEM((128, 1152), BF16),
            pltpu.VMEM((96, 576), BF16),
            pltpu.VMEM((6, 10, 32, 128), BF16),
            pltpu.VMEM((6, 10, 96, 128), BF16),
            pltpu.VMEM((4, 8, 64, 128), F32),
            pltpu.VMEM((4, 6, 64, 128), BF16),
            pltpu.VMEM((6, 8, 32, 128), BF16),
            pltpu.VMEM((4, 8, 192, 128), BF16),
            pltpu.VMEM((2, 6, 128, 128), BF16),
            pltpu.VMEM((3, 6, 128, 128), BF16),
            pltpu.VMEM((6, 10, 64, 128), BF16),
            pltpu.VMEM((4, 8, 192, 128), BF16),
            pltpu.VMEM((6, 10, 32, 128), BF16),
            pltpu.VMEM((6, 10, 32, 128), BF16),
            pltpu.VMEM((4, 8, 32, 128), F32),
            pltpu.VMEM((16, 16, 896), BF16),
            pltpu.VMEM((128, 1792), BF16),
            pltpu.VMEM((192, 1152), BF16),
            pltpu.VMEM((128, 1792), F32),
            pltpu.VMEM((2, 8, 16, 896), BF16),
            pltpu.VMEM((8, 16, 896), BF16),
            pltpu.VMEM((8, 16, 896), BF16),
            pltpu.VMEM((8, 16, 896), BF16),
            pltpu.VMEM((16, 896), BF16),
            pltpu.VMEM((8, 16, 896), BF16),
            pltpu.VMEM((288, 192), F32),
            pltpu.VMEM((16, 32, 128), BF16),
            pltpu.VMEM((16, 32, 128), BF16),
            pltpu.VMEM((32, 128), F32),
            pltpu.VMEM((8, 32, 128), F32),
            pltpu.VMEM((16, 32, 128), BF16),
            dma((4,)),
            dma((4, 8)),
            dma((4, 8)),
            dma,
            dma,
            dma((16,)),
            dma((16,)),
            dma((16,)),
            dma((16,)),
            dma((8,)),
            dma((8,)),
            dma((16,)),
            dma((16,)),
            dma((8,)),
            dma((8,)),
            dma((16,)),
            dma((16,)),
        ],
        compiler_params=pltpu.CompilerParams(
            collective_id=0, has_side_effects=True, vmem_limit_bytes=58000 * 1024
        ),
    )(
        volume,
        jnp.transpose(filters_three, (0, 2, 1)),
        filters_four,
        jnp.transpose(cotangent, (1, 2, 3, 0)),
    )
    return (gv, jnp.transpose(g3, (0, 2, 1)), g4)


def solution(mesh):
    in_specs = (
        P(None, "depth", "height", None),
        P(),
        P(None, "height", None),
        P(None, "depth", "height", None),
    )
    out_specs = (P(None, "depth", "height", None), P(), P(None, "height", None))
    return jax.shard_map(shards, mesh=mesh, in_specs=in_specs, out_specs=out_specs, check_vma=False)
```

```python
import functools
import math

import jax
import jax.numpy as jnp
from jax import lax
from jax.experimental import pallas as pl
from jax.experimental.pallas import tpu as pltpu
from jax.sharding import PartitionSpec as P

TANH_SCALE = 0.7978845608028654
CUBIC_TERM = 0.044715
MESH = pl.DeviceIdType.MESH
F32 = jnp.float32
BF16 = jnp.bfloat16

ND = 8
NH = 16
DIRECTIONS = [(dd, hh) for dd in (-1, 0, 1) for hh in (-1, 0, 1) if (dd, hh) != (0, 0)]


def gelu_parts(v):
    u = v * v
    inner = jnp.tanh(v * (TANH_SCALE + TANH_SCALE * CUBIC_TERM * u))
    half = 0.5 + 0.5 * inner
    value = v * half
    slope = half + value * (1.0 - inner) * (TANH_SCALE + 3.0 * TANH_SCALE * CUBIC_TERM * u)
    return value, slope


def stage(name, body):
    body()


def lanes_iota(shape):
    return lax.broadcasted_iota(jnp.int32, shape, len(shape) - 1)


def shifted(v, step):
    lane = lanes_iota(v.shape)
    zero = jnp.zeros((), v.dtype)
    before = jnp.where(lane < step, zero, pltpu.roll(v, step, 1))
    after = jnp.where(lane >= 128 - step, zero, pltpu.roll(v, 128 - step, 1))
    return before, after


def stack_width(row, step):
    before, after = shifted(row, step)
    return jnp.concatenate([before, row, after], axis=0)


def part(at, cells, width, far):
    if at == 0:
        return pl.ds(width, cells)
    if at < 0:
        return pl.ds(cells + width, width) if far else pl.ds(width, width)
    return pl.ds(0, width) if far else pl.ds(cells, width)


def interleave(even_row, odd_row):
    even = lanes_iota(even_row.shape) % 2 == 0
    return jnp.where(even, even_row, pltpu.roll(odd_row, 1, 1))


def interleave_odd(even_row, odd_row):
    even = lanes_iota(even_row.shape) % 2 == 0
    return jnp.where(even, pltpu.roll(even_row, 127, 1), odd_row)


def two_rows(first, second):
    return jnp.concatenate([interleave(first, second), interleave_odd(first, second)], axis=0)


def kernel(
    x_hbm, f3_hbm, f4_hbm, cot_hbm,
    gv_out, g3_out, g4_out,
    x_in, f3, f4_in, cot, f4, a3, a6,
    xb, xx, slope3, ck, pk, pq, dq, dv, d3, dd3, rim, near, gown, bank, a4, a5,
    f4acc, r4, q40, r4b, q4, t4, q4b,
    f3acc, r3, q3, t3, q3b, v3,
    in_sem, halo_s, halo_r, s40_s, s40_r, ag_s, ag_r, s4_s, s4_r, b4_s, b4_r, s3_s, s3_r, b3_s, b3_r, c3_s, c3_r,
):
    d = lax.axis_index("depth")
    h = lax.axis_index("height")

    def around(dd, hh):
        return (lax.rem(d + dd + ND, ND), lax.rem(h + hh + NH, NH))

    def partner(other):
        flip = lax.rem(lax.rem(h, 4) // 2 + lax.rem(other, 4) // 2, 2)
        return (d + flip * (1 - 2 * lax.rem(d, 2)), other)

    def each(low, high, body):
        def step(k, carry):
            body(k)
            return carry

        lax.fori_loop(low, high, step, 0)

    barrier = pltpu.get_barrier_semaphore()

    def greet(device):
        pl.semaphore_signal(barrier, inc=1, device_id=device, device_id_type=MESH)

    for dd, hh in DIRECTIONS:
        greet(around(dd, hh))
    for k in range(1, NH):
        greet(partner(lax.rem(h + k, NH)))
    for k in range(2, ND - 1):
        greet(around(k, 0))

    fetches = [
        pltpu.make_async_copy(src, dst, in_sem.at[n])
        for n, (src, dst) in enumerate(
            [(x_hbm, x_in), (f4_hbm, f4_in), (f3_hbm, f3), (cot_hbm, cot)]
        )
    ]
    for fetch in fetches:
        fetch.start()

    def rows_x():
        for i in range(4):
            block = jnp.transpose(x_in[:, i].astype(F32), (1, 0, 2)).astype(BF16)
            for j in range(8):
                xb[1 + i, 1 + j] = block[j]

    fetches[0].wait()
    stage("rows_x", rows_x)

    def rows_f4():
        taps = [f4_in[t].astype(F32) for t in range(27)] + [jnp.zeros((8, 64), F32)]
        tiles = [jnp.concatenate([taps[2 * m], taps[2 * m + 1]], axis=1) for m in range(14)]
        f4[...] = jnp.concatenate(
            [jnp.concatenate(tiles[:7], axis=1), jnp.concatenate(tiles[7:], axis=1)], axis=0
        ).astype(BF16)

    fetches[1].wait()
    stage("rows_f4", rows_f4)
    pl.semaphore_wait(barrier, 8 + NH - 1 + ND - 3)

    def halo_copy(which, n, buf, cells_d, cells_h, width, beyond=None):
        dd, hh = DIRECTIONS[n]
        if beyond is None:
            src = buf.at[part(dd, cells_d, width, False), part(hh, cells_h, width, False)]
        else:
            src = beyond.at[part(-dd, cells_d, width, True), part(-hh, cells_h, width, True)]
        return pltpu.make_async_remote_copy(
            src_ref=src,
            dst_ref=buf.at[part(dd, cells_d, width, True), part(hh, cells_h, width, True)],
            send_sem=halo_s.at[which, n],
            recv_sem=halo_r.at[which, n],
            device_id=around(dd, hh),
            device_id_type=MESH,
        )

    def halo_start(*which):
        for n in range(8):
            halo_copy(which[0], n, *which[1:]).start()

    def halo_wait(*which):
        for n in range(8):
            halo_copy(which[0], n, *which[1:]).wait_send()
        for n in range(8):
            halo_copy(which[0], n, *which[1:]).wait_recv()
        _, buf, cells_d, cells_h, width = which[:5]
        channels = buf.shape[2]
        across = (width, cells_h + 2 * width, channels, 128)
        along = (cells_d + 2 * width, width, channels, 128)

        @pl.when(d == 0)
        def _():
            buf[0:width] = jnp.zeros(across, BF16)

        @pl.when(d == ND - 1)
        def _():
            buf[cells_d + width : cells_d + 2 * width] = jnp.zeros(across, BF16)

        @pl.when(h == 0)
        def _():
            buf[:, 0:width] = jnp.zeros(along, BF16)

        @pl.when(h == NH - 1)
        def _():
            buf[:, cells_h + width : cells_h + 2 * width] = jnp.zeros(along, BF16)

    def scatter_h(src, dst, send, recv, k):
        other = lax.rem(h + k, NH)
        return pltpu.make_async_remote_copy(
            src_ref=src.at[other],
            dst_ref=dst.at[k],
            send_sem=send.at[k],
            recv_sem=recv.at[k],
            device_id=partner(other),
            device_id_type=MESH,
        )

    def share_d(src, dst, send, recv, k):
        return pltpu.make_async_remote_copy(
            src_ref=src,
            dst_ref=dst.at[k],
            send_sem=send.at[k],
            recv_sem=recv.at[k],
            device_id=around(k, 0),
            device_id_type=MESH,
        )

    def gather_send(src, dst, send, recv, k):
        return pltpu.make_async_remote_copy(
            src_ref=src,
            dst_ref=dst.at[h],
            send_sem=send.at[k],
            recv_sem=recv.at[k],
            device_id=partner(lax.rem(h + k, NH)),
            device_id_type=MESH,
        )

    def gather_recv(src, dst, send, recv, k):
        return pltpu.make_async_remote_copy(
            src_ref=src,
            dst_ref=dst.at[lax.rem(h - k + NH, NH)],
            send_sem=send.at[k],
            recv_sem=recv.at[k],
            device_id=partner(lax.rem(h + k, NH)),
            device_id_type=MESH,
        )

    halo_x = (0, xb, 4, 8, 1)
    halo_p = (1, pk, 2, 4, 2)
    halo_c = (2, ck, 2, 4, 1)
    halo_g = (3, near, 4, 8, 1, rim)
    halo_start(*halo_x)
    each(1, NH, lambda k: gather_send(f4, bank, ag_s, ag_r, k).start())
    bank[h] = f4[...]

    def dilate():
        at = 2 * lax.broadcasted_iota(jnp.int32, (64, 128), 0)
        to_even = (lanes_iota((64, 128)) == at).astype(F32).astype(BF16)
        for i in range(2):
            for j in range(4):
                wide = lax.dot_general(
                    cot[i, j], to_even, (((0,), (0,)), ((), ())), preferred_element_type=F32
                )
                ck[1 + i, 1 + j] = interleave(wide[:64], wide[64:]).astype(BF16)

    def rows_f3():
        flat = f3[...].astype(F32).reshape(864, 64)
        none = jnp.zeros((288, 64), F32)
        both = jnp.concatenate(
            [jnp.concatenate([flat, none], axis=0), jnp.concatenate([none, flat], axis=0)], axis=1
        )
        a3[...] = jnp.transpose(both).astype(BF16)
        a6[...] = jnp.concatenate(
            [flat[96 * ab : 96 * ab + 96] for ab in range(9)], axis=1
        ).astype(BF16)

    def stack_row(i, j):
        xx[i, j] = stack_width(xb[i, j], 1)

    def stack_x(i):
        for j in range(8):
            stack_row(1 + i, 1 + j)

    fetches[3].wait()
    stage("dilate", dilate)
    halo_start(*halo_c)
    fetches[2].wait()
    stage("rows_f3", rows_f3)
    stage("stack_x", lambda: each(0, 4, stack_x))
    halo_wait(*halo_x)

    def stack_rim():
        for j in range(10):
            stack_row(0, j)
            stack_row(5, j)
        for i in range(4):
            stack_row(1 + i, 0)
            stack_row(1 + i, 9)

    stage("stack_rim", stack_rim)

    def forward3(i):
        for j in range(4):
            cols = [
                jnp.concatenate(
                    [xx[2 * i + a, 2 * j + s + b] for a in range(4) for b in range(3)], axis=0
                )
                for s in range(2)
            ]
            act = jnp.dot(a3[...], jnp.concatenate(cols, axis=1), preferred_element_type=F32)
            value, slope = gelu_parts(act)
            for di in range(2):
                for s in range(2):
                    slope3[2 * i + di, 2 * j + s] = slope[
                        64 * di : 64 * di + 64, 128 * s : 128 * s + 128
                    ]
            total = value[:64] + value[64:]
            total = total[:, :128] + total[:, 128:]
            total = (total + pltpu.roll(total, 127, 1)) * 0.125
            pk[2 + i, 2 + j] = interleave(total[:32], total[32:]).astype(BF16)

    stage("forward3", lambda: each(0, 2, forward3))
    halo_start(*halo_p)

    def wait_gather(k):
        gather_send(f4, bank, ag_s, ag_r, k).wait_send()
        gather_recv(f4, bank, ag_s, ag_r, k).wait_recv()

    each(1, NH, wait_gather)

    def arrange():
        wide = [bank[s].astype(F32) for s in range(NH)]
        low = jnp.concatenate([w[:8] for w in wide], axis=0)
        high = jnp.concatenate([w[8:] for w in wide], axis=0)
        a4[...] = jnp.concatenate([low, high], axis=1).astype(BF16)
        for ab in range(9):
            a5[:, 128 * ab : 128 * ab + 128] = jnp.transpose(
                a4[:, 192 * ab : 192 * ab + 192].astype(F32)
            ).astype(BF16)

    stage("arrange", arrange)
    halo_wait(*halo_c)
    halo_wait(*halo_p)

    def stack_p(i):
        for j in range(8):
            pq[i, j] = stack_width(two_rows(pk[i, j], pk[i + 2, j]), 2)

    stage("stack_p", lambda: each(0, 4, stack_p))

    def forward4(i):
        for j in range(3):
            cols = [
                jnp.concatenate(
                    [pq[i + a, 2 * j + s + b] for a in range(3) for b in range(3)], axis=0
                )
                for s in range(2)
            ]
            act = jnp.dot(
                a4[:, :1728], jnp.concatenate(cols, axis=1), preferred_element_type=F32
            )
            _, slope = gelu_parts(act)
            for s in range(2):
                col = 2 * j + s
                both = two_rows(ck[i, col], ck[i + 2, col]).astype(F32)
                dq[i, col] = (both * slope[:, 128 * s : 128 * s + 128]).astype(BF16)

    stage("forward4", lambda: each(0, 2, forward4))

    def pair_rows():
        for j in range(6):
            one, two = dq[0, j], dq[1, j]
            even = lanes_iota(one.shape) % 2 == 0
            dv[0, j] = interleave_odd(one, two)
            dv[1, j] = jnp.where(even, two, one)
            dv[2, j] = interleave(one, two)

    stage("pair_rows", pair_rows)

    def back4(j):
        cols = [
            jnp.concatenate([dv[a, 2 * j + s + 2 - b] for a in range(3) for b in range(3)], axis=0)
            for s in range(2)
        ]
        y = jnp.dot(a5[...], jnp.concatenate(cols, axis=1), preferred_element_type=F32)
        for s in range(2):
            ys = y[:, 128 * s : 128 * s + 128]
            _, from_after = shifted(ys[:64], 2)
            from_before, _ = shifted(ys[128:], 2)
            back = (ys[64:128] + from_after + from_before) * 0.125
            even = lanes_iota(back.shape) % 2 == 0
            spread = [
                jnp.where(even, back, pltpu.roll(back, 1, 1)),
                jnp.where(even, pltpu.roll(back, 127, 1), back),
            ]
            for i in range(2):
                for di in range(2):
                    for dj in range(2):
                        row, col = 2 * i + di, 2 * (2 * j + s) + dj
                        delta = (spread[i] * slope3[row, col]).astype(BF16)
                        before, after = shifted(delta, 1)
                        dd3[row, col] = jnp.concatenate([after, delta, before], axis=0)
                        d3[1 + row, 1 + col] = delta

    stage("back4", lambda: each(0, 2, back4))
    d3[0] = jnp.zeros((10, 64, 128), BF16)
    d3[5] = jnp.zeros((10, 64, 128), BF16)
    d3[:, 0] = jnp.zeros((6, 64, 128), BF16)
    d3[:, 9] = jnp.zeros((6, 64, 128), BF16)

    f3acc[...] = jnp.zeros(f3acc.shape, F32)

    def weight3(i):
        left = jnp.concatenate(
            [
                jnp.concatenate([xb[i + a, j + b] for j in range(8)], axis=1)
                for a in range(3)
                for b in range(3)
            ],
            axis=0,
        )
        right = jnp.concatenate([dd3[i, j] for j in range(8)], axis=1)
        f3acc[...] += lax.dot_general(
            left, right, (((1,), (1,)), ((), ())), preferred_element_type=F32
        )

    stage("weight3", lambda: each(0, 4, weight3))

    def pack3():
        last = f3acc[:, 128:]
        flat = jnp.concatenate(
            [
                f3acc[:, :128],
                jnp.concatenate([last[:144], last[144:]], axis=1),
                jnp.zeros((80, 128), F32),
            ],
            axis=0,
        ).astype(BF16)
        for c in range(16):
            r3[c] = flat[32 * c : 32 * c + 32]

    stage("pack3", pack3)
    for k in range(1, NH):
        scatter_h(r3, q3, s3_s, s3_r, k).start()

    cells4 = [(i, j) for i in range(2) for j in range(4)]

    def weight4():
        even = lanes_iota((128, 128)) % 2 == 0
        left = jnp.concatenate(
            [
                jnp.where(even if i == 0 else ~even, dq[1 - i, 1 + j], jnp.zeros((), BF16))
                for i, j in cells4
            ],
            axis=1,
        )
        for g in range(5):
            taps = [ab for ab in (2 * g, 2 * g + 1) if ab < 9]
            right = jnp.concatenate(
                [
                    jnp.concatenate(
                        [pq[ab // 3 + 1 - i, j + ab % 3 + 1] for i, j in cells4], axis=1
                    )
                    for ab in taps
                ],
                axis=0,
            )
            piece = lax.dot_general(
                left, right, (((1,), (1,)), ((), ())), preferred_element_type=F32
            )
            if len(taps) == 1:
                piece = jnp.concatenate([piece, jnp.zeros((128, 64), F32)], axis=1)
            f4acc[:, 384 * g : 384 * g + piece.shape[1]] = piece

    stage("weight4", weight4)

    def pack4(s):
        rows = pl.ds(pl.multiple_of(8 * s, 8), 8)
        r4[lax.rem(s, 2), s // 2] = jnp.concatenate(
            [f4acc[rows, :896], f4acc[rows, 896:]], axis=0
        ).astype(BF16)

    stage("pack4", lambda: each(0, NH, pack4))
    core = lax.rem(h, 2)
    pair = h // 2

    def swap4():
        return pltpu.make_async_remote_copy(
            src_ref=r4.at[1 - core],
            dst_ref=q40,
            send_sem=s40_s,
            recv_sem=s40_r,
            device_id=(d, h + 1 - 2 * core),
            device_id_type=MESH,
        )

    def scatter4(k):
        other = lax.rem(pair + k, NH // 2)
        return pltpu.make_async_remote_copy(
            src_ref=r4b.at[other],
            dst_ref=q4.at[k],
            send_sem=s4_s.at[k],
            recv_sem=s4_r.at[k],
            device_id=partner(2 * other + core),
            device_id_type=MESH,
        )

    swap4().start()

    def gather_width(y, s):
        ys = y[:, 128 * s : 128 * s + 128]
        _, from_after = shifted(ys[:32], 1)
        from_before, _ = shifted(ys[64:], 1)
        return ys[32:64] + from_after + from_before

    def back_rim():
        for j in range(5):
            for a, row in ((0, 0), (2, 5)):
                source = 1 if row == 0 else 4
                cols = [
                    jnp.concatenate(
                        [
                            d3[source, 2 * j + s + 1 - b]
                            if 0 <= 2 * j + s + 1 - b <= 9
                            else jnp.zeros((64, 128), BF16)
                            for b in range(3)
                        ],
                        axis=0,
                    )
                    for s in range(2)
                ]
                y = jnp.dot(
                    a6[:, 192 * a : 192 * a + 192],
                    jnp.concatenate(cols, axis=1),
                    preferred_element_type=F32,
                )
                for s in range(2):
                    rim[row, 2 * j + s] = gather_width(y, s).astype(BF16)
        for b, col, source in ((0, 0, 1), (2, 9, 8)):
            weights = jnp.concatenate(
                [a6[:, 192 * a + 64 * b : 192 * a + 64 * b + 64] for a in range(3)], axis=1
            )
            for i in range(2):
                cols = [
                    jnp.concatenate([d3[2 * i + s + 2 - a, source] for a in range(3)], axis=0)
                    for s in range(2)
                ]
                y = jnp.dot(weights, jnp.concatenate(cols, axis=1), preferred_element_type=F32)
                for s in range(2):
                    rim[1 + 2 * i + s, col] = gather_width(y, s).astype(BF16)

    stage("back_rim", back_rim)
    halo_start(*halo_g)

    def wait_both(copy):
        copy.wait_send()
        copy.wait_recv()

    wait_both(swap4())

    def add4():
        for m in range(8):
            r4b[m] = (r4[core, m].astype(F32) + q40[m].astype(F32)).astype(BF16)

    stage("add4", add4)
    each(1, NH // 2, lambda k: scatter4(k).start())

    def back3(i):
        for j in range(4):
            cols = [
                jnp.concatenate(
                    [d3[i + 2 - a, 2 * j + s + 2 - b] for a in range(3) for b in range(3)], axis=0
                )
                for s in range(2)
            ]
            y = jnp.dot(a6[...], jnp.concatenate(cols, axis=1), preferred_element_type=F32)
            for s in range(2):
                gown[i, 2 * j + s] = gather_width(y, s)

    stage("back3a", lambda: each(0, 2, back3))

    for k in range(1, NH):
        wait_both(scatter_h(r3, q3, s3_s, s3_r, k))

    def sum3():
        total3 = r3[h].astype(F32)
        for k in range(1, NH):
            total3 = total3 + q3[k].astype(F32)
        t3[...] = total3.astype(BF16)

    stage("sum3", sum3)
    for k in range(1, ND):
        share_d(t3, q3b, b3_s, b3_r, k).start()
    stage("back3b", lambda: each(2, 4, back3))

    halo_wait(*halo_g)

    def finish_gv():
        for i in range(4):
            done = []
            for j in range(8):
                total = gown[i, j]
                if i in (0, 3):
                    total = total + near[0 if i == 0 else 5, 1 + j].astype(F32)
                if j in (0, 7):
                    total = total + near[1 + i, 0 if j == 0 else 9].astype(F32)
                if i in (0, 3) and j in (0, 7):
                    total = total + near[0 if i == 0 else 5, 0 if j == 0 else 9].astype(F32)
                done.append(total)
            gv_out[:, i] = jnp.transpose(jnp.stack(done, axis=0), (1, 0, 2)).astype(BF16)

    stage("finish_gv", finish_gv)

    each(1, NH // 2, lambda k: wait_both(scatter4(k)))

    def sum4():
        total4 = r4b[pair].astype(F32)
        for k in range(1, NH // 2):
            total4 = total4 + q4[k].astype(F32)
        t4[...] = total4.astype(BF16)

    stage("sum4", sum4)
    each(1, ND, lambda k: share_d(t4, q4b, b4_s, b4_r, k).start())

    for k in range(1, ND):
        wait_both(share_d(t3, q3b, b3_s, b3_r, k))
    whole3 = t3[...].astype(F32)
    for k in range(1, ND):
        whole3 = whole3 + q3b[k].astype(F32)
    v3[h] = (whole3 * (1.0 / math.sqrt(32 * 128 * 128))).astype(BF16)
    for k in range(1, NH):
        gather_send(v3.at[h], v3, c3_s, c3_r, k).start()

    each(1, ND, lambda k: wait_both(share_d(t4, q4b, b4_s, b4_r, k)))
    whole4 = t4[...].astype(F32)
    for k in range(1, ND):
        whole4 = whole4 + q4b[k].astype(F32)
    whole4 = whole4 * (1.0 / math.sqrt(16 * 64 * 64))
    for t in range(27):
        rows, lane = 8 * (t // 14), 64 * (t % 14)
        g4_out[t] = whole4[rows : rows + 8, lane : lane + 64]

    def wait_c3(k):
        gather_send(v3.at[h], v3, c3_s, c3_r, k).wait_send()
        gather_recv(v3.at[h], v3, c3_s, c3_r, k).wait_recv()

    for k in range(1, NH):
        wait_c3(k)
    flat3 = jnp.concatenate([v3[c].astype(F32) for c in range(14)], axis=0)
    last3 = jnp.concatenate([flat3[288:432, :64], flat3[288:432, 64:]], axis=0)
    for ab in range(9):
        rows = slice(32 * ab, 32 * ab + 32)
        g3_out[3 * ab] = flat3[rows, :64]
        g3_out[3 * ab + 1] = flat3[rows, 64:]
        g3_out[3 * ab + 2] = last3[rows]


def writer(gv, g3, g4, gv_hbm, g3_hbm, g4_hbm, sems):
    copies = [
        pltpu.make_async_copy(src, dst, sems.at[n])
        for n, (src, dst) in enumerate([(gv, gv_hbm), (g3, g3_hbm), (g4, g4_hbm)])
    ]
    for copy in copies:
        copy.start()
    for copy in copies:
        copy.wait()


def shards(volume, filters_three, filters_four, cotangent):
    vmem = pl.BlockSpec(memory_space=pltpu.VMEM)
    hbm = pl.BlockSpec(memory_space=pl.ANY)
    dma = pltpu.SemaphoreType.DMA
    gv, g3, g4 = pl.pallas_call(
        kernel,
        out_shape=(
            pltpu.VMEM((32, 4, 8, 128), BF16),
            pltpu.VMEM((27, 32, 64), F32),
            pltpu.VMEM((27, 8, 64), F32),
        ),
        in_specs=[hbm] * 4,
        out_specs=(vmem,) * 3,
        scratch_shapes=[
            pltpu.VMEM((32, 4, 8, 128), BF16),
            pltpu.VMEM((27, 32, 64), BF16),
            pltpu.VMEM((27, 8, 64), BF16),
            pltpu.VMEM((2, 4, 64, 128), BF16),
            pltpu.VMEM((16, 896), BF16),
            pltpu.VMEM((128, 1152), BF16),
            pltpu.VMEM((96, 576), BF16),
            pltpu.VMEM((6, 10, 32, 128), BF16),
            pltpu.VMEM((6, 10, 96, 128), BF16),
            pltpu.VMEM((4, 8, 64, 128), F32),
            pltpu.VMEM((4, 6, 64, 128), BF16),
            pltpu.VMEM((6, 8, 32, 128), BF16),
            pltpu.VMEM((4, 8, 192, 128), BF16),
            pltpu.VMEM((2, 6, 128, 128), BF16),
            pltpu.VMEM((3, 6, 128, 128), BF16),
            pltpu.VMEM((6, 10, 64, 128), BF16),
            pltpu.VMEM((4, 8, 192, 128), BF16),
            pltpu.VMEM((6, 10, 32, 128), BF16),
            pltpu.VMEM((6, 10, 32, 128), BF16),
            pltpu.VMEM((4, 8, 32, 128), F32),
            pltpu.VMEM((16, 16, 896), BF16),
            pltpu.VMEM((128, 1792), BF16),
            pltpu.VMEM((192, 1152), BF16),
            pltpu.VMEM((128, 1792), F32),
            pltpu.VMEM((2, 8, 16, 896), BF16),
            pltpu.VMEM((8, 16, 896), BF16),
            pltpu.VMEM((8, 16, 896), BF16),
            pltpu.VMEM((8, 16, 896), BF16),
            pltpu.VMEM((16, 896), BF16),
            pltpu.VMEM((8, 16, 896), BF16),
            pltpu.VMEM((288, 192), F32),
            pltpu.VMEM((16, 32, 128), BF16),
            pltpu.VMEM((16, 32, 128), BF16),
            pltpu.VMEM((32, 128), BF16),
            pltpu.VMEM((8, 32, 128), BF16),
            pltpu.VMEM((16, 32, 128), BF16),
            dma((4,)),
            dma((4, 8)),
            dma((4, 8)),
            dma,
            dma,
            dma((16,)),
            dma((16,)),
            dma((16,)),
            dma((16,)),
            dma((8,)),
            dma((8,)),
            dma((16,)),
            dma((16,)),
            dma((8,)),
            dma((8,)),
            dma((16,)),
            dma((16,)),
        ],
        compiler_params=pltpu.CompilerParams(
            collective_id=0, has_side_effects=True, vmem_limit_bytes=58000 * 1024
        ),
    )(
        volume,
        jnp.transpose(filters_three, (0, 2, 1)),
        filters_four,
        jnp.transpose(cotangent, (1, 2, 3, 0)),
    )
    gv, g3, g4 = pl.pallas_call(
        writer,
        out_shape=(
            pltpu.HBM((32, 4, 8, 128), BF16),
            pltpu.HBM((27, 32, 64), F32),
            pltpu.HBM((27, 8, 64), F32),
        ),
        in_specs=[hbm] * 3,
        out_specs=(hbm,) * 3,
        scratch_shapes=[dma((3,))],
        compiler_params=pltpu.CompilerParams(vmem_limit_bytes=1024 * 1024),
    )(gv, g3, g4)
    return (gv, jnp.transpose(g3, (0, 2, 1)), g4)


def solution(mesh):
    in_specs = (
        P(None, "depth", "height", None),
        P(),
        P(None, "height", None),
        P(None, "depth", "height", None),
    )
    out_specs = (P(None, "depth", "height", None), P(), P(None, "height", None))
    return jax.shard_map(shards, mesh=mesh, in_specs=in_specs, out_specs=out_specs, check_vma=False)
```

```python
import functools
import math

import jax
import jax.numpy as jnp
from jax import lax
from jax.experimental import pallas as pl
from jax.experimental.pallas import tpu as pltpu
from jax.sharding import PartitionSpec as P

TANH_SCALE = 0.7978845608028654
CUBIC_TERM = 0.044715
MESH = pl.DeviceIdType.MESH
F32 = jnp.float32
BF16 = jnp.bfloat16

ND = 8
NH = 16
DIRECTIONS = [(dd, hh) for dd in (-1, 0, 1) for hh in (-1, 0, 1) if (dd, hh) != (0, 0)]


def gelu_parts(v):
    u = v * v
    inner = jnp.tanh(v * (TANH_SCALE + TANH_SCALE * CUBIC_TERM * u))
    half = 0.5 + 0.5 * inner
    value = v * half
    slope = half + value * (1.0 - inner) * (TANH_SCALE + 3.0 * TANH_SCALE * CUBIC_TERM * u)
    return value, slope


def stage(name, body):
    body()


def lanes_iota(shape):
    return lax.broadcasted_iota(jnp.int32, shape, len(shape) - 1)


def shifted(v, step):
    lane = lanes_iota(v.shape)
    zero = jnp.zeros((), v.dtype)
    before = jnp.where(lane < step, zero, pltpu.roll(v, step, 1))
    after = jnp.where(lane >= 128 - step, zero, pltpu.roll(v, 128 - step, 1))
    return before, after


def stack_width(row, step):
    before, after = shifted(row, step)
    return jnp.concatenate([before, row, after], axis=0)


def part(at, cells, width, far):
    if at == 0:
        return pl.ds(width, cells)
    if at < 0:
        return pl.ds(cells + width, width) if far else pl.ds(width, width)
    return pl.ds(0, width) if far else pl.ds(cells, width)


def interleave(even_row, odd_row):
    even = lanes_iota(even_row.shape) % 2 == 0
    return jnp.where(even, even_row, pltpu.roll(odd_row, 1, 1))


def interleave_odd(even_row, odd_row):
    even = lanes_iota(even_row.shape) % 2 == 0
    return jnp.where(even, pltpu.roll(even_row, 127, 1), odd_row)


def two_rows(first, second):
    return jnp.concatenate([interleave(first, second), interleave_odd(first, second)], axis=0)


def kernel(
    x_hbm, f3_hbm, f4_hbm, cot_hbm,
    gv_out, g3_out, g4_out,
    x_in, f3, f4_in, cot, f4, a3, a6,
    xb, xx, slope3, ck, pk, pq, dq, dv, d3, dd3, rim, near, gown, bank, a4, a5,
    f4acc, r4, q40, r4b, q4, t4, q4b,
    f3acc, r3, q3, t3, q3b, v3,
    in_sem, halo_s, halo_r, s40_s, s40_r, ag_s, ag_r, s4_s, s4_r, b4_s, b4_r, s3_s, s3_r, b3_s, b3_r, c3_s, c3_r,
):
    d = lax.axis_index("depth")
    h = lax.axis_index("height")

    def around(dd, hh):
        return (lax.rem(d + dd + ND, ND), lax.rem(h + hh + NH, NH))

    def partner(other):
        flip = lax.rem(lax.rem(h, 4) // 2 + lax.rem(other, 4) // 2, 2)
        return (d + flip * (1 - 2 * lax.rem(d, 2)), other)

    def each(low, high, body):
        def step(k, carry):
            body(k)
            return carry

        lax.fori_loop(low, high, step, 0)

    barrier = pltpu.get_barrier_semaphore()

    def greet(device):
        pl.semaphore_signal(barrier, inc=1, device_id=device, device_id_type=MESH)

    for dd, hh in DIRECTIONS:
        greet(around(dd, hh))
    for k in range(1, NH):
        greet(partner(lax.rem(h + k, NH)))
    for k in range(2, ND - 1):
        greet(around(k, 0))

    fetches = [
        pltpu.make_async_copy(src, dst, in_sem.at[n])
        for n, (src, dst) in enumerate(
            [(x_hbm, x_in), (f4_hbm, f4_in), (f3_hbm, f3), (cot_hbm, cot)]
        )
    ]
    for fetch in fetches:
        fetch.start()

    def rows_x():
        for i in range(4):
            block = jnp.transpose(x_in[:, i].astype(F32), (1, 0, 2)).astype(BF16)
            for j in range(8):
                xb[1 + i, 1 + j] = block[j]

    fetches[0].wait()
    stage("rows_x", rows_x)

    def rows_f4():
        taps = [f4_in[t].astype(F32) for t in range(27)] + [jnp.zeros((8, 64), F32)]
        tiles = [jnp.concatenate([taps[2 * m], taps[2 * m + 1]], axis=1) for m in range(14)]
        f4[...] = jnp.concatenate(
            [jnp.concatenate(tiles[:7], axis=1), jnp.concatenate(tiles[7:], axis=1)], axis=0
        ).astype(BF16)

    fetches[1].wait()
    stage("rows_f4", rows_f4)
    pl.semaphore_wait(barrier, 8 + NH - 1 + ND - 3)

    def halo_copy(which, n, buf, cells_d, cells_h, width, beyond=None):
        dd, hh = DIRECTIONS[n]
        if beyond is None:
            src = buf.at[part(dd, cells_d, width, False), part(hh, cells_h, width, False)]
        else:
            src = beyond.at[part(-dd, cells_d, width, True), part(-hh, cells_h, width, True)]
        return pltpu.make_async_remote_copy(
            src_ref=src,
            dst_ref=buf.at[part(dd, cells_d, width, True), part(hh, cells_h, width, True)],
            send_sem=halo_s.at[which, n],
            recv_sem=halo_r.at[which, n],
            device_id=around(dd, hh),
            device_id_type=MESH,
        )

    def halo_start(*which):
        for n in range(8):
            halo_copy(which[0], n, *which[1:]).start()

    def halo_wait(*which):
        for n in range(8):
            halo_copy(which[0], n, *which[1:]).wait_send()
        for n in range(8):
            halo_copy(which[0], n, *which[1:]).wait_recv()
        _, buf, cells_d, cells_h, width = which[:5]
        channels = buf.shape[2]
        across = (width, cells_h + 2 * width, channels, 128)
        along = (cells_d + 2 * width, width, channels, 128)

        @pl.when(d == 0)
        def _():
            buf[0:width] = jnp.zeros(across, BF16)

        @pl.when(d == ND - 1)
        def _():
            buf[cells_d + width : cells_d + 2 * width] = jnp.zeros(across, BF16)

        @pl.when(h == 0)
        def _():
            buf[:, 0:width] = jnp.zeros(along, BF16)

        @pl.when(h == NH - 1)
        def _():
            buf[:, cells_h + width : cells_h + 2 * width] = jnp.zeros(along, BF16)

    def scatter_h(src, dst, send, recv, k):
        other = lax.rem(h + k, NH)
        return pltpu.make_async_remote_copy(
            src_ref=src.at[other],
            dst_ref=dst.at[k],
            send_sem=send.at[k],
            recv_sem=recv.at[k],
            device_id=partner(other),
            device_id_type=MESH,
        )

    def share_d(src, dst, send, recv, k):
        return pltpu.make_async_remote_copy(
            src_ref=src,
            dst_ref=dst.at[k],
            send_sem=send.at[k],
            recv_sem=recv.at[k],
            device_id=around(k, 0),
            device_id_type=MESH,
        )

    def gather_send(src, dst, send, recv, k):
        return pltpu.make_async_remote_copy(
            src_ref=src,
            dst_ref=dst.at[h],
            send_sem=send.at[k],
            recv_sem=recv.at[k],
            device_id=partner(lax.rem(h + k, NH)),
            device_id_type=MESH,
        )

    def gather_recv(src, dst, send, recv, k):
        return pltpu.make_async_remote_copy(
            src_ref=src,
            dst_ref=dst.at[lax.rem(h - k + NH, NH)],
            send_sem=send.at[k],
            recv_sem=recv.at[k],
            device_id=partner(lax.rem(h + k, NH)),
            device_id_type=MESH,
        )

    halo_x = (0, xb, 4, 8, 1)
    halo_p = (1, pk, 2, 4, 2)
    halo_c = (2, ck, 2, 4, 1)
    halo_g = (3, near, 4, 8, 1, rim)
    halo_start(*halo_x)
    each(1, NH, lambda k: gather_send(f4, bank, ag_s, ag_r, k).start())
    bank[h] = f4[...]

    def dilate():
        at = 2 * lax.broadcasted_iota(jnp.int32, (64, 128), 0)
        to_even = (lanes_iota((64, 128)) == at).astype(F32).astype(BF16)
        for i in range(2):
            for j in range(4):
                wide = lax.dot_general(
                    cot[i, j], to_even, (((0,), (0,)), ((), ())), preferred_element_type=F32
                )
                ck[1 + i, 1 + j] = interleave(wide[:64], wide[64:]).astype(BF16)

    def rows_f3():
        flat = f3[...].astype(F32).reshape(864, 64)
        none = jnp.zeros((288, 64), F32)
        both = jnp.concatenate(
            [jnp.concatenate([flat, none], axis=0), jnp.concatenate([none, flat], axis=0)], axis=1
        )
        a3[...] = jnp.transpose(both).astype(BF16)
        a6[...] = jnp.concatenate(
            [flat[96 * ab : 96 * ab + 96] for ab in range(9)], axis=1
        ).astype(BF16)

    def stack_row(i, j):
        xx[i, j] = stack_width(xb[i, j], 1)

    def stack_x(i):
        for j in range(8):
            stack_row(1 + i, 1 + j)

    fetches[3].wait()
    stage("dilate", dilate)
    halo_start(*halo_c)
    fetches[2].wait()
    stage("rows_f3", rows_f3)
    stage("stack_x", lambda: each(0, 4, stack_x))
    d3[0] = jnp.zeros((10, 64, 128), BF16)
    d3[5] = jnp.zeros((10, 64, 128), BF16)
    d3[:, 0] = jnp.zeros((6, 64, 128), BF16)
    d3[:, 9] = jnp.zeros((6, 64, 128), BF16)
    halo_wait(*halo_x)

    def stack_rim():
        for j in range(10):
            stack_row(0, j)
            stack_row(5, j)
        for i in range(4):
            stack_row(1 + i, 0)
            stack_row(1 + i, 9)

    stage("stack_rim", stack_rim)

    def forward3(i):
        for j in range(4):
            cols = [
                jnp.concatenate(
                    [xx[2 * i + a, 2 * j + s + b] for a in range(4) for b in range(3)], axis=0
                )
                for s in range(2)
            ]
            act = jnp.dot(a3[...], jnp.concatenate(cols, axis=1), preferred_element_type=F32)
            value, slope = gelu_parts(act)
            for di in range(2):
                for s in range(2):
                    slope3[2 * i + di, 2 * j + s] = slope[
                        64 * di : 64 * di + 64, 128 * s : 128 * s + 128
                    ]
            total = value[:64] + value[64:]
            total = total[:, :128] + total[:, 128:]
            total = (total + pltpu.roll(total, 127, 1)) * 0.125
            pk[2 + i, 2 + j] = interleave(total[:32], total[32:]).astype(BF16)

    stage("forward3", lambda: [forward3(n) for n in range(0, 2)])
    halo_start(*halo_p)

    def wait_gather(k):
        gather_send(f4, bank, ag_s, ag_r, k).wait_send()
        gather_recv(f4, bank, ag_s, ag_r, k).wait_recv()

    each(1, NH, wait_gather)

    def arrange():
        wide = [bank[s].astype(F32) for s in range(NH)]
        low = jnp.concatenate([w[:8] for w in wide], axis=0)
        high = jnp.concatenate([w[8:] for w in wide], axis=0)
        a4[...] = jnp.concatenate([low, high], axis=1).astype(BF16)
        for ab in range(9):
            a5[:, 128 * ab : 128 * ab + 128] = jnp.transpose(
                a4[:, 192 * ab : 192 * ab + 192].astype(F32)
            ).astype(BF16)

    stage("arrange", arrange)
    halo_wait(*halo_c)
    halo_wait(*halo_p)

    def stack_p(i):
        for j in range(8):
            pq[i, j] = stack_width(two_rows(pk[i, j], pk[i + 2, j]), 2)

    stage("stack_p", lambda: [stack_p(n) for n in range(0, 4)])

    def forward4(i):
        for j in range(3):
            cols = [
                jnp.concatenate(
                    [pq[i + a, 2 * j + s + b] for a in range(3) for b in range(3)], axis=0
                )
                for s in range(2)
            ]
            act = jnp.dot(
                a4[:, :1728], jnp.concatenate(cols, axis=1), preferred_element_type=F32
            )
            _, slope = gelu_parts(act)
            for s in range(2):
                col = 2 * j + s
                both = two_rows(ck[i, col], ck[i + 2, col]).astype(F32)
                dq[i, col] = (both * slope[:, 128 * s : 128 * s + 128]).astype(BF16)

    stage("forward4", lambda: [forward4(n) for n in range(0, 2)])

    def pair_rows():
        for j in range(6):
            one, two = dq[0, j], dq[1, j]
            even = lanes_iota(one.shape) % 2 == 0
            dv[0, j] = interleave_odd(one, two)
            dv[1, j] = jnp.where(even, two, one)
            dv[2, j] = interleave(one, two)

    stage("pair_rows", pair_rows)

    def back4(j):
        cols = [
            jnp.concatenate([dv[a, 2 * j + s + 2 - b] for a in range(3) for b in range(3)], axis=0)
            for s in range(2)
        ]
        y = jnp.dot(a5[...], jnp.concatenate(cols, axis=1), preferred_element_type=F32)
        for s in range(2):
            ys = y[:, 128 * s : 128 * s + 128]
            _, from_after = shifted(ys[:64], 2)
            from_before, _ = shifted(ys[128:], 2)
            back = (ys[64:128] + from_after + from_before) * 0.125
            even = lanes_iota(back.shape) % 2 == 0
            spread = [
                jnp.where(even, back, pltpu.roll(back, 1, 1)),
                jnp.where(even, pltpu.roll(back, 127, 1), back),
            ]
            for i in range(2):
                for di in range(2):
                    for dj in range(2):
                        row, col = 2 * i + di, 2 * (2 * j + s) + dj
                        delta = (spread[i] * slope3[row, col]).astype(BF16)
                        before, after = shifted(delta, 1)
                        dd3[row, col] = jnp.concatenate([after, delta, before], axis=0)
                        d3[1 + row, 1 + col] = delta

    stage("back4", lambda: [back4(n) for n in range(0, 2)])

    f3acc[...] = jnp.zeros(f3acc.shape, F32)

    def weight3(i):
        left = jnp.concatenate(
            [
                jnp.concatenate([xb[i + a, j + b] for j in range(8)], axis=1)
                for a in range(3)
                for b in range(3)
            ],
            axis=0,
        )
        right = jnp.concatenate([dd3[i, j] for j in range(8)], axis=1)
        f3acc[...] += lax.dot_general(
            left, right, (((1,), (1,)), ((), ())), preferred_element_type=F32
        )

    stage("weight3", lambda: [weight3(n) for n in range(0, 4)])

    def pack3():
        last = f3acc[:, 128:]
        flat = jnp.concatenate(
            [
                f3acc[:, :128],
                jnp.concatenate([last[:144], last[144:]], axis=1),
                jnp.zeros((80, 128), F32),
            ],
            axis=0,
        ).astype(BF16)
        for c in range(16):
            r3[c] = flat[32 * c : 32 * c + 32]

    stage("pack3", pack3)
    for k in range(1, NH):
        scatter_h(r3, q3, s3_s, s3_r, k).start()

    cells4 = [(i, j) for i in range(2) for j in range(4)]

    def weight4():
        even = lanes_iota((128, 128)) % 2 == 0
        left = jnp.concatenate(
            [
                jnp.where(even if i == 0 else ~even, dq[1 - i, 1 + j], jnp.zeros((), BF16))
                for i, j in cells4
            ],
            axis=1,
        )
        for g in range(5):
            taps = [ab for ab in (2 * g, 2 * g + 1) if ab < 9]
            right = jnp.concatenate(
                [
                    jnp.concatenate(
                        [pq[ab // 3 + 1 - i, j + ab % 3 + 1] for i, j in cells4], axis=1
                    )
                    for ab in taps
                ],
                axis=0,
            )
            piece = lax.dot_general(
                left, right, (((1,), (1,)), ((), ())), preferred_element_type=F32
            )
            if len(taps) == 1:
                piece = jnp.concatenate([piece, jnp.zeros((128, 64), F32)], axis=1)
            f4acc[:, 384 * g : 384 * g + piece.shape[1]] = piece

    stage("weight4", weight4)

    def pack4(s):
        rows = pl.ds(pl.multiple_of(8 * s, 8), 8)
        r4[lax.rem(s, 2), s // 2] = jnp.concatenate(
            [f4acc[rows, :896], f4acc[rows, 896:]], axis=0
        ).astype(BF16)

    stage("pack4", lambda: each(0, NH, pack4))
    core = lax.rem(h, 2)
    pair = h // 2

    def swap4():
        return pltpu.make_async_remote_copy(
            src_ref=r4.at[1 - core],
            dst_ref=q40,
            send_sem=s40_s,
            recv_sem=s40_r,
            device_id=(d, h + 1 - 2 * core),
            device_id_type=MESH,
        )

    def scatter4(k):
        other = lax.rem(pair + k, NH // 2)
        return pltpu.make_async_remote_copy(
            src_ref=r4b.at[other],
            dst_ref=q4.at[k],
            send_sem=s4_s.at[k],
            recv_sem=s4_r.at[k],
            device_id=partner(2 * other + core),
            device_id_type=MESH,
        )

    swap4().start()

    def gather_width(y, s):
        ys = y[:, 128 * s : 128 * s + 128]
        _, from_after = shifted(ys[:32], 1)
        from_before, _ = shifted(ys[64:], 1)
        return ys[32:64] + from_after + from_before

    def back_rim():
        for j in range(5):
            for a, row in ((0, 0), (2, 5)):
                source = 1 if row == 0 else 4
                cols = [
                    jnp.concatenate(
                        [
                            d3[source, 2 * j + s + 1 - b]
                            if 0 <= 2 * j + s + 1 - b <= 9
                            else jnp.zeros((64, 128), BF16)
                            for b in range(3)
                        ],
                        axis=0,
                    )
                    for s in range(2)
                ]
                y = jnp.dot(
                    a6[:, 192 * a : 192 * a + 192],
                    jnp.concatenate(cols, axis=1),
                    preferred_element_type=F32,
                )
                for s in range(2):
                    rim[row, 2 * j + s] = gather_width(y, s).astype(BF16)
        for b, col, source in ((0, 0, 1), (2, 9, 8)):
            weights = jnp.concatenate(
                [a6[:, 192 * a + 64 * b : 192 * a + 64 * b + 64] for a in range(3)], axis=1
            )
            for i in range(2):
                cols = [
                    jnp.concatenate([d3[2 * i + s + 2 - a, source] for a in range(3)], axis=0)
                    for s in range(2)
                ]
                y = jnp.dot(weights, jnp.concatenate(cols, axis=1), preferred_element_type=F32)
                for s in range(2):
                    rim[1 + 2 * i + s, col] = gather_width(y, s).astype(BF16)

    stage("back_rim", back_rim)
    halo_start(*halo_g)

    def wait_both(copy):
        copy.wait_send()
        copy.wait_recv()

    wait_both(swap4())

    def add4():
        for m in range(8):
            r4b[m] = (r4[core, m].astype(F32) + q40[m].astype(F32)).astype(BF16)

    stage("add4", add4)
    each(1, NH // 2, lambda k: scatter4(k).start())

    def back3(i):
        for j in range(4):
            cols = [
                jnp.concatenate(
                    [d3[i + 2 - a, 2 * j + s + 2 - b] for a in range(3) for b in range(3)], axis=0
                )
                for s in range(2)
            ]
            y = jnp.dot(a6[...], jnp.concatenate(cols, axis=1), preferred_element_type=F32)
            for s in range(2):
                gown[i, 2 * j + s] = gather_width(y, s)

    stage("back3a", lambda: [back3(n) for n in range(0, 2)])

    for k in range(1, NH):
        wait_both(scatter_h(r3, q3, s3_s, s3_r, k))

    def sum3():
        total3 = r3[h].astype(F32)
        for k in range(1, NH):
            total3 = total3 + q3[k].astype(F32)
        t3[...] = total3.astype(BF16)

    stage("sum3", sum3)
    for k in range(1, ND):
        share_d(t3, q3b, b3_s, b3_r, k).start()
    stage("back3b", lambda: [back3(n) for n in range(2, 4)])

    each(1, NH // 2, lambda k: wait_both(scatter4(k)))

    def sum4():
        total4 = r4b[pair].astype(F32)
        for k in range(1, NH // 2):
            total4 = total4 + q4[k].astype(F32)
        t4[...] = total4.astype(BF16)

    stage("sum4", sum4)
    each(1, ND, lambda k: share_d(t4, q4b, b4_s, b4_r, k).start())

    for k in range(1, ND):
        wait_both(share_d(t3, q3b, b3_s, b3_r, k))
    whole3 = t3[...].astype(F32)
    for k in range(1, ND):
        whole3 = whole3 + q3b[k].astype(F32)
    v3[h] = (whole3 * (1.0 / math.sqrt(32 * 128 * 128))).astype(BF16)
    for k in range(1, NH):
        gather_send(v3.at[h], v3, c3_s, c3_r, k).start()

    halo_wait(*halo_g)

    def finish_gv():
        for i in range(4):
            done = []
            for j in range(8):
                total = gown[i, j]
                if i in (0, 3):
                    total = total + near[0 if i == 0 else 5, 1 + j].astype(F32)
                if j in (0, 7):
                    total = total + near[1 + i, 0 if j == 0 else 9].astype(F32)
                if i in (0, 3) and j in (0, 7):
                    total = total + near[0 if i == 0 else 5, 0 if j == 0 else 9].astype(F32)
                done.append(total)
            gv_out[:, i] = jnp.transpose(jnp.stack(done, axis=0), (1, 0, 2)).astype(BF16)

    stage("finish_gv", finish_gv)

    each(1, ND, lambda k: wait_both(share_d(t4, q4b, b4_s, b4_r, k)))
    whole4 = t4[...].astype(F32)
    for k in range(1, ND):
        whole4 = whole4 + q4b[k].astype(F32)
    whole4 = whole4 * (1.0 / math.sqrt(16 * 64 * 64))
    for t in range(27):
        rows, lane = 8 * (t // 14), 64 * (t % 14)
        g4_out[t] = whole4[rows : rows + 8, lane : lane + 64]

    def wait_c3(k):
        gather_send(v3.at[h], v3, c3_s, c3_r, k).wait_send()
        gather_recv(v3.at[h], v3, c3_s, c3_r, k).wait_recv()

    for k in range(1, NH):
        wait_c3(k)
    flat3 = jnp.concatenate([v3[c].astype(F32) for c in range(14)], axis=0)
    last3 = jnp.concatenate([flat3[288:432, :64], flat3[288:432, 64:]], axis=0)
    for ab in range(9):
        rows = slice(32 * ab, 32 * ab + 32)
        g3_out[3 * ab] = flat3[rows, :64]
        g3_out[3 * ab + 1] = flat3[rows, 64:]
        g3_out[3 * ab + 2] = last3[rows]


def writer(gv, g3, g4, gv_hbm, g3_hbm, g4_hbm, sems):
    copies = [
        pltpu.make_async_copy(src, dst, sems.at[n])
        for n, (src, dst) in enumerate([(gv, gv_hbm), (g3, g3_hbm), (g4, g4_hbm)])
    ]
    for copy in copies:
        copy.start()
    for copy in copies:
        copy.wait()


def shards(volume, filters_three, filters_four, cotangent):
    vmem = pl.BlockSpec(memory_space=pltpu.VMEM)
    hbm = pl.BlockSpec(memory_space=pl.ANY)
    dma = pltpu.SemaphoreType.DMA
    gv, g3, g4 = pl.pallas_call(
        kernel,
        out_shape=(
            pltpu.VMEM((32, 4, 8, 128), BF16),
            pltpu.VMEM((27, 32, 64), F32),
            pltpu.VMEM((27, 8, 64), F32),
        ),
        in_specs=[hbm] * 4,
        out_specs=(vmem,) * 3,
        scratch_shapes=[
            pltpu.VMEM((32, 4, 8, 128), BF16),
            pltpu.VMEM((27, 32, 64), BF16),
            pltpu.VMEM((27, 8, 64), BF16),
            pltpu.VMEM((2, 4, 64, 128), BF16),
            pltpu.VMEM((16, 896), BF16),
            pltpu.VMEM((128, 1152), BF16),
            pltpu.VMEM((96, 576), BF16),
            pltpu.VMEM((6, 10, 32, 128), BF16),
            pltpu.VMEM((6, 10, 96, 128), BF16),
            pltpu.VMEM((4, 8, 64, 128), F32),
            pltpu.VMEM((4, 6, 64, 128), BF16),
            pltpu.VMEM((6, 8, 32, 128), BF16),
            pltpu.VMEM((4, 8, 192, 128), BF16),
            pltpu.VMEM((2, 6, 128, 128), BF16),
            pltpu.VMEM((3, 6, 128, 128), BF16),
            pltpu.VMEM((6, 10, 64, 128), BF16),
            pltpu.VMEM((4, 8, 192, 128), BF16),
            pltpu.VMEM((6, 10, 32, 128), BF16),
            pltpu.VMEM((6, 10, 32, 128), BF16),
            pltpu.VMEM((4, 8, 32, 128), F32),
            pltpu.VMEM((16, 16, 896), BF16),
            pltpu.VMEM((128, 1792), BF16),
            pltpu.VMEM((192, 1152), BF16),
            pltpu.VMEM((128, 1792), F32),
            pltpu.VMEM((2, 8, 16, 896), BF16),
            pltpu.VMEM((8, 16, 896), BF16),
            pltpu.VMEM((8, 16, 896), BF16),
            pltpu.VMEM((8, 16, 896), BF16),
            pltpu.VMEM((16, 896), BF16),
            pltpu.VMEM((8, 16, 896), BF16),
            pltpu.VMEM((288, 192), F32),
            pltpu.VMEM((16, 32, 128), BF16),
            pltpu.VMEM((16, 32, 128), BF16),
            pltpu.VMEM((32, 128), BF16),
            pltpu.VMEM((8, 32, 128), BF16),
            pltpu.VMEM((16, 32, 128), BF16),
            dma((4,)),
            dma((4, 8)),
            dma((4, 8)),
            dma,
            dma,
            dma((16,)),
            dma((16,)),
            dma((16,)),
            dma((16,)),
            dma((8,)),
            dma((8,)),
            dma((16,)),
            dma((16,)),
            dma((8,)),
            dma((8,)),
            dma((16,)),
            dma((16,)),
        ],
        compiler_params=pltpu.CompilerParams(
            collective_id=0, has_side_effects=True, vmem_limit_bytes=58000 * 1024
        ),
    )(
        volume,
        jnp.transpose(filters_three, (0, 2, 1)),
        filters_four,
        jnp.transpose(cotangent, (1, 2, 3, 0)),
    )
    gv, g3, g4 = pl.pallas_call(
        writer,
        out_shape=(
            pltpu.HBM((32, 4, 8, 128), BF16),
            pltpu.HBM((27, 32, 64), F32),
            pltpu.HBM((27, 8, 64), F32),
        ),
        in_specs=[hbm] * 3,
        out_specs=(hbm,) * 3,
        scratch_shapes=[dma((3,))],
        compiler_params=pltpu.CompilerParams(vmem_limit_bytes=1024 * 1024),
    )(gv, g3, g4)
    return (gv, jnp.transpose(g3, (0, 2, 1)), g4)


def solution(mesh):
    in_specs = (
        P(None, "depth", "height", None),
        P(),
        P(None, "height", None),
        P(None, "depth", "height", None),
    )
    out_specs = (P(None, "depth", "height", None), P(), P(None, "height", None))
    return jax.shard_map(shards, mesh=mesh, in_specs=in_specs, out_specs=out_specs, check_vma=False)
```

```python
import functools
import math

import jax
import jax.numpy as jnp
from jax import lax
from jax.experimental import pallas as pl
from jax.experimental.pallas import tpu as pltpu
from jax.sharding import PartitionSpec as P

TANH_SCALE = 0.7978845608028654
CUBIC_TERM = 0.044715
MESH = pl.DeviceIdType.MESH
F32 = jnp.float32
BF16 = jnp.bfloat16

ND = 8
NH = 16
DIRECTIONS = [(dd, hh) for dd in (-1, 0, 1) for hh in (-1, 0, 1) if (dd, hh) != (0, 0)]


def gelu_parts(v):
    u = v * v
    inner = jnp.tanh(v * (TANH_SCALE + TANH_SCALE * CUBIC_TERM * u))
    half = 0.5 + 0.5 * inner
    value = v * half
    slope = half + value * (1.0 - inner) * (TANH_SCALE + 3.0 * TANH_SCALE * CUBIC_TERM * u)
    return value, slope


def stage(name, body):
    body()


def lanes_iota(shape):
    return lax.broadcasted_iota(jnp.int32, shape, len(shape) - 1)


def shifted(v, step):
    lane = lanes_iota(v.shape)
    zero = jnp.zeros((), v.dtype)
    before = jnp.where(lane < step, zero, pltpu.roll(v, step, 1))
    after = jnp.where(lane >= 128 - step, zero, pltpu.roll(v, 128 - step, 1))
    return before, after


def stack_width(row, step):
    before, after = shifted(row, step)
    return jnp.concatenate([before, row, after], axis=0)


def part(at, cells, width, far):
    if at == 0:
        return pl.ds(width, cells)
    if at < 0:
        return pl.ds(cells + width, width) if far else pl.ds(width, width)
    return pl.ds(0, width) if far else pl.ds(cells, width)


def interleave(even_row, odd_row):
    even = lanes_iota(even_row.shape) % 2 == 0
    return jnp.where(even, even_row, pltpu.roll(odd_row, 1, 1))


def interleave_odd(even_row, odd_row):
    even = lanes_iota(even_row.shape) % 2 == 0
    return jnp.where(even, pltpu.roll(even_row, 127, 1), odd_row)


def two_rows(first, second):
    return jnp.concatenate([interleave(first, second), interleave_odd(first, second)], axis=0)


def kernel(
    x_hbm, f3_hbm, f4_hbm, cot_hbm,
    gv_out, g3_out, g4_out,
    x_in, f3, f4_in, cot, f4, a3, a6,
    xb, xx, slope3, ck, pk, pq, dq, dv, d3, dd3, rim, near, gown, bank, a4, a5,
    f4acc, r4, q40, r4b, q4, t4, q4b,
    f3acc, r3, q3, t3, q3b, v3,
    in_sem, halo_s, halo_r, s40_s, s40_r, ag_s, ag_r, s4_s, s4_r, b4_s, b4_r, s3_s, s3_r, b3_s, b3_r, c3_s, c3_r,
):
    d = lax.axis_index("depth")
    h = lax.axis_index("height")

    def around(dd, hh):
        return (lax.rem(d + dd + ND, ND), lax.rem(h + hh + NH, NH))

    def partner(other):
        flip = lax.rem(lax.rem(h, 4) // 2 + lax.rem(other, 4) // 2, 2)
        return (d + flip * (1 - 2 * lax.rem(d, 2)), other)

    def each(low, high, body):
        def step(k, carry):
            body(k)
            return carry

        lax.fori_loop(low, high, step, 0)

    barrier = pltpu.get_barrier_semaphore()

    def greet(device):
        pl.semaphore_signal(barrier, inc=1, device_id=device, device_id_type=MESH)

    for dd, hh in DIRECTIONS:
        greet(around(dd, hh))
    for k in range(1, NH):
        greet(partner(lax.rem(h + k, NH)))
    for k in range(2, ND - 1):
        greet(around(k, 0))

    fetches = [
        pltpu.make_async_copy(src, dst, in_sem.at[n])
        for n, (src, dst) in enumerate(
            [(x_hbm, x_in), (f4_hbm, f4_in), (f3_hbm, f3), (cot_hbm, cot)]
        )
    ]
    for fetch in fetches:
        fetch.start()

    def rows_x():
        for i in range(4):
            block = jnp.transpose(x_in[:, i].astype(F32), (1, 0, 2)).astype(BF16)
            for j in range(8):
                xb[1 + i, 1 + j] = block[j]

    fetches[0].wait()
    stage("rows_x", rows_x)

    def rows_f4():
        taps = [f4_in[t].astype(F32) for t in range(27)] + [jnp.zeros((8, 64), F32)]
        tiles = [jnp.concatenate([taps[2 * m], taps[2 * m + 1]], axis=1) for m in range(14)]
        f4[...] = jnp.concatenate(
            [jnp.concatenate(tiles[:7], axis=1), jnp.concatenate(tiles[7:], axis=1)], axis=0
        ).astype(BF16)

    fetches[1].wait()
    stage("rows_f4", rows_f4)
    pl.semaphore_wait(barrier, 8 + NH - 1 + ND - 3)

    def halo_copy(which, n, buf, cells_d, cells_h, width, beyond=None):
        dd, hh = DIRECTIONS[n]
        if beyond is None:
            src = buf.at[part(dd, cells_d, width, False), part(hh, cells_h, width, False)]
        else:
            src = beyond.at[part(-dd, cells_d, width, True), part(-hh, cells_h, width, True)]
        return pltpu.make_async_remote_copy(
            src_ref=src,
            dst_ref=buf.at[part(dd, cells_d, width, True), part(hh, cells_h, width, True)],
            send_sem=halo_s.at[which, n],
            recv_sem=halo_r.at[which, n],
            device_id=around(dd, hh),
            device_id_type=MESH,
        )

    def pooled_copy(row, n):
        dd, hh = DIRECTIONS[n]
        return pltpu.make_async_remote_copy(
            src_ref=pk.at[pl.ds(2 + row, 1), part(hh, 4, 2, False)],
            dst_ref=pk.at[pl.ds(2 - 2 * dd + row, 1), part(hh, 4, 2, True)],
            send_sem=halo_s.at[1 + 3 * row, n],
            recv_sem=halo_r.at[1 + 3 * row, n],
            device_id=around(dd, hh),
            device_id_type=MESH,
        )

    def halo_start(*which):
        for n in range(8):
            halo_copy(which[0], n, *which[1:]).start()

    def halo_wait(*which):
        for n in range(8):
            halo_copy(which[0], n, *which[1:]).wait_send()
        for n in range(8):
            halo_copy(which[0], n, *which[1:]).wait_recv()
        zero_outside(*which[1:5])

    def zero_outside(buf, cells_d, cells_h, width):
        channels = buf.shape[2]
        across = (width, cells_h + 2 * width, channels, 128)
        along = (cells_d + 2 * width, width, channels, 128)

        @pl.when(d == 0)
        def _():
            buf[0:width] = jnp.zeros(across, BF16)

        @pl.when(d == ND - 1)
        def _():
            buf[cells_d + width : cells_d + 2 * width] = jnp.zeros(across, BF16)

        @pl.when(h == 0)
        def _():
            buf[:, 0:width] = jnp.zeros(along, BF16)

        @pl.when(h == NH - 1)
        def _():
            buf[:, cells_h + width : cells_h + 2 * width] = jnp.zeros(along, BF16)

    def scatter_h(src, dst, send, recv, k):
        other = lax.rem(h + k, NH)
        return pltpu.make_async_remote_copy(
            src_ref=src.at[other],
            dst_ref=dst.at[k],
            send_sem=send.at[k],
            recv_sem=recv.at[k],
            device_id=partner(other),
            device_id_type=MESH,
        )

    def share_d(src, dst, send, recv, k):
        return pltpu.make_async_remote_copy(
            src_ref=src,
            dst_ref=dst.at[k],
            send_sem=send.at[k],
            recv_sem=recv.at[k],
            device_id=around(k, 0),
            device_id_type=MESH,
        )

    def gather_send(src, dst, send, recv, k):
        return pltpu.make_async_remote_copy(
            src_ref=src,
            dst_ref=dst.at[h],
            send_sem=send.at[k],
            recv_sem=recv.at[k],
            device_id=partner(lax.rem(h + k, NH)),
            device_id_type=MESH,
        )

    def gather_recv(src, dst, send, recv, k):
        return pltpu.make_async_remote_copy(
            src_ref=src,
            dst_ref=dst.at[lax.rem(h - k + NH, NH)],
            send_sem=send.at[k],
            recv_sem=recv.at[k],
            device_id=partner(lax.rem(h + k, NH)),
            device_id_type=MESH,
        )

    halo_x = (0, xb, 4, 8, 1)
    halo_c = (2, ck, 2, 4, 1)
    halo_g = (3, near, 4, 8, 1, rim)
    halo_start(*halo_x)
    each(1, NH, lambda k: gather_send(f4, bank, ag_s, ag_r, k).start())
    bank[h] = f4[...]

    def dilate():
        at = 2 * lax.broadcasted_iota(jnp.int32, (64, 128), 0)
        to_even = (lanes_iota((64, 128)) == at).astype(F32).astype(BF16)
        for i in range(2):
            for j in range(4):
                wide = lax.dot_general(
                    cot[i, j], to_even, (((0,), (0,)), ((), ())), preferred_element_type=F32
                )
                ck[1 + i, 1 + j] = interleave(wide[:64], wide[64:]).astype(BF16)

    def rows_f3():
        flat = f3[...].astype(F32).reshape(864, 64)
        none = jnp.zeros((288, 64), F32)
        both = jnp.concatenate(
            [jnp.concatenate([flat, none], axis=0), jnp.concatenate([none, flat], axis=0)], axis=1
        )
        a3[...] = jnp.transpose(both).astype(BF16)
        a6[...] = jnp.concatenate(
            [flat[96 * ab : 96 * ab + 96] for ab in range(9)], axis=1
        ).astype(BF16)

    def stack_row(i, j):
        xx[i, j] = stack_width(xb[i, j], 1)

    def stack_x(i):
        for j in range(8):
            stack_row(1 + i, 1 + j)

    fetches[3].wait()
    stage("dilate", dilate)
    halo_start(*halo_c)
    fetches[2].wait()
    stage("rows_f3", rows_f3)
    stage("stack_x", lambda: each(0, 4, stack_x))
    d3[0] = jnp.zeros((10, 64, 128), BF16)
    d3[5] = jnp.zeros((10, 64, 128), BF16)
    d3[:, 0] = jnp.zeros((6, 64, 128), BF16)
    d3[:, 9] = jnp.zeros((6, 64, 128), BF16)
    halo_wait(*halo_x)

    def stack_rim():
        for j in range(10):
            stack_row(0, j)
            stack_row(5, j)
        for i in range(4):
            stack_row(1 + i, 0)
            stack_row(1 + i, 9)

    stage("stack_rim", stack_rim)

    def forward3(i):
        for j in range(4):
            cols = [
                jnp.concatenate(
                    [xx[2 * i + a, 2 * j + s + b] for a in range(4) for b in range(3)], axis=0
                )
                for s in range(2)
            ]
            act = jnp.dot(a3[...], jnp.concatenate(cols, axis=1), preferred_element_type=F32)
            value, slope = gelu_parts(act)
            for di in range(2):
                for s in range(2):
                    slope3[2 * i + di, 2 * j + s] = slope[
                        64 * di : 64 * di + 64, 128 * s : 128 * s + 128
                    ]
            total = value[:64] + value[64:]
            total = total[:, :128] + total[:, 128:]
            total = (total + pltpu.roll(total, 127, 1)) * 0.125
            pk[2 + i, 2 + j] = interleave(total[:32], total[32:]).astype(BF16)

    def forward_and_send(i):
        forward3(i)
        for n in range(8):
            pooled_copy(i, n).start()

    stage("forward3", lambda: [forward_and_send(n) for n in range(0, 2)])

    def wait_gather(k):
        gather_send(f4, bank, ag_s, ag_r, k).wait_send()
        gather_recv(f4, bank, ag_s, ag_r, k).wait_recv()

    each(1, NH, wait_gather)

    def arrange():
        wide = [bank[s].astype(F32) for s in range(NH)]
        low = jnp.concatenate([w[:8] for w in wide], axis=0)
        high = jnp.concatenate([w[8:] for w in wide], axis=0)
        a4[...] = jnp.concatenate([low, high], axis=1).astype(BF16)
        for ab in range(9):
            a5[:, 128 * ab : 128 * ab + 128] = jnp.transpose(
                a4[:, 192 * ab : 192 * ab + 192].astype(F32)
            ).astype(BF16)

    stage("arrange", arrange)
    halo_wait(*halo_c)
    for row in range(2):
        for n in range(8):
            pooled_copy(row, n).wait_send()
        for n in range(8):
            pooled_copy(row, n).wait_recv()
    zero_outside(pk, 2, 4, 2)

    def stack_p(i):
        for j in range(8):
            pq[i, j] = stack_width(two_rows(pk[i, j], pk[i + 2, j]), 2)

    stage("stack_p", lambda: [stack_p(n) for n in range(0, 4)])

    def forward4(i):
        for j in range(3):
            cols = [
                jnp.concatenate(
                    [pq[i + a, 2 * j + s + b] for a in range(3) for b in range(3)], axis=0
                )
                for s in range(2)
            ]
            act = jnp.dot(
                a4[:, :1728], jnp.concatenate(cols, axis=1), preferred_element_type=F32
            )
            _, slope = gelu_parts(act)
            for s in range(2):
                col = 2 * j + s
                both = two_rows(ck[i, col], ck[i + 2, col]).astype(F32)
                dq[i, col] = (both * slope[:, 128 * s : 128 * s + 128]).astype(BF16)

    stage("forward4", lambda: [forward4(n) for n in range(0, 2)])

    def pair_rows():
        for j in range(6):
            one, two = dq[0, j], dq[1, j]
            even = lanes_iota(one.shape) % 2 == 0
            dv[0, j] = interleave_odd(one, two)
            dv[1, j] = jnp.where(even, two, one)
            dv[2, j] = interleave(one, two)

    stage("pair_rows", pair_rows)

    def back4(j):
        cols = [
            jnp.concatenate([dv[a, 2 * j + s + 2 - b] for a in range(3) for b in range(3)], axis=0)
            for s in range(2)
        ]
        y = jnp.dot(a5[...], jnp.concatenate(cols, axis=1), preferred_element_type=F32)
        for s in range(2):
            ys = y[:, 128 * s : 128 * s + 128]
            _, from_after = shifted(ys[:64], 2)
            from_before, _ = shifted(ys[128:], 2)
            back = (ys[64:128] + from_after + from_before) * 0.125
            even = lanes_iota(back.shape) % 2 == 0
            spread = [
                jnp.where(even, back, pltpu.roll(back, 1, 1)),
                jnp.where(even, pltpu.roll(back, 127, 1), back),
            ]
            for i in range(2):
                for di in range(2):
                    for dj in range(2):
                        row, col = 2 * i + di, 2 * (2 * j + s) + dj
                        delta = (spread[i] * slope3[row, col]).astype(BF16)
                        before, after = shifted(delta, 1)
                        dd3[row, col] = jnp.concatenate([after, delta, before], axis=0)
                        d3[1 + row, 1 + col] = delta

    stage("back4", lambda: [back4(n) for n in range(0, 2)])

    f3acc[...] = jnp.zeros(f3acc.shape, F32)

    def weight3(i):
        left = jnp.concatenate(
            [
                jnp.concatenate([xb[i + a, j + b] for j in range(8)], axis=1)
                for a in range(3)
                for b in range(3)
            ],
            axis=0,
        )
        right = jnp.concatenate([dd3[i, j] for j in range(8)], axis=1)
        f3acc[...] += lax.dot_general(
            left, right, (((1,), (1,)), ((), ())), preferred_element_type=F32
        )

    stage("weight3", lambda: [weight3(n) for n in range(0, 4)])

    def pack3():
        last = f3acc[:, 128:]
        flat = jnp.concatenate(
            [
                f3acc[:, :128],
                jnp.concatenate([last[:144], last[144:]], axis=1),
                jnp.zeros((80, 128), F32),
            ],
            axis=0,
        ).astype(BF16)
        for c in range(16):
            r3[c] = flat[32 * c : 32 * c + 32]

    stage("pack3", pack3)
    for k in range(1, NH):
        scatter_h(r3, q3, s3_s, s3_r, k).start()

    cells4 = [(i, j) for i in range(2) for j in range(4)]

    def weight4():
        even = lanes_iota((128, 128)) % 2 == 0
        left = jnp.concatenate(
            [
                jnp.where(even if i == 0 else ~even, dq[1 - i, 1 + j], jnp.zeros((), BF16))
                for i, j in cells4
            ],
            axis=1,
        )
        for g in range(5):
            taps = [ab for ab in (2 * g, 2 * g + 1) if ab < 9]
            right = jnp.concatenate(
                [
                    jnp.concatenate(
                        [pq[ab // 3 + 1 - i, j + ab % 3 + 1] for i, j in cells4], axis=1
                    )
                    for ab in taps
                ],
                axis=0,
            )
            piece = lax.dot_general(
                left, right, (((1,), (1,)), ((), ())), preferred_element_type=F32
            )
            if len(taps) == 1:
                piece = jnp.concatenate([piece, jnp.zeros((128, 64), F32)], axis=1)
            f4acc[:, 384 * g : 384 * g + piece.shape[1]] = piece

    stage("weight4", weight4)

    def pack4(s):
        rows = pl.ds(pl.multiple_of(8 * s, 8), 8)
        r4[lax.rem(s, 2), s // 2] = jnp.concatenate(
            [f4acc[rows, :896], f4acc[rows, 896:]], axis=0
        ).astype(BF16)

    stage("pack4", lambda: each(0, NH, pack4))
    core = lax.rem(h, 2)
    pair = h // 2

    def swap4():
        return pltpu.make_async_remote_copy(
            src_ref=r4.at[1 - core],
            dst_ref=q40,
            send_sem=s40_s,
            recv_sem=s40_r,
            device_id=(d, h + 1 - 2 * core),
            device_id_type=MESH,
        )

    def scatter4(k):
        other = lax.rem(pair + k, NH // 2)
        return pltpu.make_async_remote_copy(
            src_ref=r4b.at[other],
            dst_ref=q4.at[k],
            send_sem=s4_s.at[k],
            recv_sem=s4_r.at[k],
            device_id=partner(2 * other + core),
            device_id_type=MESH,
        )

    swap4().start()

    def gather_width(y, s):
        ys = y[:, 128 * s : 128 * s + 128]
        _, from_after = shifted(ys[:32], 1)
        from_before, _ = shifted(ys[64:], 1)
        return ys[32:64] + from_after + from_before

    def back_rim():
        for j in range(5):
            for a, row in ((0, 0), (2, 5)):
                source = 1 if row == 0 else 4
                cols = [
                    jnp.concatenate(
                        [
                            d3[source, 2 * j + s + 1 - b]
                            if 0 <= 2 * j + s + 1 - b <= 9
                            else jnp.zeros((64, 128), BF16)
                            for b in range(3)
                        ],
                        axis=0,
                    )
                    for s in range(2)
                ]
                y = jnp.dot(
                    a6[:, 192 * a : 192 * a + 192],
                    jnp.concatenate(cols, axis=1),
                    preferred_element_type=F32,
                )
                for s in range(2):
                    rim[row, 2 * j + s] = gather_width(y, s).astype(BF16)
        for b, col, source in ((0, 0, 1), (2, 9, 8)):
            weights = jnp.concatenate(
                [a6[:, 192 * a + 64 * b : 192 * a + 64 * b + 64] for a in range(3)], axis=1
            )
            for i in range(2):
                cols = [
                    jnp.concatenate([d3[2 * i + s + 2 - a, source] for a in range(3)], axis=0)
                    for s in range(2)
                ]
                y = jnp.dot(weights, jnp.concatenate(cols, axis=1), preferred_element_type=F32)
                for s in range(2):
                    rim[1 + 2 * i + s, col] = gather_width(y, s).astype(BF16)

    stage("back_rim", back_rim)
    halo_start(*halo_g)

    def wait_both(copy):
        copy.wait_send()
        copy.wait_recv()

    wait_both(swap4())

    def add4():
        for m in range(8):
            r4b[m] = (r4[core, m].astype(F32) + q40[m].astype(F32)).astype(BF16)

    stage("add4", add4)
    each(1, NH // 2, lambda k: scatter4(k).start())

    def back3(i):
        for j in range(4):
            cols = [
                jnp.concatenate(
                    [d3[i + 2 - a, 2 * j + s + 2 - b] for a in range(3) for b in range(3)], axis=0
                )
                for s in range(2)
            ]
            y = jnp.dot(a6[...], jnp.concatenate(cols, axis=1), preferred_element_type=F32)
            for s in range(2):
                gown[i, 2 * j + s] = gather_width(y, s)

    stage("back3a", lambda: [back3(n) for n in range(0, 2)])

    for k in range(1, NH):
        wait_both(scatter_h(r3, q3, s3_s, s3_r, k))

    def sum3():
        total3 = r3[h].astype(F32)
        for k in range(1, NH):
            total3 = total3 + q3[k].astype(F32)
        t3[...] = total3.astype(BF16)

    stage("sum3", sum3)
    for k in range(1, ND):
        share_d(t3, q3b, b3_s, b3_r, k).start()
    stage("back3b", lambda: [back3(n) for n in range(2, 4)])

    for k in range(1, ND):
        wait_both(share_d(t3, q3b, b3_s, b3_r, k))
    whole3 = t3[...].astype(F32)
    for k in range(1, ND):
        whole3 = whole3 + q3b[k].astype(F32)
    v3[h] = (whole3 * (1.0 / math.sqrt(32 * 128 * 128))).astype(BF16)
    for k in range(1, NH):
        gather_send(v3.at[h], v3, c3_s, c3_r, k).start()

    each(1, NH // 2, lambda k: wait_both(scatter4(k)))

    def sum4():
        total4 = r4b[pair].astype(F32)
        for k in range(1, NH // 2):
            total4 = total4 + q4[k].astype(F32)
        t4[...] = total4.astype(BF16)

    stage("sum4", sum4)
    each(1, ND, lambda k: share_d(t4, q4b, b4_s, b4_r, k).start())

    halo_wait(*halo_g)

    def finish_gv():
        for i in range(4):
            done = []
            for j in range(8):
                total = gown[i, j]
                if i in (0, 3):
                    total = total + near[0 if i == 0 else 5, 1 + j].astype(F32)
                if j in (0, 7):
                    total = total + near[1 + i, 0 if j == 0 else 9].astype(F32)
                if i in (0, 3) and j in (0, 7):
                    total = total + near[0 if i == 0 else 5, 0 if j == 0 else 9].astype(F32)
                done.append(total)
            gv_out[:, i] = jnp.transpose(jnp.stack(done, axis=0), (1, 0, 2)).astype(BF16)

    stage("finish_gv", finish_gv)

    each(1, ND, lambda k: wait_both(share_d(t4, q4b, b4_s, b4_r, k)))
    whole4 = t4[...].astype(F32)
    for k in range(1, ND):
        whole4 = whole4 + q4b[k].astype(F32)
    whole4 = whole4 * (1.0 / math.sqrt(16 * 64 * 64))
    for t in range(27):
        rows, lane = 8 * (t // 14), 64 * (t % 14)
        g4_out[t] = whole4[rows : rows + 8, lane : lane + 64]

    def wait_c3(k):
        gather_send(v3.at[h], v3, c3_s, c3_r, k).wait_send()
        gather_recv(v3.at[h], v3, c3_s, c3_r, k).wait_recv()

    for k in range(1, NH):
        wait_c3(k)
    flat3 = jnp.concatenate([v3[c].astype(F32) for c in range(14)], axis=0)
    last3 = jnp.concatenate([flat3[288:432, :64], flat3[288:432, 64:]], axis=0)
    for ab in range(9):
        rows = slice(32 * ab, 32 * ab + 32)
        g3_out[3 * ab] = flat3[rows, :64]
        g3_out[3 * ab + 1] = flat3[rows, 64:]
        g3_out[3 * ab + 2] = last3[rows]


def writer(gv, g3, g4, gv_hbm, g3_hbm, g4_hbm, sems):
    copies = [
        pltpu.make_async_copy(src, dst, sems.at[n])
        for n, (src, dst) in enumerate([(gv, gv_hbm), (g3, g3_hbm), (g4, g4_hbm)])
    ]
    for copy in copies:
        copy.start()
    for copy in copies:
        copy.wait()


def shards(volume, filters_three, filters_four, cotangent):
    vmem = pl.BlockSpec(memory_space=pltpu.VMEM)
    hbm = pl.BlockSpec(memory_space=pl.ANY)
    dma = pltpu.SemaphoreType.DMA
    gv, g3, g4 = pl.pallas_call(
        kernel,
        out_shape=(
            pltpu.VMEM((32, 4, 8, 128), BF16),
            pltpu.VMEM((27, 32, 64), F32),
            pltpu.VMEM((27, 8, 64), F32),
        ),
        in_specs=[hbm] * 4,
        out_specs=(vmem,) * 3,
        scratch_shapes=[
            pltpu.VMEM((32, 4, 8, 128), BF16),
            pltpu.VMEM((27, 32, 64), BF16),
            pltpu.VMEM((27, 8, 64), BF16),
            pltpu.VMEM((2, 4, 64, 128), BF16),
            pltpu.VMEM((16, 896), BF16),
            pltpu.VMEM((128, 1152), BF16),
            pltpu.VMEM((96, 576), BF16),
            pltpu.VMEM((6, 10, 32, 128), BF16),
            pltpu.VMEM((6, 10, 96, 128), BF16),
            pltpu.VMEM((4, 8, 64, 128), F32),
            pltpu.VMEM((4, 6, 64, 128), BF16),
            pltpu.VMEM((6, 8, 32, 128), BF16),
            pltpu.VMEM((4, 8, 192, 128), BF16),
            pltpu.VMEM((2, 6, 128, 128), BF16),
            pltpu.VMEM((3, 6, 128, 128), BF16),
            pltpu.VMEM((6, 10, 64, 128), BF16),
            pltpu.VMEM((4, 8, 192, 128), BF16),
            pltpu.VMEM((6, 10, 32, 128), BF16),
            pltpu.VMEM((6, 10, 32, 128), BF16),
            pltpu.VMEM((4, 8, 32, 128), F32),
            pltpu.VMEM((16, 16, 896), BF16),
            pltpu.VMEM((128, 1792), BF16),
            pltpu.VMEM((192, 1152), BF16),
            pltpu.VMEM((128, 1792), F32),
            pltpu.VMEM((2, 8, 16, 896), BF16),
            pltpu.VMEM((8, 16, 896), BF16),
            pltpu.VMEM((8, 16, 896), BF16),
            pltpu.VMEM((8, 16, 896), BF16),
            pltpu.VMEM((16, 896), BF16),
            pltpu.VMEM((8, 16, 896), BF16),
            pltpu.VMEM((288, 192), F32),
            pltpu.VMEM((16, 32, 128), BF16),
            pltpu.VMEM((16, 32, 128), BF16),
            pltpu.VMEM((32, 128), BF16),
            pltpu.VMEM((8, 32, 128), BF16),
            pltpu.VMEM((16, 32, 128), BF16),
            dma((4,)),
            dma((5, 8)),
            dma((5, 8)),
            dma,
            dma,
            dma((16,)),
            dma((16,)),
            dma((16,)),
            dma((16,)),
            dma((8,)),
            dma((8,)),
            dma((16,)),
            dma((16,)),
            dma((8,)),
            dma((8,)),
            dma((16,)),
            dma((16,)),
        ],
        compiler_params=pltpu.CompilerParams(
            collective_id=0, has_side_effects=True, vmem_limit_bytes=58000 * 1024
        ),
    )(
        volume,
        jnp.transpose(filters_three, (0, 2, 1)),
        filters_four,
        jnp.transpose(cotangent, (1, 2, 3, 0)),
    )
    gv, g3, g4 = pl.pallas_call(
        writer,
        out_shape=(
            pltpu.HBM((32, 4, 8, 128), BF16),
            pltpu.HBM((27, 32, 64), F32),
            pltpu.HBM((27, 8, 64), F32),
        ),
        in_specs=[hbm] * 3,
        out_specs=(hbm,) * 3,
        scratch_shapes=[dma((3,))],
        compiler_params=pltpu.CompilerParams(vmem_limit_bytes=1024 * 1024),
    )(gv, g3, g4)
    return (gv, jnp.transpose(g3, (0, 2, 1)), g4)


def solution(mesh):
    in_specs = (
        P(None, "depth", "height", None),
        P(),
        P(None, "height", None),
        P(None, "depth", "height", None),
    )
    out_specs = (P(None, "depth", "height", None), P(), P(None, "height", None))
    return jax.shard_map(shards, mesh=mesh, in_specs=in_specs, out_specs=out_specs, check_vma=False)
```

```python
import functools
import math

import jax
import jax.numpy as jnp
from jax import lax
from jax.experimental import pallas as pl
from jax.experimental.pallas import tpu as pltpu
from jax.sharding import PartitionSpec as P

TANH_SCALE = 0.7978845608028654
CUBIC_TERM = 0.044715
MESH = pl.DeviceIdType.MESH
F32 = jnp.float32
BF16 = jnp.bfloat16

ND = 8
NH = 16
FILLED = 14
DIRECTIONS = [(dd, hh) for dd in (-1, 0, 1) for hh in (-1, 0, 1) if (dd, hh) != (0, 0)]


def gelu_parts(v):
    u = v * v
    inner = jnp.tanh(v * (TANH_SCALE + TANH_SCALE * CUBIC_TERM * u))
    half = 0.5 + 0.5 * inner
    value = v * half
    slope = half + value * (1.0 - inner) * (TANH_SCALE + 3.0 * TANH_SCALE * CUBIC_TERM * u)
    return value, slope


def stage(name, body):
    body()


def lanes_iota(shape):
    return lax.broadcasted_iota(jnp.int32, shape, len(shape) - 1)


def shifted(v, step):
    lane = lanes_iota(v.shape)
    zero = jnp.zeros((), v.dtype)
    before = jnp.where(lane < step, zero, pltpu.roll(v, step, 1))
    after = jnp.where(lane >= 128 - step, zero, pltpu.roll(v, 128 - step, 1))
    return before, after


def stack_width(row, step):
    before, after = shifted(row, step)
    return jnp.concatenate([before, row, after], axis=0)


def part(at, cells, width, far):
    if at == 0:
        return pl.ds(width, cells)
    if at < 0:
        return pl.ds(cells + width, width) if far else pl.ds(width, width)
    return pl.ds(0, width) if far else pl.ds(cells, width)


def interleave(even_row, odd_row):
    even = lanes_iota(even_row.shape) % 2 == 0
    return jnp.where(even, even_row, pltpu.roll(odd_row, 1, 1))


def interleave_odd(even_row, odd_row):
    even = lanes_iota(even_row.shape) % 2 == 0
    return jnp.where(even, pltpu.roll(even_row, 127, 1), odd_row)


def two_rows(first, second):
    return jnp.concatenate([interleave(first, second), interleave_odd(first, second)], axis=0)


def kernel(
    x_hbm, f3_hbm, f4_hbm, cot_hbm,
    gv_out, g3_out, g4_out,
    x_in, f3, f4_in, cot, f4, a3, a6,
    xb, xx, slope3, ck, pk, pq, dq, dv, d3, dd3, rim, near, gown, bank, a4, a5,
    f4acc, r4, q40, r4b, q4, t4, q4b,
    f3acc, r3, q3, t3, q3b, v3,
    in_sem, halo_s, halo_r, s40_s, s40_r, ag_s, ag_r, s4_s, s4_r, b4_s, b4_r, s3_s, s3_r, b3_s, b3_r, c3_s, c3_r,
):
    d = lax.axis_index("depth")
    h = lax.axis_index("height")

    def around(dd, hh):
        return (lax.rem(d + dd + ND, ND), lax.rem(h + hh + NH, NH))

    def partner(other):
        flip = lax.rem(lax.rem(h, 4) // 2 + lax.rem(other, 4) // 2, 2)
        return (d + flip * (1 - 2 * lax.rem(d, 2)), other)

    def each(low, high, body):
        def step(k, carry):
            body(k)
            return carry

        lax.fori_loop(low, high, step, 0)

    barrier = pltpu.get_barrier_semaphore()

    def greet(device):
        pl.semaphore_signal(barrier, inc=1, device_id=device, device_id_type=MESH)

    for dd, hh in DIRECTIONS:
        greet(around(dd, hh))
    for k in range(1, NH):
        greet(partner(lax.rem(h + k, NH)))
    for k in range(2, ND - 1):
        greet(around(k, 0))

    fetches = [
        pltpu.make_async_copy(src, dst, in_sem.at[n])
        for n, (src, dst) in enumerate(
            [(x_hbm, x_in), (f4_hbm, f4_in), (f3_hbm, f3), (cot_hbm, cot)]
        )
    ]
    for fetch in fetches:
        fetch.start()

    def rows_x():
        for i in range(4):
            block = jnp.transpose(x_in[:, i].astype(F32), (1, 0, 2)).astype(BF16)
            for j in range(8):
                xb[1 + i, 1 + j] = block[j]

    fetches[0].wait()
    stage("rows_x", rows_x)

    def rows_f4():
        taps = [f4_in[t].astype(F32) for t in range(27)] + [jnp.zeros((8, 64), F32)]
        tiles = [jnp.concatenate([taps[2 * m], taps[2 * m + 1]], axis=1) for m in range(14)]
        f4[...] = jnp.concatenate(
            [jnp.concatenate(tiles[:7], axis=1), jnp.concatenate(tiles[7:], axis=1)], axis=0
        ).astype(BF16)

    fetches[1].wait()
    stage("rows_f4", rows_f4)
    pl.semaphore_wait(barrier, 8 + NH - 1 + ND - 3)

    def halo_copy(which, n, buf, cells_d, cells_h, width, beyond=None):
        dd, hh = DIRECTIONS[n]
        if beyond is None:
            src = buf.at[part(dd, cells_d, width, False), part(hh, cells_h, width, False)]
        else:
            src = beyond.at[part(-dd, cells_d, width, True), part(-hh, cells_h, width, True)]
        return pltpu.make_async_remote_copy(
            src_ref=src,
            dst_ref=buf.at[part(dd, cells_d, width, True), part(hh, cells_h, width, True)],
            send_sem=halo_s.at[which, n],
            recv_sem=halo_r.at[which, n],
            device_id=around(dd, hh),
            device_id_type=MESH,
        )

    def pooled_copy(row, n):
        dd, hh = DIRECTIONS[n]
        return pltpu.make_async_remote_copy(
            src_ref=pk.at[pl.ds(2 + row, 1), part(hh, 4, 2, False)],
            dst_ref=pk.at[pl.ds(2 - 2 * dd + row, 1), part(hh, 4, 2, True)],
            send_sem=halo_s.at[1 + 3 * row, n],
            recv_sem=halo_r.at[1 + 3 * row, n],
            device_id=around(dd, hh),
            device_id_type=MESH,
        )

    def halo_start(*which):
        for n in range(8):
            halo_copy(which[0], n, *which[1:]).start()

    def halo_wait(*which):
        for n in range(8):
            halo_copy(which[0], n, *which[1:]).wait_send()
        for n in range(8):
            halo_copy(which[0], n, *which[1:]).wait_recv()
        zero_outside(*which[1:5])

    def zero_outside(buf, cells_d, cells_h, width):
        channels = buf.shape[2]
        across = (width, cells_h + 2 * width, channels, 128)
        along = (cells_d + 2 * width, width, channels, 128)

        @pl.when(d == 0)
        def _():
            buf[0:width] = jnp.zeros(across, BF16)

        @pl.when(d == ND - 1)
        def _():
            buf[cells_d + width : cells_d + 2 * width] = jnp.zeros(across, BF16)

        @pl.when(h == 0)
        def _():
            buf[:, 0:width] = jnp.zeros(along, BF16)

        @pl.when(h == NH - 1)
        def _():
            buf[:, cells_h + width : cells_h + 2 * width] = jnp.zeros(along, BF16)

    def scatter_h(src, dst, send, recv, k):
        other = lax.rem(h + k, NH)
        return pltpu.make_async_remote_copy(
            src_ref=src.at[other],
            dst_ref=dst.at[k],
            send_sem=send.at[k],
            recv_sem=recv.at[k],
            device_id=partner(other),
            device_id_type=MESH,
        )

    def share_d(src, dst, send, recv, k):
        return pltpu.make_async_remote_copy(
            src_ref=src,
            dst_ref=dst.at[k],
            send_sem=send.at[k],
            recv_sem=recv.at[k],
            device_id=around(k, 0),
            device_id_type=MESH,
        )

    def gather_send(src, dst, send, recv, k):
        return pltpu.make_async_remote_copy(
            src_ref=src,
            dst_ref=dst.at[h],
            send_sem=send.at[k],
            recv_sem=recv.at[k],
            device_id=partner(lax.rem(h + k, NH)),
            device_id_type=MESH,
        )

    def gather_recv(src, dst, send, recv, k):
        return pltpu.make_async_remote_copy(
            src_ref=src,
            dst_ref=dst.at[lax.rem(h - k + NH, NH)],
            send_sem=send.at[k],
            recv_sem=recv.at[k],
            device_id=partner(lax.rem(h + k, NH)),
            device_id_type=MESH,
        )

    halo_x = (0, xb, 4, 8, 1)
    halo_c = (2, ck, 2, 4, 1)
    halo_g = (3, near, 4, 8, 1, rim)
    halo_start(*halo_x)
    each(1, NH, lambda k: gather_send(f4, bank, ag_s, ag_r, k).start())
    bank[h] = f4[...]

    def dilate():
        at = 2 * lax.broadcasted_iota(jnp.int32, (64, 128), 0)
        to_even = (lanes_iota((64, 128)) == at).astype(F32).astype(BF16)
        for i in range(2):
            for j in range(4):
                wide = lax.dot_general(
                    cot[i, j], to_even, (((0,), (0,)), ((), ())), preferred_element_type=F32
                )
                ck[1 + i, 1 + j] = interleave(wide[:64], wide[64:]).astype(BF16)

    def rows_f3():
        flat = f3[...].astype(F32).reshape(864, 64)
        none = jnp.zeros((288, 64), F32)
        both = jnp.concatenate(
            [jnp.concatenate([flat, none], axis=0), jnp.concatenate([none, flat], axis=0)], axis=1
        )
        a3[...] = jnp.transpose(both).astype(BF16)
        a6[...] = jnp.concatenate(
            [flat[96 * ab : 96 * ab + 96] for ab in range(9)], axis=1
        ).astype(BF16)

    def stack_row(i, j):
        xx[i, j] = stack_width(xb[i, j], 1)

    def stack_x(i):
        for j in range(8):
            stack_row(1 + i, 1 + j)

    fetches[3].wait()
    stage("dilate", dilate)
    halo_start(*halo_c)
    fetches[2].wait()
    stage("rows_f3", rows_f3)
    stage("stack_x", lambda: each(0, 4, stack_x))
    d3[0] = jnp.zeros((10, 64, 128), BF16)
    d3[5] = jnp.zeros((10, 64, 128), BF16)
    d3[:, 0] = jnp.zeros((6, 64, 128), BF16)
    d3[:, 9] = jnp.zeros((6, 64, 128), BF16)
    halo_wait(*halo_x)

    def stack_rim():
        for j in range(10):
            stack_row(0, j)
            stack_row(5, j)
        for i in range(4):
            stack_row(1 + i, 0)
            stack_row(1 + i, 9)

    stage("stack_rim", stack_rim)

    def forward3(i):
        for j in range(4):
            cols = [
                jnp.concatenate(
                    [xx[2 * i + a, 2 * j + s + b] for a in range(4) for b in range(3)], axis=0
                )
                for s in range(2)
            ]
            act = jnp.dot(a3[...], jnp.concatenate(cols, axis=1), preferred_element_type=F32)
            value, slope = gelu_parts(act)
            for di in range(2):
                for s in range(2):
                    slope3[2 * i + di, 2 * j + s] = slope[
                        64 * di : 64 * di + 64, 128 * s : 128 * s + 128
                    ]
            total = value[:64] + value[64:]
            total = total[:, :128] + total[:, 128:]
            total = (total + pltpu.roll(total, 127, 1)) * 0.125
            pk[2 + i, 2 + j] = interleave(total[:32], total[32:]).astype(BF16)

    def forward_and_send(i):
        forward3(i)
        for n in range(8):
            pooled_copy(i, n).start()

    stage("forward3", lambda: [forward_and_send(n) for n in range(0, 2)])

    def wait_gather(k):
        gather_send(f4, bank, ag_s, ag_r, k).wait_send()
        gather_recv(f4, bank, ag_s, ag_r, k).wait_recv()

    each(1, NH, wait_gather)

    def arrange():
        wide = [bank[s].astype(F32) for s in range(NH)]
        low = jnp.concatenate([w[:8] for w in wide], axis=0)
        high = jnp.concatenate([w[8:] for w in wide], axis=0)
        a4[...] = jnp.concatenate([low, high], axis=1).astype(BF16)
        for ab in range(9):
            a5[:, 128 * ab : 128 * ab + 128] = jnp.transpose(
                a4[:, 192 * ab : 192 * ab + 192].astype(F32)
            ).astype(BF16)

    stage("arrange", arrange)
    halo_wait(*halo_c)
    for row in range(2):
        for n in range(8):
            pooled_copy(row, n).wait_send()
        for n in range(8):
            pooled_copy(row, n).wait_recv()
    zero_outside(pk, 2, 4, 2)

    def stack_p(i):
        for j in range(8):
            pq[i, j] = stack_width(two_rows(pk[i, j], pk[i + 2, j]), 2)

    stage("stack_p", lambda: [stack_p(n) for n in range(0, 4)])

    def forward4(i):
        for j in range(3):
            cols = [
                jnp.concatenate(
                    [pq[i + a, 2 * j + s + b] for a in range(3) for b in range(3)], axis=0
                )
                for s in range(2)
            ]
            act = jnp.dot(
                a4[:, :1728], jnp.concatenate(cols, axis=1), preferred_element_type=F32
            )
            _, slope = gelu_parts(act)
            for s in range(2):
                col = 2 * j + s
                both = two_rows(ck[i, col], ck[i + 2, col]).astype(F32)
                dq[i, col] = (both * slope[:, 128 * s : 128 * s + 128]).astype(BF16)

    stage("forward4", lambda: [forward4(n) for n in range(0, 2)])

    def pair_rows():
        for j in range(6):
            one, two = dq[0, j], dq[1, j]
            even = lanes_iota(one.shape) % 2 == 0
            dv[0, j] = interleave_odd(one, two)
            dv[1, j] = jnp.where(even, two, one)
            dv[2, j] = interleave(one, two)

    stage("pair_rows", pair_rows)

    def back4(j):
        cols = [
            jnp.concatenate([dv[a, 2 * j + s + 2 - b] for a in range(3) for b in range(3)], axis=0)
            for s in range(2)
        ]
        y = jnp.dot(a5[...], jnp.concatenate(cols, axis=1), preferred_element_type=F32)
        for s in range(2):
            ys = y[:, 128 * s : 128 * s + 128]
            _, from_after = shifted(ys[:64], 2)
            from_before, _ = shifted(ys[128:], 2)
            back = (ys[64:128] + from_after + from_before) * 0.125
            even = lanes_iota(back.shape) % 2 == 0
            spread = [
                jnp.where(even, back, pltpu.roll(back, 1, 1)),
                jnp.where(even, pltpu.roll(back, 127, 1), back),
            ]
            for i in range(2):
                for di in range(2):
                    for dj in range(2):
                        row, col = 2 * i + di, 2 * (2 * j + s) + dj
                        delta = (spread[i] * slope3[row, col]).astype(BF16)
                        before, after = shifted(delta, 1)
                        dd3[row, col] = jnp.concatenate([after, delta, before], axis=0)
                        d3[1 + row, 1 + col] = delta

    stage("back4", lambda: [back4(n) for n in range(0, 2)])

    f3acc[...] = jnp.zeros(f3acc.shape, F32)

    def weight3(i):
        left = jnp.concatenate(
            [
                jnp.concatenate([xb[i + a, j + b] for j in range(8)], axis=1)
                for a in range(3)
                for b in range(3)
            ],
            axis=0,
        )
        right = jnp.concatenate([dd3[i, j] for j in range(8)], axis=1)
        f3acc[...] += lax.dot_general(
            left, right, (((1,), (1,)), ((), ())), preferred_element_type=F32
        )

    stage("weight3", lambda: [weight3(n) for n in range(0, 4)])

    def pack3():
        last = f3acc[:, 128:]
        flat = jnp.concatenate(
            [
                f3acc[:, :128],
                jnp.concatenate([last[:144], last[144:]], axis=1),
                jnp.zeros((80, 128), F32),
            ],
            axis=0,
        ).astype(BF16)
        for c in range(16):
            r3[c] = flat[32 * c : 32 * c + 32]

    stage("pack3", pack3)
    def scatter3(k):
        @pl.when(lax.rem(h + k, NH) < FILLED)
        def _():
            scatter_h(r3, q3, s3_s, s3_r, k).start()

    for k in (8, 9, 7, 10, 6, 11, 5, 12, 4, 13, 3, 14, 2, 15, 1):
        scatter3(k)

    cells4 = [(i, j) for i in range(2) for j in range(4)]

    def weight4():
        even = lanes_iota((128, 128)) % 2 == 0
        left = jnp.concatenate(
            [
                jnp.where(even if i == 0 else ~even, dq[1 - i, 1 + j], jnp.zeros((), BF16))
                for i, j in cells4
            ],
            axis=1,
        )
        for g in range(5):
            taps = [ab for ab in (2 * g, 2 * g + 1) if ab < 9]
            right = jnp.concatenate(
                [
                    jnp.concatenate(
                        [pq[ab // 3 + 1 - i, j + ab % 3 + 1] for i, j in cells4], axis=1
                    )
                    for ab in taps
                ],
                axis=0,
            )
            piece = lax.dot_general(
                left, right, (((1,), (1,)), ((), ())), preferred_element_type=F32
            )
            if len(taps) == 1:
                piece = jnp.concatenate([piece, jnp.zeros((128, 64), F32)], axis=1)
            f4acc[:, 384 * g : 384 * g + piece.shape[1]] = piece

    stage("weight4", weight4)

    def pack4(s):
        rows = pl.ds(pl.multiple_of(8 * s, 8), 8)
        r4[lax.rem(s, 2), s // 2] = jnp.concatenate(
            [f4acc[rows, :896], f4acc[rows, 896:]], axis=0
        ).astype(BF16)

    stage("pack4", lambda: each(0, NH, pack4))
    core = lax.rem(h, 2)
    pair = h // 2

    def swap4():
        return pltpu.make_async_remote_copy(
            src_ref=r4.at[1 - core],
            dst_ref=q40,
            send_sem=s40_s,
            recv_sem=s40_r,
            device_id=(d, h + 1 - 2 * core),
            device_id_type=MESH,
        )

    def scatter4(k):
        other = lax.rem(pair + k, NH // 2)
        return pltpu.make_async_remote_copy(
            src_ref=r4b.at[other],
            dst_ref=q4.at[k],
            send_sem=s4_s.at[k],
            recv_sem=s4_r.at[k],
            device_id=partner(2 * other + core),
            device_id_type=MESH,
        )

    swap4().start()

    def gather_width(y, s):
        ys = y[:, 128 * s : 128 * s + 128]
        _, from_after = shifted(ys[:32], 1)
        from_before, _ = shifted(ys[64:], 1)
        return ys[32:64] + from_after + from_before

    def back_rim():
        for j in range(5):
            for a, row in ((0, 0), (2, 5)):
                source = 1 if row == 0 else 4
                cols = [
                    jnp.concatenate(
                        [
                            d3[source, 2 * j + s + 1 - b]
                            if 0 <= 2 * j + s + 1 - b <= 9
                            else jnp.zeros((64, 128), BF16)
                            for b in range(3)
                        ],
                        axis=0,
                    )
                    for s in range(2)
                ]
                y = jnp.dot(
                    a6[:, 192 * a : 192 * a + 192],
                    jnp.concatenate(cols, axis=1),
                    preferred_element_type=F32,
                )
                for s in range(2):
                    rim[row, 2 * j + s] = gather_width(y, s).astype(BF16)
        for b, col, source in ((0, 0, 1), (2, 9, 8)):
            weights = jnp.concatenate(
                [a6[:, 192 * a + 64 * b : 192 * a + 64 * b + 64] for a in range(3)], axis=1
            )
            for i in range(2):
                cols = [
                    jnp.concatenate([d3[2 * i + s + 2 - a, source] for a in range(3)], axis=0)
                    for s in range(2)
                ]
                y = jnp.dot(weights, jnp.concatenate(cols, axis=1), preferred_element_type=F32)
                for s in range(2):
                    rim[1 + 2 * i + s, col] = gather_width(y, s).astype(BF16)

    stage("back_rim", back_rim)
    halo_start(*halo_g)

    def wait_both(copy):
        copy.wait_send()
        copy.wait_recv()

    wait_both(swap4())

    def add4():
        for m in range(8):
            r4b[m] = (r4[core, m].astype(F32) + q40[m].astype(F32)).astype(BF16)

    stage("add4", add4)
    each(1, NH // 2, lambda k: scatter4(k).start())

    def back3(i):
        for j in range(4):
            cols = [
                jnp.concatenate(
                    [d3[i + 2 - a, 2 * j + s + 2 - b] for a in range(3) for b in range(3)], axis=0
                )
                for s in range(2)
            ]
            y = jnp.dot(a6[...], jnp.concatenate(cols, axis=1), preferred_element_type=F32)
            for s in range(2):
                gown[i, 2 * j + s] = gather_width(y, s)

    stage("back3a", lambda: [back3(n) for n in range(0, 2)])

    def wait_3(k):
        @pl.when(lax.rem(h + k, NH) < FILLED)
        def _():
            scatter_h(r3, q3, s3_s, s3_r, k).wait_send()

    for k in range(1, NH):
        wait_3(k)

    @pl.when(h < FILLED)
    def _():
        for k in range(1, NH):
            scatter_h(r3, q3, s3_s, s3_r, k).wait_recv()

    def sum3():
        total3 = r3[h].astype(F32)
        for k in range(1, NH):
            total3 = total3 + q3[k].astype(F32)
        t3[...] = jnp.where(h < FILLED, total3, 0.0).astype(BF16)

    stage("sum3", sum3)
    for k in range(1, ND):
        share_d(t3, q3b, b3_s, b3_r, k).start()
    stage("back3b", lambda: [back3(n) for n in range(2, 4)])

    for k in range(1, ND):
        wait_both(share_d(t3, q3b, b3_s, b3_r, k))
    whole3 = t3[...].astype(F32)
    for k in range(1, ND):
        whole3 = whole3 + q3b[k].astype(F32)
    v3[h] = (whole3 * (1.0 / math.sqrt(32 * 128 * 128))).astype(BF16)
    @pl.when(h < FILLED)
    def _():
        for k in (8, 9, 7, 10, 6, 11, 5, 12, 4, 13, 3, 14, 2, 15, 1):
            gather_send(v3.at[h], v3, c3_s, c3_r, k).start()

    each(1, NH // 2, lambda k: wait_both(scatter4(k)))

    def sum4():
        total4 = r4b[pair].astype(F32)
        for k in range(1, NH // 2):
            total4 = total4 + q4[k].astype(F32)
        t4[...] = total4.astype(BF16)

    stage("sum4", sum4)
    each(1, ND, lambda k: share_d(t4, q4b, b4_s, b4_r, k).start())

    halo_wait(*halo_g)

    def finish_gv():
        for i in range(4):
            done = []
            for j in range(8):
                total = gown[i, j]
                if i in (0, 3):
                    total = total + near[0 if i == 0 else 5, 1 + j].astype(F32)
                if j in (0, 7):
                    total = total + near[1 + i, 0 if j == 0 else 9].astype(F32)
                if i in (0, 3) and j in (0, 7):
                    total = total + near[0 if i == 0 else 5, 0 if j == 0 else 9].astype(F32)
                done.append(total)
            gv_out[:, i] = jnp.transpose(jnp.stack(done, axis=0), (1, 0, 2)).astype(BF16)

    stage("finish_gv", finish_gv)

    each(1, ND, lambda k: wait_both(share_d(t4, q4b, b4_s, b4_r, k)))
    whole4 = t4[...].astype(F32)
    for k in range(1, ND):
        whole4 = whole4 + q4b[k].astype(F32)
    whole4 = whole4 * (1.0 / math.sqrt(16 * 64 * 64))
    for t in range(27):
        rows, lane = 8 * (t // 14), 64 * (t % 14)
        g4_out[t] = whole4[rows : rows + 8, lane : lane + 64]

    def wait_c3(k):
        @pl.when(lax.rem(h - k + NH, NH) < FILLED)
        def _():
            gather_recv(v3.at[h], v3, c3_s, c3_r, k).wait_recv()

    for k in range(1, NH):
        wait_c3(k)

    @pl.when(h < FILLED)
    def _():
        for k in range(1, NH):
            gather_send(v3.at[h], v3, c3_s, c3_r, k).wait_send()

    flat3 = jnp.concatenate([v3[c].astype(F32) for c in range(14)], axis=0)
    last3 = jnp.concatenate([flat3[288:432, :64], flat3[288:432, 64:]], axis=0)
    for ab in range(9):
        rows = slice(32 * ab, 32 * ab + 32)
        g3_out[3 * ab] = flat3[rows, :64]
        g3_out[3 * ab + 1] = flat3[rows, 64:]
        g3_out[3 * ab + 2] = last3[rows]


def writer(gv, g3, g4, gv_hbm, g3_hbm, g4_hbm, sems):
    copies = [
        pltpu.make_async_copy(src, dst, sems.at[n])
        for n, (src, dst) in enumerate([(gv, gv_hbm), (g3, g3_hbm), (g4, g4_hbm)])
    ]
    for copy in copies:
        copy.start()
    for copy in copies:
        copy.wait()


def shards(volume, filters_three, filters_four, cotangent):
    vmem = pl.BlockSpec(memory_space=pltpu.VMEM)
    hbm = pl.BlockSpec(memory_space=pl.ANY)
    dma = pltpu.SemaphoreType.DMA
    gv, g3, g4 = pl.pallas_call(
        kernel,
        out_shape=(
            pltpu.VMEM((32, 4, 8, 128), BF16),
            pltpu.VMEM((27, 32, 64), F32),
            pltpu.VMEM((27, 8, 64), F32),
        ),
        in_specs=[hbm] * 4,
        out_specs=(vmem,) * 3,
        scratch_shapes=[
            pltpu.VMEM((32, 4, 8, 128), BF16),
            pltpu.VMEM((27, 32, 64), BF16),
            pltpu.VMEM((27, 8, 64), BF16),
            pltpu.VMEM((2, 4, 64, 128), BF16),
            pltpu.VMEM((16, 896), BF16),
            pltpu.VMEM((128, 1152), BF16),
            pltpu.VMEM((96, 576), BF16),
            pltpu.VMEM((6, 10, 32, 128), BF16),
            pltpu.VMEM((6, 10, 96, 128), BF16),
            pltpu.VMEM((4, 8, 64, 128), F32),
            pltpu.VMEM((4, 6, 64, 128), BF16),
            pltpu.VMEM((6, 8, 32, 128), BF16),
            pltpu.VMEM((4, 8, 192, 128), BF16),
            pltpu.VMEM((2, 6, 128, 128), BF16),
            pltpu.VMEM((3, 6, 128, 128), BF16),
            pltpu.VMEM((6, 10, 64, 128), BF16),
            pltpu.VMEM((4, 8, 192, 128), BF16),
            pltpu.VMEM((6, 10, 32, 128), BF16),
            pltpu.VMEM((6, 10, 32, 128), BF16),
            pltpu.VMEM((4, 8, 32, 128), F32),
            pltpu.VMEM((16, 16, 896), BF16),
            pltpu.VMEM((128, 1792), BF16),
            pltpu.VMEM((192, 1152), BF16),
            pltpu.VMEM((128, 1792), F32),
            pltpu.VMEM((2, 8, 16, 896), BF16),
            pltpu.VMEM((8, 16, 896), BF16),
            pltpu.VMEM((8, 16, 896), BF16),
            pltpu.VMEM((8, 16, 896), BF16),
            pltpu.VMEM((16, 896), BF16),
            pltpu.VMEM((8, 16, 896), BF16),
            pltpu.VMEM((288, 192), F32),
            pltpu.VMEM((16, 32, 128), BF16),
            pltpu.VMEM((16, 32, 128), BF16),
            pltpu.VMEM((32, 128), BF16),
            pltpu.VMEM((8, 32, 128), BF16),
            pltpu.VMEM((16, 32, 128), BF16),
            dma((4,)),
            dma((5, 8)),
            dma((5, 8)),
            dma,
            dma,
            dma((16,)),
            dma((16,)),
            dma((16,)),
            dma((16,)),
            dma((8,)),
            dma((8,)),
            dma((16,)),
            dma((16,)),
            dma((8,)),
            dma((8,)),
            dma((16,)),
            dma((16,)),
        ],
        compiler_params=pltpu.CompilerParams(
            collective_id=0, has_side_effects=True, vmem_limit_bytes=58000 * 1024
        ),
    )(
        volume,
        jnp.transpose(filters_three, (0, 2, 1)),
        filters_four,
        jnp.transpose(cotangent, (1, 2, 3, 0)),
    )
    gv, g3, g4 = pl.pallas_call(
        writer,
        out_shape=(
            pltpu.HBM((32, 4, 8, 128), BF16),
            pltpu.HBM((27, 32, 64), F32),
            pltpu.HBM((27, 8, 64), F32),
        ),
        in_specs=[hbm] * 3,
        out_specs=(hbm,) * 3,
        scratch_shapes=[dma((3,))],
        compiler_params=pltpu.CompilerParams(vmem_limit_bytes=1024 * 1024),
    )(gv, g3, g4)
    return (gv, jnp.transpose(g3, (0, 2, 1)), g4)


def solution(mesh):
    in_specs = (
        P(None, "depth", "height", None),
        P(),
        P(None, "height", None),
        P(None, "depth", "height", None),
    )
    out_specs = (P(None, "depth", "height", None), P(), P(None, "height", None))
    return jax.shard_map(shards, mesh=mesh, in_specs=in_specs, out_specs=out_specs, check_vma=False)
```

```python
import functools
import math

import jax
import jax.numpy as jnp
from jax import lax
from jax.experimental import pallas as pl
from jax.experimental.pallas import tpu as pltpu
from jax.sharding import PartitionSpec as P

TANH_SCALE = 0.7978845608028654
CUBIC_TERM = 0.044715
MESH = pl.DeviceIdType.MESH
F32 = jnp.float32
BF16 = jnp.bfloat16

ND = 8
NH = 16
DIRECTIONS = [(dd, hh) for dd in (-1, 0, 1) for hh in (-1, 0, 1) if (dd, hh) != (0, 0)]


def gelu_parts(v):
    u = v * v
    inner = jnp.tanh(v * (TANH_SCALE + TANH_SCALE * CUBIC_TERM * u))
    half = 0.5 + 0.5 * inner
    value = v * half
    slope = half + value * (1.0 - inner) * (TANH_SCALE + 3.0 * TANH_SCALE * CUBIC_TERM * u)
    return value, slope


def stage(name, body):
    body()


def lanes_iota(shape):
    return lax.broadcasted_iota(jnp.int32, shape, len(shape) - 1)


def shifted(v, step):
    lane = lanes_iota(v.shape)
    zero = jnp.zeros((), v.dtype)
    before = jnp.where(lane < step, zero, pltpu.roll(v, step, 1))
    after = jnp.where(lane >= 128 - step, zero, pltpu.roll(v, 128 - step, 1))
    return before, after


def stack_width(row, step):
    before, after = shifted(row, step)
    return jnp.concatenate([before, row, after], axis=0)


def part(at, cells, width, far):
    if at == 0:
        return pl.ds(width, cells)
    if at < 0:
        return pl.ds(cells + width, width) if far else pl.ds(width, width)
    return pl.ds(0, width) if far else pl.ds(cells, width)


def interleave(even_row, odd_row):
    even = lanes_iota(even_row.shape) % 2 == 0
    return jnp.where(even, even_row, pltpu.roll(odd_row, 1, 1))


def interleave_odd(even_row, odd_row):
    even = lanes_iota(even_row.shape) % 2 == 0
    return jnp.where(even, pltpu.roll(even_row, 127, 1), odd_row)


def two_rows(first, second):
    return jnp.concatenate([interleave(first, second), interleave_odd(first, second)], axis=0)


def kernel(
    x_hbm, f3_hbm, f4_hbm, cot_hbm,
    gv_out, g3_out, g4_out,
    x_in, f3, f4_in, cot, f4, a3, a6,
    xb, xx, slope3, ck, pk, pq, dq, dv, d3, dd3, rim, near, gown, bank, a4, a5,
    f4acc, r4, q40, r4b, q4, t4, q4b,
    f3acc, r3, q3, t3, q3b, v3,
    in_sem, halo_s, halo_r, s40_s, s40_r, ag_s, ag_r, s4_s, s4_r, b4_s, b4_r, s3_s, s3_r, b3_s, b3_r, c3_s, c3_r,
):
    d = lax.axis_index("depth")
    h = lax.axis_index("height")

    def around(dd, hh):
        return (lax.rem(d + dd + ND, ND), lax.rem(h + hh + NH, NH))

    def partner(other):
        flip = lax.rem(lax.rem(h, 4) // 2 + lax.rem(other, 4) // 2, 2)
        return (d + flip * (1 - 2 * lax.rem(d, 2)), other)

    def each(low, high, body):
        def step(k, carry):
            body(k)
            return carry

        lax.fori_loop(low, high, step, 0)

    barrier = pltpu.get_barrier_semaphore()

    def greet(device):
        pl.semaphore_signal(barrier, inc=1, device_id=device, device_id_type=MESH)

    for dd, hh in DIRECTIONS:
        greet(around(dd, hh))
    for k in range(1, NH):
        greet(partner(lax.rem(h + k, NH)))
    for k in range(2, ND - 1):
        greet(around(k, 0))

    fetches = [
        pltpu.make_async_copy(src, dst, in_sem.at[n])
        for n, (src, dst) in enumerate(
            [(x_hbm, x_in), (f4_hbm, f4_in), (f3_hbm, f3), (cot_hbm, cot)]
        )
    ]
    for fetch in fetches:
        fetch.start()

    def rows_x():
        for i in range(4):
            block = jnp.transpose(x_in[:, i].astype(F32), (1, 0, 2)).astype(BF16)
            for j in range(8):
                xb[1 + i, 1 + j] = block[j]

    fetches[0].wait()
    stage("rows_x", rows_x)

    def rows_f4():
        taps = [f4_in[t].astype(F32) for t in range(27)] + [jnp.zeros((8, 64), F32)]
        tiles = [jnp.concatenate([taps[2 * m], taps[2 * m + 1]], axis=1) for m in range(14)]
        f4[...] = jnp.concatenate(
            [jnp.concatenate(tiles[:7], axis=1), jnp.concatenate(tiles[7:], axis=1)], axis=0
        ).astype(BF16)

    fetches[1].wait()
    stage("rows_f4", rows_f4)
    pl.semaphore_wait(barrier, 8 + NH - 1 + ND - 3)

    def halo_copy(which, n, buf, cells_d, cells_h, width, beyond=None):
        dd, hh = DIRECTIONS[n]
        if beyond is None:
            src = buf.at[part(dd, cells_d, width, False), part(hh, cells_h, width, False)]
        else:
            src = beyond.at[part(-dd, cells_d, width, True), part(-hh, cells_h, width, True)]
        return pltpu.make_async_remote_copy(
            src_ref=src,
            dst_ref=buf.at[part(dd, cells_d, width, True), part(hh, cells_h, width, True)],
            send_sem=halo_s.at[which, n],
            recv_sem=halo_r.at[which, n],
            device_id=around(dd, hh),
            device_id_type=MESH,
        )

    def pooled_copy(row, n):
        dd, hh = DIRECTIONS[n]
        return pltpu.make_async_remote_copy(
            src_ref=pk.at[pl.ds(2 + row, 1), part(hh, 4, 2, False)],
            dst_ref=pk.at[pl.ds(2 - 2 * dd + row, 1), part(hh, 4, 2, True)],
            send_sem=halo_s.at[1 + 3 * row, n],
            recv_sem=halo_r.at[1 + 3 * row, n],
            device_id=around(dd, hh),
            device_id_type=MESH,
        )

    def halo_start(*which):
        for n in range(8):
            halo_copy(which[0], n, *which[1:]).start()

    def halo_wait(*which):
        for n in range(8):
            halo_copy(which[0], n, *which[1:]).wait_send()
        for n in range(8):
            halo_copy(which[0], n, *which[1:]).wait_recv()
        zero_outside(*which[1:5])

    def zero_outside(buf, cells_d, cells_h, width):
        channels = buf.shape[2]
        across = (width, cells_h + 2 * width, channels, 128)
        along = (cells_d + 2 * width, width, channels, 128)

        @pl.when(d == 0)
        def _():
            buf[0:width] = jnp.zeros(across, BF16)

        @pl.when(d == ND - 1)
        def _():
            buf[cells_d + width : cells_d + 2 * width] = jnp.zeros(across, BF16)

        @pl.when(h == 0)
        def _():
            buf[:, 0:width] = jnp.zeros(along, BF16)

        @pl.when(h == NH - 1)
        def _():
            buf[:, cells_h + width : cells_h + 2 * width] = jnp.zeros(along, BF16)

    def scatter_h(src, dst, send, recv, k):
        other = lax.rem(h + k, NH)
        return pltpu.make_async_remote_copy(
            src_ref=src.at[other],
            dst_ref=dst.at[k],
            send_sem=send.at[k],
            recv_sem=recv.at[k],
            device_id=partner(other),
            device_id_type=MESH,
        )

    def share_d(src, dst, send, recv, k):
        return pltpu.make_async_remote_copy(
            src_ref=src,
            dst_ref=dst.at[k],
            send_sem=send.at[k],
            recv_sem=recv.at[k],
            device_id=around(k, 0),
            device_id_type=MESH,
        )

    def gather_send(src, dst, send, recv, k):
        return pltpu.make_async_remote_copy(
            src_ref=src,
            dst_ref=dst.at[h],
            send_sem=send.at[k],
            recv_sem=recv.at[k],
            device_id=partner(lax.rem(h + k, NH)),
            device_id_type=MESH,
        )

    def gather_recv(src, dst, send, recv, k):
        return pltpu.make_async_remote_copy(
            src_ref=src,
            dst_ref=dst.at[lax.rem(h - k + NH, NH)],
            send_sem=send.at[k],
            recv_sem=recv.at[k],
            device_id=partner(lax.rem(h + k, NH)),
            device_id_type=MESH,
        )

    halo_x = (0, xb, 4, 8, 1)
    halo_c = (2, ck, 2, 4, 1)
    halo_g = (3, near, 4, 8, 1, rim)
    halo_start(*halo_x)
    each(1, NH, lambda k: gather_send(f4, bank, ag_s, ag_r, k).start())
    bank[h] = f4[...]

    def dilate():
        at = 2 * lax.broadcasted_iota(jnp.int32, (64, 128), 0)
        to_even = (lanes_iota((64, 128)) == at).astype(F32).astype(BF16)
        for i in range(2):
            for j in range(4):
                wide = lax.dot_general(
                    cot[i, j], to_even, (((0,), (0,)), ((), ())), preferred_element_type=F32
                )
                ck[1 + i, 1 + j] = interleave(wide[:64], wide[64:]).astype(BF16)

    def rows_f3():
        flat = f3[...].astype(F32).reshape(864, 64)
        none = jnp.zeros((288, 64), F32)
        both = jnp.concatenate(
            [jnp.concatenate([flat, none], axis=0), jnp.concatenate([none, flat], axis=0)], axis=1
        )
        a3[...] = jnp.transpose(both).astype(BF16)
        a6[...] = jnp.concatenate(
            [flat[96 * ab : 96 * ab + 96] for ab in range(9)], axis=1
        ).astype(BF16)

    def stack_row(i, j):
        xx[i, j] = stack_width(xb[i, j], 1)

    def stack_x(i):
        for j in range(8):
            stack_row(1 + i, 1 + j)

    fetches[3].wait()
    stage("dilate", dilate)
    halo_start(*halo_c)
    fetches[2].wait()
    stage("rows_f3", rows_f3)
    stage("stack_x", lambda: [stack_x(i) for i in range(4)])
    d3[0] = jnp.zeros((10, 64, 128), BF16)
    d3[5] = jnp.zeros((10, 64, 128), BF16)
    d3[:, 0] = jnp.zeros((6, 64, 128), BF16)
    d3[:, 9] = jnp.zeros((6, 64, 128), BF16)
    halo_wait(*halo_x)

    def stack_rim():
        for j in range(10):
            stack_row(0, j)
            stack_row(5, j)
        for i in range(4):
            stack_row(1 + i, 0)
            stack_row(1 + i, 9)

    stage("stack_rim", stack_rim)

    def forward3(i):
        for j in range(4):
            cols = [
                jnp.concatenate(
                    [xx[2 * i + a, 2 * j + s + b] for a in range(4) for b in range(3)], axis=0
                )
                for s in range(2)
            ]
            act = jnp.dot(a3[...], jnp.concatenate(cols, axis=1), preferred_element_type=F32)
            value, slope = gelu_parts(act)
            for di in range(2):
                for s in range(2):
                    slope3[2 * i + di, 2 * j + s] = slope[
                        64 * di : 64 * di + 64, 128 * s : 128 * s + 128
                    ]
            total = value[:64] + value[64:]
            total = total[:, :128] + total[:, 128:]
            total = (total + pltpu.roll(total, 127, 1)) * 0.125
            pk[2 + i, 2 + j] = interleave(total[:32], total[32:]).astype(BF16)

    def forward_and_send(i):
        forward3(i)
        for n in range(8):
            pooled_copy(i, n).start()

    stage("forward3", lambda: [forward_and_send(n) for n in range(0, 2)])

    def wait_gather(k):
        gather_send(f4, bank, ag_s, ag_r, k).wait_send()
        gather_recv(f4, bank, ag_s, ag_r, k).wait_recv()

    each(1, NH, wait_gather)

    def arrange():
        wide = [bank[s].astype(F32) for s in range(NH)]
        low = jnp.concatenate([w[:8] for w in wide], axis=0)
        high = jnp.concatenate([w[8:] for w in wide], axis=0)
        a4[...] = jnp.concatenate([low, high], axis=1).astype(BF16)
        for ab in range(9):
            a5[:, 128 * ab : 128 * ab + 128] = jnp.transpose(
                a4[:, 192 * ab : 192 * ab + 192].astype(F32)
            ).astype(BF16)

    stage("arrange", arrange)
    halo_wait(*halo_c)
    for row in range(2):
        for n in range(8):
            pooled_copy(row, n).wait_send()
        for n in range(8):
            pooled_copy(row, n).wait_recv()
    zero_outside(pk, 2, 4, 2)

    def stack_p(i):
        for j in range(8):
            pq[i, j] = stack_width(two_rows(pk[i, j], pk[i + 2, j]), 2)

    stage("stack_p", lambda: [stack_p(n) for n in range(0, 4)])

    def forward4(i):
        for j in range(3):
            cols = [
                jnp.concatenate(
                    [pq[i + a, 2 * j + s + b] for a in range(3) for b in range(3)], axis=0
                )
                for s in range(2)
            ]
            act = jnp.dot(
                a4[:, :1728], jnp.concatenate(cols, axis=1), preferred_element_type=F32
            )
            _, slope = gelu_parts(act)
            for s in range(2):
                col = 2 * j + s
                both = two_rows(ck[i, col], ck[i + 2, col]).astype(F32)
                dq[i, col] = (both * slope[:, 128 * s : 128 * s + 128]).astype(BF16)

    stage("forward4", lambda: [forward4(n) for n in range(0, 2)])

    def pair_rows():
        for j in range(6):
            one, two = dq[0, j], dq[1, j]
            even = lanes_iota(one.shape) % 2 == 0
            dv[0, j] = interleave_odd(one, two)
            dv[1, j] = jnp.where(even, two, one)
            dv[2, j] = interleave(one, two)

    stage("pair_rows", pair_rows)

    def back4(j):
        cols = [
            jnp.concatenate([dv[a, 2 * j + s + 2 - b] for a in range(3) for b in range(3)], axis=0)
            for s in range(2)
        ]
        y = jnp.dot(a5[...], jnp.concatenate(cols, axis=1), preferred_element_type=F32)
        for s in range(2):
            ys = y[:, 128 * s : 128 * s + 128]
            _, from_after = shifted(ys[:64], 2)
            from_before, _ = shifted(ys[128:], 2)
            back = (ys[64:128] + from_after + from_before) * 0.125
            even = lanes_iota(back.shape) % 2 == 0
            spread = [
                jnp.where(even, back, pltpu.roll(back, 1, 1)),
                jnp.where(even, pltpu.roll(back, 127, 1), back),
            ]
            for i in range(2):
                for di in range(2):
                    for dj in range(2):
                        row, col = 2 * i + di, 2 * (2 * j + s) + dj
                        delta = (spread[i] * slope3[row, col]).astype(BF16)
                        before, after = shifted(delta, 1)
                        dd3[row, col] = jnp.concatenate([after, delta, before], axis=0)
                        d3[1 + row, 1 + col] = delta

    stage("back4", lambda: [back4(n) for n in range(0, 2)])

    f3acc[...] = jnp.zeros(f3acc.shape, F32)

    def weight3(i):
        left = jnp.concatenate(
            [
                jnp.concatenate([xb[i + a, j + b] for j in range(8)], axis=1)
                for a in range(3)
                for b in range(3)
            ],
            axis=0,
        )
        right = jnp.concatenate([dd3[i, j] for j in range(8)], axis=1)
        f3acc[...] += lax.dot_general(
            left, right, (((1,), (1,)), ((), ())), preferred_element_type=F32
        )

    stage("weight3", lambda: [weight3(n) for n in range(0, 4)])

    def pack3():
        last = f3acc[:, 128:]
        flat = jnp.concatenate(
            [
                f3acc[:, :128],
                jnp.concatenate([last[:144], last[144:]], axis=1),
                jnp.zeros((80, 128), F32),
            ],
            axis=0,
        ).astype(BF16)
        for c in range(16):
            r3[c] = flat[32 * c : 32 * c + 32]

    stage("pack3", pack3)
    for k in range(1, NH):
        scatter_h(r3, q3, s3_s, s3_r, k).start()

    cells4 = [(i, j) for i in range(2) for j in range(4)]

    def weight4():
        even = lanes_iota((128, 128)) % 2 == 0
        left = jnp.concatenate(
            [
                jnp.where(even if i == 0 else ~even, dq[1 - i, 1 + j], jnp.zeros((), BF16))
                for i, j in cells4
            ],
            axis=1,
        )
        for g in range(5):
            taps = [ab for ab in (2 * g, 2 * g + 1) if ab < 9]
            right = jnp.concatenate(
                [
                    jnp.concatenate(
                        [pq[ab // 3 + 1 - i, j + ab % 3 + 1] for i, j in cells4], axis=1
                    )
                    for ab in taps
                ],
                axis=0,
            )
            piece = lax.dot_general(
                left, right, (((1,), (1,)), ((), ())), preferred_element_type=F32
            )
            if len(taps) == 1:
                piece = jnp.concatenate([piece, jnp.zeros((128, 64), F32)], axis=1)
            f4acc[:, 384 * g : 384 * g + piece.shape[1]] = piece

    stage("weight4", weight4)

    def pack4(s):
        rows = slice(8 * s, 8 * s + 8)
        r4[s % 2, s // 2] = jnp.concatenate(
            [f4acc[rows, :896], f4acc[rows, 896:]], axis=0
        ).astype(BF16)

    stage("pack4", lambda: [pack4(s) for s in range(NH)])
    core = lax.rem(h, 2)
    pair = h // 2

    def swap4():
        return pltpu.make_async_remote_copy(
            src_ref=r4.at[1 - core],
            dst_ref=q40,
            send_sem=s40_s,
            recv_sem=s40_r,
            device_id=(d, h + 1 - 2 * core),
            device_id_type=MESH,
        )

    def scatter4(k):
        other = lax.rem(pair + k, NH // 2)
        return pltpu.make_async_remote_copy(
            src_ref=r4b.at[other],
            dst_ref=q4.at[k],
            send_sem=s4_s.at[k],
            recv_sem=s4_r.at[k],
            device_id=partner(2 * other + core),
            device_id_type=MESH,
        )

    swap4().start()

    def gather_width(y, s):
        ys = y[:, 128 * s : 128 * s + 128]
        _, from_after = shifted(ys[:32], 1)
        from_before, _ = shifted(ys[64:], 1)
        return ys[32:64] + from_after + from_before

    def back_rim():
        for j in range(5):
            for a, row in ((0, 0), (2, 5)):
                source = 1 if row == 0 else 4
                cols = [
                    jnp.concatenate(
                        [
                            d3[source, 2 * j + s + 1 - b]
                            if 0 <= 2 * j + s + 1 - b <= 9
                            else jnp.zeros((64, 128), BF16)
                            for b in range(3)
                        ],
                        axis=0,
                    )
                    for s in range(2)
                ]
                y = jnp.dot(
                    a6[:, 192 * a : 192 * a + 192],
                    jnp.concatenate(cols, axis=1),
                    preferred_element_type=F32,
                )
                for s in range(2):
                    rim[row, 2 * j + s] = gather_width(y, s).astype(BF16)
        for b, col, source in ((0, 0, 1), (2, 9, 8)):
            weights = jnp.concatenate(
                [a6[:, 192 * a + 64 * b : 192 * a + 64 * b + 64] for a in range(3)], axis=1
            )
            for i in range(2):
                cols = [
                    jnp.concatenate([d3[2 * i + s + 2 - a, source] for a in range(3)], axis=0)
                    for s in range(2)
                ]
                y = jnp.dot(weights, jnp.concatenate(cols, axis=1), preferred_element_type=F32)
                for s in range(2):
                    rim[1 + 2 * i + s, col] = gather_width(y, s).astype(BF16)

    stage("back_rim", back_rim)
    halo_start(*halo_g)

    def wait_both(copy):
        copy.wait_send()
        copy.wait_recv()

    wait_both(swap4())

    def add4():
        for m in range(8):
            r4b[m] = (r4[core, m].astype(F32) + q40[m].astype(F32)).astype(BF16)

    stage("add4", add4)
    each(1, NH // 2, lambda k: scatter4(k).start())

    def back3(i):
        for j in range(4):
            cols = [
                jnp.concatenate(
                    [d3[i + 2 - a, 2 * j + s + 2 - b] for a in range(3) for b in range(3)], axis=0
                )
                for s in range(2)
            ]
            y = jnp.dot(a6[...], jnp.concatenate(cols, axis=1), preferred_element_type=F32)
            for s in range(2):
                gown[i, 2 * j + s] = gather_width(y, s)

    stage("back3a", lambda: [back3(n) for n in range(0, 2)])

    for k in range(1, NH):
        wait_both(scatter_h(r3, q3, s3_s, s3_r, k))

    def sum3():
        total3 = r3[h].astype(F32)
        for k in range(1, NH):
            total3 = total3 + q3[k].astype(F32)
        t3[...] = total3.astype(BF16)

    stage("sum3", sum3)
    for k in range(1, ND):
        share_d(t3, q3b, b3_s, b3_r, k).start()
    stage("back3b", lambda: [back3(n) for n in range(2, 4)])

    for k in range(1, ND):
        wait_both(share_d(t3, q3b, b3_s, b3_r, k))
    whole3 = t3[...].astype(F32)
    for k in range(1, ND):
        whole3 = whole3 + q3b[k].astype(F32)
    v3[h] = (whole3 * (1.0 / math.sqrt(32 * 128 * 128))).astype(BF16)
    for k in range(1, NH):
        gather_send(v3.at[h], v3, c3_s, c3_r, k).start()

    each(1, NH // 2, lambda k: wait_both(scatter4(k)))

    def sum4():
        total4 = r4b[pair].astype(F32)
        for k in range(1, NH // 2):
            total4 = total4 + q4[k].astype(F32)
        t4[...] = total4.astype(BF16)

    stage("sum4", sum4)
    each(1, ND, lambda k: share_d(t4, q4b, b4_s, b4_r, k).start())

    halo_wait(*halo_g)

    def finish_gv():
        for i in range(4):
            done = []
            for j in range(8):
                total = gown[i, j]
                if i in (0, 3):
                    total = total + near[0 if i == 0 else 5, 1 + j].astype(F32)
                if j in (0, 7):
                    total = total + near[1 + i, 0 if j == 0 else 9].astype(F32)
                if i in (0, 3) and j in (0, 7):
                    total = total + near[0 if i == 0 else 5, 0 if j == 0 else 9].astype(F32)
                done.append(total)
            gv_out[:, i] = jnp.transpose(jnp.stack(done, axis=0), (1, 0, 2)).astype(BF16)

    stage("finish_gv", finish_gv)

    each(1, ND, lambda k: wait_both(share_d(t4, q4b, b4_s, b4_r, k)))
    whole4 = t4[...].astype(F32)
    for k in range(1, ND):
        whole4 = whole4 + q4b[k].astype(F32)
    whole4 = whole4 * (1.0 / math.sqrt(16 * 64 * 64))
    for t in range(27):
        rows, lane = 8 * (t // 14), 64 * (t % 14)
        g4_out[t] = whole4[rows : rows + 8, lane : lane + 64]

    def wait_c3(k):
        gather_send(v3.at[h], v3, c3_s, c3_r, k).wait_send()
        gather_recv(v3.at[h], v3, c3_s, c3_r, k).wait_recv()

    for k in range(1, NH):
        wait_c3(k)
    flat3 = jnp.concatenate([v3[c].astype(F32) for c in range(14)], axis=0)
    last3 = jnp.concatenate([flat3[288:432, :64], flat3[288:432, 64:]], axis=0)
    for ab in range(9):
        rows = slice(32 * ab, 32 * ab + 32)
        g3_out[3 * ab] = flat3[rows, :64]
        g3_out[3 * ab + 1] = flat3[rows, 64:]
        g3_out[3 * ab + 2] = last3[rows]


def writer(gv, g3, g4, gv_hbm, g3_hbm, g4_hbm, sems):
    copies = [
        pltpu.make_async_copy(src, dst, sems.at[n])
        for n, (src, dst) in enumerate([(gv, gv_hbm), (g3, g3_hbm), (g4, g4_hbm)])
    ]
    for copy in copies:
        copy.start()
    for copy in copies:
        copy.wait()


def shards(volume, filters_three, filters_four, cotangent):
    vmem = pl.BlockSpec(memory_space=pltpu.VMEM)
    hbm = pl.BlockSpec(memory_space=pl.ANY)
    dma = pltpu.SemaphoreType.DMA
    gv, g3, g4 = pl.pallas_call(
        kernel,
        out_shape=(
            pltpu.VMEM((32, 4, 8, 128), BF16),
            pltpu.VMEM((27, 32, 64), F32),
            pltpu.VMEM((27, 8, 64), F32),
        ),
        in_specs=[hbm] * 4,
        out_specs=(vmem,) * 3,
        scratch_shapes=[
            pltpu.VMEM((32, 4, 8, 128), BF16),
            pltpu.VMEM((27, 32, 64), BF16),
            pltpu.VMEM((27, 8, 64), BF16),
            pltpu.VMEM((2, 4, 64, 128), BF16),
            pltpu.VMEM((16, 896), BF16),
            pltpu.VMEM((128, 1152), BF16),
            pltpu.VMEM((96, 576), BF16),
            pltpu.VMEM((6, 10, 32, 128), BF16),
            pltpu.VMEM((6, 10, 96, 128), BF16),
            pltpu.VMEM((4, 8, 64, 128), F32),
            pltpu.VMEM((4, 6, 64, 128), BF16),
            pltpu.VMEM((6, 8, 32, 128), BF16),
            pltpu.VMEM((4, 8, 192, 128), BF16),
            pltpu.VMEM((2, 6, 128, 128), BF16),
            pltpu.VMEM((3, 6, 128, 128), BF16),
            pltpu.VMEM((6, 10, 64, 128), BF16),
            pltpu.VMEM((4, 8, 192, 128), BF16),
            pltpu.VMEM((6, 10, 32, 128), BF16),
            pltpu.VMEM((6, 10, 32, 128), BF16),
            pltpu.VMEM((4, 8, 32, 128), F32),
            pltpu.VMEM((16, 16, 896), BF16),
            pltpu.VMEM((128, 1792), BF16),
            pltpu.VMEM((192, 1152), BF16),
            pltpu.VMEM((128, 1792), F32),
            pltpu.VMEM((2, 8, 16, 896), BF16),
            pltpu.VMEM((8, 16, 896), BF16),
            pltpu.VMEM((8, 16, 896), BF16),
            pltpu.VMEM((8, 16, 896), BF16),
            pltpu.VMEM((16, 896), BF16),
            pltpu.VMEM((8, 16, 896), BF16),
            pltpu.VMEM((288, 192), F32),
            pltpu.VMEM((16, 32, 128), BF16),
            pltpu.VMEM((16, 32, 128), BF16),
            pltpu.VMEM((32, 128), BF16),
            pltpu.VMEM((8, 32, 128), BF16),
            pltpu.VMEM((16, 32, 128), BF16),
            dma((4,)),
            dma((5, 8)),
            dma((5, 8)),
            dma,
            dma,
            dma((16,)),
            dma((16,)),
            dma((16,)),
            dma((16,)),
            dma((8,)),
            dma((8,)),
            dma((16,)),
            dma((16,)),
            dma((8,)),
            dma((8,)),
            dma((16,)),
            dma((16,)),
        ],
        compiler_params=pltpu.CompilerParams(
            collective_id=0, has_side_effects=True, vmem_limit_bytes=58000 * 1024
        ),
    )(
        volume,
        jnp.transpose(filters_three, (0, 2, 1)),
        filters_four,
        jnp.transpose(cotangent, (1, 2, 3, 0)),
    )
    gv, g3, g4 = pl.pallas_call(
        writer,
        out_shape=(
            pltpu.HBM((32, 4, 8, 128), BF16),
            pltpu.HBM((27, 32, 64), F32),
            pltpu.HBM((27, 8, 64), F32),
        ),
        in_specs=[hbm] * 3,
        out_specs=(hbm,) * 3,
        scratch_shapes=[dma((3,))],
        compiler_params=pltpu.CompilerParams(vmem_limit_bytes=1024 * 1024),
    )(gv, g3, g4)
    return (gv, jnp.transpose(g3, (0, 2, 1)), g4)


def solution(mesh):
    in_specs = (
        P(None, "depth", "height", None),
        P(),
        P(None, "height", None),
        P(None, "depth", "height", None),
    )
    out_specs = (P(None, "depth", "height", None), P(), P(None, "height", None))
    return jax.shard_map(shards, mesh=mesh, in_specs=in_specs, out_specs=out_specs, check_vma=False)
```
